32 devices in a mesh: seq: 8 (over y, x, core), tp: 4 (over z).
Axes of the slice: x: 2, y: 2, z: 4, core: 2. Of those that a mesh axis runs over, the one named last changes fastest.
Arguments:
- patches: bfloat16 [3072, 768], P(('seq', 'tp')), may hold values from -6 to 6
- specials: bfloat16 [20, 768], P('tp'), may hold values from -6 to 6
- pos_table: bfloat16 [1625, 768], replicated, may hold values from -3 to 3
- image_length: int32 [4], replicated, may hold values from 256 to 1369, as said below
- slot_band: int32 [48], replicated, may hold values from 0 to 47, as said below
- w_qkv: bfloat16 [3, 768, 768], P(None, None, 'tp'), may hold values from -0.21875 to 0.21875
- qv_bias: float32 [2, 768], P(None, 'tp'), may hold values from -2 to 2
- w_out: bfloat16 [768, 768], P('tp'), may hold values from -3 to 3
- branch_bias: float32 [2, 768], replicated, may hold values from -2 to 2
- ln_gain: float32 [2, 768], replicated, may hold values from 0.5 to 1.5
- ln_bias: float32 [2, 768], replicated, may hold values from -2 to 2
- layer_scale: float32 [2, 768], replicated, may hold values from 0.5 to 1.5
- w_up: bfloat16 [768, 3072], P(None, 'tp'), may hold values from -0.21875 to 0.21875
- up_bias: float32 [3072], P('tp'), may hold values from -2 to 2
- w_down: bfloat16 [3072, 768], P('tp'), may hold values from -0.109375 to 0.109375
- cot_patch: bfloat16 [3072, 768], P('seq'), may hold values from -6 to 6
- cot_special: bfloat16 [20, 768], replicated, may hold values from -6 to 6
Outputs:
- out_patch: bfloat16 [3072, 768], P(('seq', 'tp'))
- out_special: bfloat16 [20, 768], P('tp')
- grad_patch: float32 [3072, 768], P(('seq', 'tp'))
- grad_special: float32 [20, 768], P('tp')
- grad_pos: float32 [1625, 768], replicated
- grad_qkv: float32 [3, 768, 768], P(None, None, 'tp')
- grad_qv_bias: float32 [2, 768], P(None, 'tp')
- grad_out: float32 [768, 768], P('tp')
- grad_branch_bias: float32 [2, 768], replicated
- grad_ln_gain: float32 [2, 768], replicated
- grad_ln_bias: float32 [2, 768], replicated
- grad_layer_scale: float32 [2, 768], replicated
- grad_up: float32 [768, 3072], P(None, 'tp')
- grad_up_bias: float32 [3072], P('tp')
- grad_down: float32 [3072, 768], P('tp')
The draws below stay inside these ranges and needn't reach their ends.
Inputs may be any that keep to these rules, and one draw needn't show every extreme that they name: `image_length`: exactly 1 of the 4 images have 1369 patches and the others 256. `slot_band`: a permutation of the band numbers; bands are numbered image by image from 0, each image taking ceil(length / 64) consecutive numbers, and numbers past the last image's bands are empty.
All inputs are finite; a program needn't handle non-finite values.
Results may differ from the reference program's by a relative error of at most 0.023.
Values may be sent and summed in bfloat16 or wider, within the bound.
No kernel may reach another device: no remote copies, remote signals or barrier semaphores. Data moves between devices by JAX's collectives and lax.ppermute only.
A program may use at most 128 MiB of HBM per device.

```python
import math
import jax
import jax.numpy as jnp
from jax import lax

D = 768
HEADS = 12
DH = 64
FF = 3072
SPECIALS = 5
PATCH_BIG = 1369
PATCH_SMALL = 256
BAND = 64
BANDS_ALL = 48
TOKENS = 3072
NBIG = 1
NIMG = 4
NSPEC = 20
POS_ROWS = 1625


def image_sizes(key):
    ranking = jax.random.permutation(key, NIMG)
    return jnp.where(ranking < NBIG, PATCH_BIG, PATCH_SMALL).astype(jnp.int32)


def draw_image_length(key, part):
    return image_sizes(key)


def draw_slot_band(key, part):
    lengths = image_sizes(key)
    key = jax.random.fold_in(key, 7)
    pick_key, order_key = jax.random.split(key)
    band_counts = ((lengths + BAND - 1) // BAND).astype(jnp.int32)
    band_starts = (jnp.cumsum(band_counts) - band_counts).astype(jnp.int32)
    chosen = jax.random.randint(pick_key, (), 0, NIMG)
    first_band = band_starts[chosen]
    last_band = first_band + band_counts[chosen] - 1
    ordering = jax.random.permutation(order_key, BANDS_ALL).astype(jnp.int32)
    at_first = jnp.argmax(ordering == first_band)
    ordering = ordering.at[at_first].set(ordering[0]).at[0].set(first_band)
    at_last = jnp.argmax(ordering == last_band)
    ordering = ordering.at[at_last].set(ordering[BANDS_ALL - 1]).at[BANDS_ALL - 1].set(last_band)
    return ordering.astype(jnp.int32)


def levels(key, extent, shards, least, high):
    loudness = 1.0
    for dim, shards_of in shards:
        steps = jax.random.uniform(jax.random.fold_in(jax.random.fold_in(key, 6), dim), (shards_of,), jnp.float32, least / len(shards), high / len(shards))
        loudness = loudness * jnp.repeat(jnp.exp(steps), extent[dim] // shards_of).reshape((-1,) + (1,) * (len(extent) - 1 - dim))
    return loudness


def gaussian(stream_key, extent, scale, bound, pieces=(), held_as=jnp.bfloat16):
    level = levels(stream_key, extent, pieces, -0.22, 0.18) if pieces else 1.0
    entries = jax.random.normal(stream_key, extent, jnp.float32) * scale * level
    return jnp.minimum(jnp.maximum(entries, -bound), bound).astype(held_as)


def setup_inputs(seed: int = 0) -> dict:
    key_list = jax.random.split(jax.random.key(seed), 18)
    patches = gaussian(key_list[0], (TOKENS, D), 1.0, 6.0, ((0, 32),))
    specials = gaussian(key_list[1], (NSPEC, D), 1.0, 6.0, ((0, 4),))
    pos_table = gaussian(key_list[2], (POS_ROWS, D), 0.5, 3.0)
    image_length = draw_image_length(jax.random.fold_in(key_list[17], 71), 0)
    slot_band = draw_slot_band(jax.random.fold_in(key_list[17], 71), 0)
    w_qkv = gaussian(key_list[5], (3, D, D), D ** -0.5, 0.21875, ((2, 4),))
    qv_bias = gaussian(key_list[6], (2, D), 0.3, 2.0, ((1, 4),), jnp.float32)
    w_out = gaussian(key_list[7], (D, D), (max(1, D // 192)) ** -0.5, 3.0, ((0, 4),))
    branch_bias = gaussian(key_list[8], (2, D), 0.3, 2.0, (), jnp.float32)
    ln_gain = jnp.clip(1.0 + 0.1 * jax.random.normal(key_list[9], (2, D), jnp.float32), 0.5, 1.5)
    ln_bias = gaussian(key_list[10], (2, D), 0.3, 2.0, (), jnp.float32)
    layer_scale = jnp.clip(jax.random.uniform(key_list[11], (2, D), jnp.float32, 0.5, 1.5), 0.5, 1.5)
    w_up = gaussian(key_list[12], (D, FF), D ** -0.5, 0.21875, ((1, 4),))
    up_bias = gaussian(key_list[13], (FF,), 0.3, 2.0, ((0, 4),), jnp.float32)
    w_down = gaussian(key_list[14], (FF, D), FF ** -0.5, 0.109375, ((0, 4),))
    cot_patch = gaussian(key_list[15], (TOKENS, D), 1.0, 6.0, ((0, 8),))
    cot_special = gaussian(key_list[16], (NSPEC, D), 1.0, 6.0)
    return dict(patches=patches, specials=specials, pos_table=pos_table, image_length=image_length, slot_band=slot_band, w_qkv=w_qkv, qv_bias=qv_bias, w_out=w_out, branch_bias=branch_bias, ln_gain=ln_gain, ln_bias=ln_bias, layer_scale=layer_scale, w_up=w_up, up_bias=up_bias, w_down=w_down, cot_patch=cot_patch, cot_special=cot_special)


@jax.custom_vjp
def low(v):
    return lax.optimization_barrier(v.astype(jnp.bfloat16)).astype(jnp.float32)

@jax.custom_vjp
def low_back(v):
    return v

def low_keep(v):
    return (low(v), None)

def low_pass(kept, grad):
    return (grad,)

def back_keep(v):
    return (v, None)

def back_low(kept, grad):
    return (low(grad),)
low.defvjp(low_keep, low_pass)
low_back.defvjp(back_keep, back_low)
eps_norm = 1e-06
masked_score = -1e+30
highest = lax.Precision.HIGHEST

def band_layout(image_length, slot_band):
    band_counts = ((image_length + BAND - 1) // BAND).astype(jnp.int32)
    band_starts = (jnp.cumsum(band_counts) - band_counts).astype(jnp.int32)
    used_bands = jnp.sum(band_counts).astype(jnp.int32)
    passed = (slot_band[:, None] >= band_starts[None, :]).astype(jnp.int32)
    holder = (lax.optimization_barrier(jnp.sum(passed, axis=1)) - 1).astype(jnp.int32)
    picked = holder[:, None] == jnp.arange(NIMG, dtype=jnp.int32)[None, :]
    first_band = lax.optimization_barrier(jnp.sum(jnp.where(picked, band_starts[None, :], 0), axis=1)).astype(jnp.int32)
    holder_length = lax.optimization_barrier(jnp.sum(jnp.where(picked, image_length[None, :], 0), axis=1)).astype(jnp.int32)
    within = (slot_band - first_band)[:, None] * BAND + jnp.arange(BAND, dtype=jnp.int32)[None, :]
    usable = (slot_band < used_bands)[:, None] & (within < holder_length[:, None])
    image_id = jnp.where(usable, holder[:, None], -1).reshape(-1).astype(jnp.int32)
    table_offset = jnp.where(holder_length == PATCH_BIG, 0, PATCH_BIG).astype(jnp.int32)
    position = jnp.where(usable, table_offset[:, None] + within, 0).reshape(-1).astype(jnp.int32)
    return (image_id, position)

def layer_norm(values, gain, shift):
    centre = lax.optimization_barrier(jnp.mean(values, axis=-1, keepdims=True))
    centred = values - centre
    spread = lax.optimization_barrier(jnp.mean(centred * centred, axis=-1, keepdims=True))
    return centred * lax.rsqrt(spread + eps_norm) * gain + shift

def product(left, right):
    return jnp.dot(left, right, precision=highest, preferred_element_type=jnp.float32)

def attend(queries, query_image, key_rows, value_rows, key_image):
    scores = jnp.einsum('qhd,khd->hqk', queries, key_rows, precision=highest) * DH ** (-0.5)
    scores = low_back(scores)
    allowed = ((query_image[:, None] == key_image[None, :]) & (query_image[:, None] >= 0))[None]
    masked = jnp.where(allowed, scores, masked_score)
    row_top = lax.optimization_barrier(jnp.max(masked, axis=-1, keepdims=True))
    weights = jnp.where(allowed, jnp.exp(masked - row_top), 0.0)
    row_total = lax.optimization_barrier(jnp.sum(weights, axis=-1, keepdims=True))
    row_total = jnp.where(query_image[None, :, None] >= 0, row_total, 1.0)
    rounded = low(weights)
    summed = jnp.einsum('hqk,khd->hqd', rounded, value_rows, precision=highest)
    return jnp.transpose(summed / row_total, (1, 0, 2))

def forward(patches, specials, pos_table, w_qkv, qv_bias, w_out, branch_bias, ln_gain, ln_bias, layer_scale, w_up, up_bias, w_down, image_id, position):
    usable = (image_id >= 0).astype(jnp.float32)
    placed = patches + usable[:, None] * pos_table[position]
    stream = jnp.concatenate([placed, specials], axis=0)
    row_image = jnp.concatenate([image_id, jnp.arange(NSPEC, dtype=jnp.int32) // SPECIALS])
    normed = low(layer_norm(stream, ln_gain[0], ln_bias[0]))
    queries = low_back(low(product(normed, w_qkv[0]) + qv_bias[0]))
    key_rows = low_back(low(product(normed, w_qkv[1])))
    value_rows = low_back(low(product(normed, w_qkv[2]) + qv_bias[1]))
    row_count = stream.shape[0]
    queries = queries.reshape(row_count, HEADS, DH)
    key_rows = key_rows.reshape(row_count, HEADS, DH)
    value_rows = value_rows.reshape(row_count, HEADS, DH)
    block_rows = math.gcd(TOKENS, 512)

    def attend_block(parts):
        return attend(parts[0], parts[1], key_rows, value_rows, row_image)
    blocked = jax.checkpoint(attend_block)
    patch_part = lax.map(blocked, (queries[:TOKENS].reshape(TOKENS // block_rows, block_rows, HEADS, DH), image_id.reshape(TOKENS // block_rows, block_rows)))
    special_part = blocked((queries[TOKENS:], row_image[TOKENS:]))
    attended = jnp.concatenate([patch_part.reshape(TOKENS, D), special_part.reshape(NSPEC, D)], axis=0)
    attended = low_back(low(attended))
    branch_one = low_back(product(attended, w_out))
    mid_stream = stream + layer_scale[0] * (branch_one + branch_bias[0])
    normed_two = low(layer_norm(mid_stream, ln_gain[1], ln_bias[1]))
    hidden_pre = low_back(product(normed_two, w_up) + up_bias)
    hidden = low(jax.nn.gelu(hidden_pre, approximate=False))
    branch_two = low_back(product(hidden, w_down))
    result = mid_stream + layer_scale[1] * (branch_two + branch_bias[1])
    return (result[:TOKENS], result[TOKENS:])

def reference(patches, specials, pos_table, image_length, slot_band, w_qkv, qv_bias, w_out, branch_bias, ln_gain, ln_bias, layer_scale, w_up, up_bias, w_down, cot_patch, cot_special):
    image_id, position = band_layout(image_length, slot_band)
    floats = [item.astype(jnp.float32) for item in (patches, specials, pos_table, w_qkv, qv_bias, w_out, branch_bias, ln_gain, ln_bias, layer_scale, w_up, up_bias, w_down)]

    def run(*params):
        return forward(*params, image_id, position)
    outputs, pull = jax.vjp(run, *floats)
    grads = pull((cot_patch.astype(jnp.float32), cot_special.astype(jnp.float32)))
    return (outputs[0].astype(jnp.bfloat16), outputs[1].astype(jnp.bfloat16), grads[0], grads[1], grads[2], grads[3], grads[4], grads[5], grads[6], grads[7], grads[8], grads[9], grads[10], grads[11], grads[12])
```

```python
import functools

import jax
import jax.numpy as jnp
from jax import lax
from jax.experimental import pallas as pl
from jax.experimental.pallas import tpu as pltpu
from jax.sharding import PartitionSpec as P

DH = 64
SPECIALS = 5
PATCH_BIG = 1369
BAND = 64

GROUP = 16
LANES = 256
FAR = 1e30
EPS = 1e-06
BIG_BANDS = (PATCH_BIG + BAND - 1) // BAND
WINDOW = -(-(BIG_BANDS + 1) * BAND // 256) * 256
VMEM_LIMIT = 60 * 1024 * 1024

bf16 = jnp.bfloat16
f32 = jnp.float32


def dot(a, b):
    return jnp.dot(a, b, preferred_element_type=f32)


def dot_nt(a, b):
    return lax.dot_general(a, b, (((1,), (1,)), ((), ())), preferred_element_type=f32)


def dot_tn(a, b):
    return lax.dot_general(a, b, (((0,), (0,)), ((), ())), preferred_element_type=f32)


def lanes_of(shape):
    return lax.broadcasted_iota(jnp.int32, shape, len(shape) - 1)


def norm_parts(values):
    centre = jnp.mean(values, axis=-1, keepdims=True)
    centred = values - centre
    spread = jnp.mean(centred * centred, axis=-1, keepdims=True)
    scale = lax.rsqrt(spread + EPS)
    return centred * scale, scale


def norm_back(unit, scale, eg):
    first = jnp.mean(eg, axis=-1, keepdims=True)
    second = jnp.mean(eg * unit, axis=-1, keepdims=True)
    return scale * (eg - first - unit * second)


def key_head(lane, h):
    return (lane >= h * DH) & (lane < (h + 1) * DH)


def value_head(lane, h):
    start = (0, DH, 3 * DH)[h]
    return (lane >= start) & (lane < start + DH)


def key_side(lane, h, images):
    image_lane = (lane >= 3 * DH) & (lane <= 3 * DH + images)
    lse_start = 3 * DH + images + 1 + 3 * h
    return key_head(lane, h) | image_lane | ((lane >= lse_start) & (lane < lse_start + 3))


def value_side(lane, h):
    start = 2 * DH + 3 * h
    return value_head(lane, h) | ((lane >= start) & (lane < start + 3))


def three_pieces(x):
    high = x.astype(bf16).astype(f32)
    rest = x - high
    middle = rest.astype(bf16).astype(f32)
    return high, middle, (rest - middle).astype(bf16).astype(f32)


def stacked(rows, picks):
    zero = jnp.zeros_like(rows)
    return jnp.concatenate([jnp.where(pick, rows, zero) for pick in picks], axis=0)


def spread_sum(stack, picks):
    count = stack.shape[0] // len(picks)
    total = None
    for h, pick in enumerate(picks):
        part = jnp.where(pick, stack[h * count : (h + 1) * count], 0.0)
        total = part if total is None else total + part
    return total


def call(body, outs, ins, scratch=(), outside=()):
    spaces = []
    for i, item in enumerate(ins):
        smem = item.dtype == jnp.int32 and item.ndim == 1
        space = pl.ANY if i in outside else pltpu.SMEM if smem else pltpu.VMEM
        spaces.append(pl.BlockSpec(memory_space=space))
    return pl.pallas_call(
        body,
        out_shape=[jax.ShapeDtypeStruct(s, d) for s, d in outs],
        in_specs=spaces,
        out_specs=[pl.BlockSpec(memory_space=pltpu.VMEM) for _ in outs],
        scratch_shapes=list(scratch),
        compiler_params=pltpu.CompilerParams(vmem_limit_bytes=VMEM_LIMIT),
    )(*ins)


def for_each(count, body):
    if count <= 8:
        for i in range(count):
            body(i)
    else:

        def step(i, carry):
            body(i)
            return carry

        lax.fori_loop(0, count, step, 0)


def embed_kernel(sizes, place, *refs):
    tp_count, quarter, special, images = sizes
    xs = refs[:tp_count]
    pos, w_cat, b_cat, gain, shift, row_image = refs[tp_count : tp_count + 6]
    stream, own, normed, query, pack, key_own, value_own = refs[tp_count + 6 :]
    rows = quarter * tp_count
    me = place[0]
    for k in range(tp_count):
        spot = lax.rem(me - k + tp_count, tp_count)
        patch_at = pl.multiple_of(spot * quarter, 16)
        special_at = pl.multiple_of(rows + spot * special, 16)
        part = xs[k][:quarter].astype(f32) + pos[pl.ds(patch_at, quarter)].astype(f32)
        stream[pl.ds(patch_at, quarter)] = part
        tail = xs[k][quarter:].astype(f32)
        stream[pl.ds(special_at, special)] = tail
        if k == 0:
            own[:quarter] = part
            own[quarter:] = tail
    unit, _ = norm_parts(stream[...])
    rounded = (unit * gain[...] + shift[...]).astype(bf16)
    normed[...] = rounded
    projected = (dot(rounded, w_cat[...]) + b_cat[...]).astype(bf16)
    image = row_image[...]
    total = image.shape[0]
    lane = lanes_of((total, LANES))
    image_lane = (lane >= 3 * DH) & (lane <= 3 * DH + images)
    scaled = projected[:, :LANES].astype(f32) * (DH**-0.5)
    far = jnp.where(image_lane & (lane != 3 * DH + image), FAR, 0.0)
    query[...] = jnp.where(lane < 3 * DH, scaled, far).astype(bf16)
    pack[...] = projected[:, LANES:]
    own_lane = 3 * DH + jnp.where(image < 0, images, image)
    lse_lane = (lane > 3 * DH + images) & (lane <= 3 * DH + images + 9)
    aux = jnp.where((lane == own_lane) | lse_lane, -1.0, 0.0)
    key_own[...] = jnp.where(
        lane < 3 * DH, projected[:, LANES : 2 * LANES].astype(f32), aux
    ).astype(bf16)
    half = lanes_of((total, 128))
    value_own[:, :128] = projected[:, 512:640]
    value_own[:, 128:] = jnp.where(
        half < DH,
        jnp.where(half < 9, -1.0, 0.0),
        projected[:, 384:512].astype(f32),
    ).astype(bf16)


def attend_kernel(sizes, slots, windows, *refs):
    blocks_count, bands, images, rows = sizes
    blocks = refs[:blocks_count]
    key_own, value_own, query = refs[blocks_count : blocks_count + 3]
    keys, values, attended, attended_b, query_out = refs[blocks_count + 3 :]
    lane = lanes_of((1, LANES))
    lse_lane = (lane > 3 * DH + images) & (lane <= 3 * DH + images + 9)
    empty = jnp.where((lane == 3 * DH + images) | lse_lane, -1.0, 0.0)
    buffer_rows = keys.shape[0]

    def clear(i, carry):
        at = pl.multiple_of(i * BAND, BAND)
        keys[pl.ds(at, BAND)] = jnp.broadcast_to(empty, (BAND, LANES)).astype(bf16)
        values[pl.ds(at, BAND)] = jnp.zeros((BAND, LANES), bf16)
        return carry

    lax.fori_loop(0, buffer_rows // BAND, clear, 0)
    band_lane = lanes_of((BAND, LANES))
    half = lanes_of((BAND, 128))
    in_band = lax.broadcasted_iota(jnp.int32, (BAND, LANES), 0)
    band_lse = (band_lane > 3 * DH + images) & (band_lane <= 3 * DH + images + 9)
    delta_aux = jnp.where(half < 9, -1.0, 0.0)
    per_block = blocks[0].shape[0] // BAND
    slot_count = blocks_count * per_block
    for b in range(blocks_count):

        def place(j, b=b):
            slot = b * per_block + j
            valid = slots[2 * slot_count + slot]

            @pl.when(valid > 0)
            def _():
                at = pl.multiple_of(slots[slot], BAND)
                image = slots[slot_count + slot]
                source = blocks[b][pl.ds(pl.multiple_of(j * BAND, BAND), BAND)]
                own_lane = 3 * DH + jnp.where(in_band < valid, image, images)
                aux = jnp.where((band_lane == own_lane) | band_lse, -1.0, 0.0)
                keys[pl.ds(at, BAND)] = jnp.where(
                    band_lane < 3 * DH, source[:, :LANES].astype(f32), aux
                ).astype(bf16)
                values[pl.ds(at, BAND), :128] = source[:, 256:384]
                values[pl.ds(at, BAND), 128:] = jnp.where(
                    half < DH, delta_aux, source[:, 128:256].astype(f32)
                ).astype(bf16)

        for_each(per_block, place)

    def place_special(i):
        at = pl.multiple_of(windows[bands + i], BAND)
        source = pl.ds(pl.multiple_of(rows + i * GROUP, GROUP), GROUP)
        keys[pl.ds(at, GROUP)] = key_own[source]
        values[pl.ds(at, GROUP)] = value_own[source]

    for_each(images, place_special)
    key_picks = [key_side(lane, h, images) for h in range(3)]
    value_picks = [value_head(lane, h) for h in range(3)]

    def unit(window, start, count):
        at = pl.multiple_of(windows[window], BAND)
        spot = pl.ds(start, count)
        own = query[spot]
        key_part = keys[pl.ds(at, WINDOW)]
        value_part = values[pl.ds(at, WINDOW)]
        scores = dot_nt(stacked(own, key_picks), key_part)
        top = jnp.maximum(jnp.max(scores, axis=-1, keepdims=True), -0.1 * FAR)
        weights = jnp.exp(scores - top)
        total = jnp.sum(weights, axis=-1, keepdims=True)
        usable = total > 0.0
        safe = jnp.where(usable, total, 1.0)
        summed = dot(weights.astype(bf16), value_part) / safe
        result = spread_sum(summed, value_picks)
        attended[spot] = result
        attended_b[spot] = result.astype(bf16)
        lse = jnp.where(usable, top + jnp.log(safe), 0.0)
        row = own.astype(f32)
        for h in range(3):
            for piece, part in enumerate(three_pieces(lse[h * count : (h + 1) * count])):
                row = jnp.where(lane == 3 * DH + images + 1 + 3 * h + piece, part, row)
        query_out[spot] = row.astype(bf16)

    for u in range(bands):
        unit(u, u * BAND, BAND)
    for_each(
        images,
        lambda i: unit(bands + i, pl.multiple_of(rows + i * GROUP, GROUP), GROUP),
    )


def feed_kernel(sizes, place, *refs):
    tp_count, quarter, special = sizes
    attended = refs[:tp_count]
    w_outs = refs[tp_count : 2 * tp_count]
    (stream, scale, bias, gain, shift, w_up, up_bias, grad_hidden) = refs[
        2 * tp_count : 2 * tp_count + 8
    ]
    mid_own, one_own, normed, hidden_out, grad_pre_out = refs[2 * tp_count + 8 : 2 * tp_count + 13]
    parts = refs[2 * tp_count + 13 : 3 * tp_count + 13]
    mid, partial = refs[3 * tp_count + 13 :]
    rows = quarter * tp_count
    me = place[0]
    one = dot(attended[0][...], w_outs[0][...])
    for k in range(1, tp_count):
        one += dot(attended[k][...], w_outs[k][...])
    partial[...] = one
    value = stream[...] + scale[0:1] * (one + bias[0:1])
    mid[...] = value
    own_patch = pl.ds(pl.multiple_of(me * quarter, 16), quarter)
    own_special = pl.ds(pl.multiple_of(rows + me * special, 16), special)
    mid_own[:quarter] = mid[own_patch]
    mid_own[quarter:] = mid[own_special]
    one_own[:quarter] = partial[own_patch]
    one_own[quarter:] = partial[own_special]
    unit, _ = norm_parts(value)
    rounded = (unit * gain[...] + shift[...]).astype(bf16)
    normed[...] = rounded
    pre = dot(rounded, w_up[...]) + up_bias[...]
    share = 0.5 * (1.0 + lax.erf(pre * (0.5**0.5)))
    hidden_out[...] = (pre * share).astype(bf16)
    slope = share + pre * jnp.exp(-0.5 * pre * pre) * (0.5 / jnp.pi) ** 0.5
    grad_pre = (grad_hidden[...] * slope).astype(bf16)
    grad_pre_out[...] = grad_pre
    partial[...] = dot_nt(grad_pre, w_up[...])
    send_blocks(me, parts, partial, quarter, special)


def send_blocks(me, parts, partial, quarter, special):
    tp_count = len(parts)
    rows = quarter * tp_count
    for k in range(tp_count):
        spot = lax.rem(me + k, tp_count)
        patch_at = pl.ds(pl.multiple_of(spot * quarter, 16), quarter)
        special_at = pl.ds(pl.multiple_of(rows + spot * special, 16), special)
        parts[k][:quarter] = partial[patch_at].astype(parts[k].dtype)
        parts[k][quarter:] = partial[special_at].astype(parts[k].dtype)


def mid_back_kernel(tp_count, *refs):
    parts = refs[:tp_count]
    mid, one, grad_result, weight, scale, bias, gain = refs[tp_count : tp_count + 7]
    w_outs = refs[tp_count + 7 : 2 * tp_count + 7]
    grad_mid_out, grad_one_out, small = refs[2 * tp_count + 7 : 2 * tp_count + 10]
    sends = refs[2 * tp_count + 10 :]
    incoming = parts[0][...]
    for k in range(1, tp_count):
        incoming += parts[k][...].astype(f32)
    unit, scaling = norm_parts(mid[...])
    grad_mid = grad_result[...] + norm_back(unit, scaling, incoming * gain[...])
    weighted = incoming * weight[...]
    weighted_mid = grad_mid * weight[...]
    small[0:1] = jnp.sum(weighted * unit, axis=0, keepdims=True)
    small[1:2] = jnp.sum(weighted, axis=0, keepdims=True)
    small[2:3] = jnp.sum(weighted_mid * (one[...] + bias[0:1]), axis=0, keepdims=True)
    small[3:4] = jnp.sum(weighted_mid, axis=0, keepdims=True) * scale[0:1]
    small[4:8] = jnp.zeros((4, small.shape[1]), f32)
    grad_mid_out[...] = grad_mid
    grad_one = (grad_mid * scale[0:1]).astype(bf16)
    grad_one_out[...] = grad_one
    for k in range(tp_count):
        sends[k][...] = dot_nt(grad_one, w_outs[(tp_count - k) % tp_count][...]).astype(bf16)


def delta_kernel(sizes, place, *refs):
    tp_count, quarter, special = sizes
    parts = refs[:tp_count]
    attended, out, whole = refs[tp_count:]
    rows = quarter * tp_count
    me = place[0]
    for k in range(tp_count):
        spot = lax.rem(me - k + tp_count, tp_count)
        whole[pl.ds(pl.multiple_of(spot * quarter, 16), quarter)] = parts[k][:quarter].astype(f32)
        whole[pl.ds(pl.multiple_of(rows + spot * special, 16), special)] = parts[k][
            quarter:
        ].astype(f32)
    value = whole[...]
    product = value * attended[...]
    lane = lanes_of(value.shape)
    for h in range(3):
        delta = jnp.sum(jnp.where(value_head(lane, h), product, 0.0), axis=-1, keepdims=True)
        for piece, part in enumerate(three_pieces(delta)):
            value = jnp.where(lane == 2 * DH + 3 * h + piece, part, value)
    out[...] = value.astype(bf16)


def query_grad_kernel(sizes, windows, query, grad, keys, values, out):
    bands, images, rows = sizes
    lane = lanes_of((1, LANES))
    key_picks = [key_side(lane, h, images) for h in range(3)]
    value_picks = [value_side(lane, h) for h in range(3)]
    head_picks = [key_head(lane, h) for h in range(3)]

    def unit(window, start, count):
        at = pl.multiple_of(windows[window], BAND)
        spot = pl.ds(start, count)
        key_part = keys[pl.ds(at, WINDOW)]
        probs = jnp.exp(dot_nt(stacked(query[spot], key_picks), key_part))
        pulled = dot_nt(stacked(grad[spot], value_picks), values[pl.ds(at, WINDOW)])
        scores = (probs * pulled).astype(bf16)
        result = spread_sum(dot(scores, key_part), head_picks) * DH**-0.5
        out[spot] = result.astype(bf16)

    for u in range(bands):
        unit(u, u * BAND, BAND)
    for_each(
        images,
        lambda i: unit(bands + i, pl.multiple_of(rows + i * GROUP, GROUP), GROUP),
    )


def pair_grad_kernel(sizes, place, slots, windows, *refs):
    blocks_count, bands, images, tp_count, quarter, special = sizes
    query_blocks = refs[:blocks_count]
    grad_blocks = refs[blocks_count : 2 * blocks_count]
    rest = refs[2 * blocks_count :]
    query_own, grad_own, key_own, value_own, grad_query, w_cat, joined = rest[:7]
    parts = rest[7 : 7 + tp_count]
    queries, grads, partial = rest[7 + tp_count :]
    rows = quarter * tp_count
    lane = lanes_of((1, LANES))
    image_lane = (lane >= 3 * DH) & (lane <= 3 * DH + images)
    empty = jnp.where(image_lane, FAR, 0.0)

    def clear(i, carry):
        at = pl.multiple_of(i * BAND, BAND)
        queries[pl.ds(at, BAND)] = jnp.broadcast_to(empty, (BAND, LANES)).astype(bf16)
        grads[pl.ds(at, BAND)] = jnp.zeros((BAND, LANES), bf16)
        return carry

    lax.fori_loop(0, queries.shape[0] // BAND, clear, 0)
    per_block = query_blocks[0].shape[0] // BAND
    slot_count = blocks_count * per_block
    for b in range(blocks_count):

        def put(j, b=b):
            slot = b * per_block + j

            @pl.when(slots[2 * slot_count + slot] > 0)
            def _():
                at = pl.multiple_of(slots[slot], BAND)
                source = pl.ds(pl.multiple_of(j * BAND, BAND), BAND)
                if blocks_count == 1:
                    pltpu.sync_copy(query_blocks[b].at[source], queries.at[pl.ds(at, BAND)])
                    pltpu.sync_copy(grad_blocks[b].at[source], grads.at[pl.ds(at, BAND)])
                else:
                    queries[pl.ds(at, BAND)] = query_blocks[b][source]
                    grads[pl.ds(at, BAND)] = grad_blocks[b][source]

        for_each(per_block, put)

    def put_special(i):
        at = pl.multiple_of(windows[bands + i], BAND)
        source = pl.ds(pl.multiple_of(rows + i * GROUP, GROUP), GROUP)
        queries[pl.ds(at, GROUP)] = query_own[source]
        grads[pl.ds(at, GROUP)] = grad_own[source]

    for_each(images, put_special)
    key_picks = [key_side(lane, h, images) for h in range(3)]
    value_picks = [value_side(lane, h) for h in range(3)]
    key_heads = [key_head(lane, h) for h in range(3)]
    value_heads = [value_head(lane, h) for h in range(3)]

    def unit(window, start, count):
        at = pl.multiple_of(windows[window], BAND)
        spot = pl.ds(start, count)
        query_part = queries[pl.ds(at, WINDOW)]
        grad_part = grads[pl.ds(at, WINDOW)]
        probs = jnp.exp(dot_nt(stacked(key_own[spot], key_picks), query_part))
        pulled = dot_nt(stacked(value_own[spot], value_picks), grad_part)
        scores = (probs * pulled).astype(bf16)
        grad_key = spread_sum(dot(scores, query_part), key_heads)
        grad_value = spread_sum(dot(probs.astype(bf16), grad_part), value_heads)
        joined[spot, 256:384] = grad_key[:, :128].astype(bf16)
        half = lanes_of((count, 128))
        joined[spot, 384:512] = jnp.where(half < DH, grad_key[:, 128:], grad_value[:, 128:]).astype(
            bf16
        )
        joined[spot, 512:640] = grad_value[:, :128].astype(bf16)

    joined[:, :256] = grad_query[...]
    for u in range(bands):
        unit(u, u * BAND, BAND)
    for_each(
        images,
        lambda i: unit(bands + i, pl.multiple_of(rows + i * GROUP, GROUP), GROUP),
    )
    partial[...] = dot_nt(joined[...], w_cat[...])
    send_blocks(place[0], parts, partial, quarter, special)


def stream_back_kernel(sizes, *refs):
    tp_count, quarter = sizes
    parts = refs[:tp_count]
    stream, grad_mid, weight, gain, early = refs[tp_count : tp_count + 5]
    out, send, small = refs[tp_count + 5 :]
    incoming = parts[0][...]
    for k in range(1, tp_count):
        incoming += parts[k][...].astype(f32)
    unit, scaling = norm_parts(stream[...])
    result = grad_mid[...] + norm_back(unit, scaling, incoming * gain[...])
    out[...] = result
    weighted = incoming * weight[...]
    first = jnp.sum(weighted * unit, axis=0, keepdims=True)
    second = jnp.sum(weighted, axis=0, keepdims=True)
    sums = jnp.concatenate([first, second, early[2:8]], axis=0)
    small[...] = sums
    send[:quarter] = result[:quarter].astype(bf16)
    high = sums.astype(bf16)
    send[quarter : quarter + 16] = jnp.concatenate(
        [high.astype(f32), sums - high.astype(f32)], axis=0
    ).astype(bf16)


def join_kernel(sizes, place, *refs):
    tp_count, quarter = sizes
    parts = refs[:tp_count]
    out = refs[tp_count]
    me = place[0]
    for k in range(tp_count):
        spot = lax.rem(me - k + tp_count, tp_count)
        out[pl.ds(pl.multiple_of(spot * quarter, 16), quarter)] = parts[k][:quarter]
        out[pl.ds(pl.multiple_of(quarter * tp_count + spot * 16, 16), 16)] = parts[k][quarter:]


def position_kernel(sizes, slots, images_at, origin, *refs):
    blocks_count, images, rows, tp_count = sizes
    blocks = refs[:blocks_count]
    out, small, ordered, tiny, big, low = refs[blocks_count:]
    per_block = rows // BAND
    slot_count = blocks_count * per_block
    in_band = lax.broadcasted_iota(jnp.int32, (BAND, 1), 0)
    for b in range(blocks_count):
        spot = origin[b]
        tiny[pl.ds(pl.multiple_of(spot * tp_count * 16, 16), tp_count * 16)] = blocks[b][
            rows:
        ].astype(f32)

        def put(j, b=b):
            slot = b * per_block + j
            valid = slots[2 * slot_count + slot]

            @pl.when(valid > 0)
            def _():
                at = pl.multiple_of(slots[3 * slot_count + slot], BAND)
                source = blocks[b][pl.ds(pl.multiple_of(j * BAND, BAND), BAND)]
                ordered[pl.ds(at, BAND)] = jnp.where(in_band < valid, source.astype(f32), 0.0)

        for_each(per_block, put)
    total = tiny[0:16]
    for i in range(1, blocks_count * tp_count):
        total += tiny[i * 16 : (i + 1) * 16]
    small[...] = total[:8] + total[8:]
    big[...] = jnp.zeros_like(big)
    low[...] = jnp.zeros_like(low)

    def add(i):
        at = pl.multiple_of(images_at[i], BAND)
        is_big = images_at[images + i] > 0

        @pl.when(is_big)
        def _():
            big[...] += ordered[pl.ds(at, big.shape[0])]

        @pl.when(jnp.logical_not(is_big))
        def _():
            low[...] += ordered[pl.ds(at, low.shape[0])]

    for_each(images, add)
    out[:PATCH_BIG] = big[:PATCH_BIG]
    out[PATCH_BIG:] = low[: out.shape[0] - PATCH_BIG]


def rotated(x, k):
    count = lax.axis_size("tp")
    return lax.ppermute(x, "tp", [(i, (i + k) % count) for i in range(count)])


def from_group(x):
    return [x] + [rotated(x, k) for k in range(1, lax.axis_size("tp"))]


def to_group(blocks):
    return [blocks[0]] + [rotated(blocks[k], k) for k in range(1, len(blocks))]


def partner(x, k):
    count = lax.axis_size("seq")
    return lax.ppermute(x, "seq", [(i, i ^ k) for i in range(count)])


def from_bands(x):
    if lax.axis_size("seq") != 8:
        return [lax.all_gather(x, "seq", axis=0, tiled=True)]
    even = [x] + [partner(x, k) for k in (2, 4, 6)]
    odd = [partner(block, 1) for block in even]
    return [block for pair in zip(even, odd) for block in pair]


def after(value, *others):
    return lax.optimization_barrier((value,) + tuple(others))[0]


def pad_special(rows, group):
    width = rows.shape[1]
    grouped = rows.reshape(-1, SPECIALS, width)
    return jnp.pad(grouped, ((0, 0), (0, group - SPECIALS), (0, 0))).reshape(-1, width)


def cut_special(rows):
    width = rows.shape[1]
    return rows.reshape(-1, GROUP, width)[:, :SPECIALS].reshape(-1, width)


def joined_columns(query, key, value, axis):
    cut = functools.partial(lax.slice_in_dim, axis=axis)
    return jnp.concatenate(
        [
            query,
            jnp.zeros_like(cut(query, 0, DH)),
            key,
            cut(value, 2 * DH, 3 * DH),
            cut(value, 0, 2 * DH),
        ],
        axis=axis,
    )


def split_columns(joined):
    cut = functools.partial(lax.slice_in_dim, joined, axis=-1)
    return (
        cut(0, 3 * DH),
        cut(4 * DH, 7 * DH),
        jnp.concatenate([cut(8 * DH, 10 * DH), cut(7 * DH, 8 * DH)], axis=-1),
    )


def on_device(
    patches,
    specials,
    pos_table,
    image_length,
    slot_band,
    w_qkv,
    qv_bias,
    w_out,
    branch_bias,
    ln_gain,
    ln_bias,
    layer_scale,
    w_up,
    up_bias,
    w_down,
    cot_patch,
    cot_special,
):
    seq_count = lax.axis_size("seq")
    tp_count = lax.axis_size("tp")
    seq_place = lax.axis_index("seq")
    tp_place = lax.axis_index("tp")
    quarter, width = patches.shape
    images = image_length.shape[0]
    rows = quarter * tp_count
    bands = rows // BAND
    slot_count = slot_band.shape[0]
    special = (specials.shape[0] // SPECIALS) * GROUP
    special_rows = special * tp_count
    total = rows + special_rows
    block = quarter + special
    place = jnp.reshape(tp_place, (1,)).astype(jnp.int32)

    band_counts = (image_length + BAND - 1) // BAND
    band_starts = jnp.cumsum(band_counts) - band_counts
    used = jnp.sum(band_counts)
    passed = (slot_band[:, None] >= band_starts[None, :]).astype(jnp.int32)
    holder = jnp.sum(passed, axis=1) - 1
    picked = holder[:, None] == jnp.arange(images, dtype=jnp.int32)[None, :]
    first_band = jnp.sum(jnp.where(picked, band_starts[None, :], 0), axis=1)
    holder_length = jnp.sum(jnp.where(picked, image_length[None, :], 0), axis=1)
    slot_used = slot_band < used
    slot_valid = jnp.where(
        slot_used, jnp.clip(holder_length - (slot_band - first_band) * BAND, 0, BAND), 0
    )
    slot_at = jnp.where(slot_used, (slot_band + holder + 1) * BAND, 0)
    image_at = (band_starts + jnp.arange(images, dtype=jnp.int32)) * BAND
    slot_window = jnp.sum(jnp.where(picked, image_at[None, :], 0), axis=1)
    table = jnp.stack([slot_at, holder, slot_valid, slot_band * BAND])
    own_table = lax.dynamic_slice_in_dim(
        jnp.concatenate([table, slot_window[None], holder_length[None], first_band[None]]),
        seq_place * bands,
        bands,
        axis=1,
    )
    windows = jnp.concatenate([jnp.where(own_table[2] > 0, own_table[4], 0), image_at]).astype(
        jnp.int32
    )
    if seq_count == 8:
        origin = jnp.bitwise_xor(jnp.arange(8, dtype=jnp.int32), seq_place.astype(jnp.int32))
        slots = table.reshape(4, 8, bands)[:, origin].reshape(-1)
    else:
        origin = jnp.zeros((1,), jnp.int32)
        slots = table.reshape(-1)
    slots = slots.astype(jnp.int32)
    in_band = jnp.arange(BAND, dtype=jnp.int32)
    row_used = in_band[None, :] < own_table[2][:, None]
    row_image = jnp.where(row_used, own_table[1][:, None], -1).reshape(rows, 1)
    group_row = jnp.arange(special_rows, dtype=jnp.int32)
    special_used = group_row % GROUP < SPECIALS
    special_image = jnp.where(special_used, group_row // GROUP, -1)[:, None]
    all_image = jnp.concatenate([row_image, special_image], axis=0)
    first = (seq_place == 0).astype(f32)
    all_weight = jnp.concatenate([jnp.ones((rows,), f32), special_used.astype(f32) * first])[
        :, None
    ]
    own_weight = jnp.concatenate(
        [jnp.ones((quarter,), f32), special_used[:special].astype(f32) * first]
    )[:, None]
    weight_b = all_weight.astype(bf16)

    x_own = jnp.concatenate([patches, pad_special(specials, GROUP)], axis=0)
    x_parts = from_group(x_own)
    offset = jnp.where(own_table[5] == PATCH_BIG, 0, PATCH_BIG)
    position = offset[:, None] + (own_table[0] // BAND - own_table[1] - 1 - own_table[6])[
        :, None
    ] * BAND + in_band[None, :]
    position = jnp.where(row_used, position, 0).reshape(-1)
    pos_rows = jnp.where(row_used.reshape(-1, 1), pos_table[position], 0)
    w_cat = joined_columns(w_qkv[0], w_qkv[1], w_qkv[2], 1)
    b_cat = joined_columns(qv_bias[:1], jnp.zeros_like(qv_bias[:1]), qv_bias[1:], 1)
    w_out_pad = jnp.concatenate(
        [w_out[: 2 * DH], jnp.zeros_like(w_out[:DH]), w_out[2 * DH :]], axis=0
    )
    cot_all = jnp.concatenate([cot_patch, pad_special(cot_special, GROUP)], axis=0)
    grad_two = (cot_all.astype(f32) * layer_scale[1]).astype(bf16)
    grad_hidden = dot_nt(grad_two, w_down)
    grad_result = jnp.concatenate(
        [
            lax.dynamic_slice_in_dim(cot_patch, tp_place * quarter, quarter),
            pad_special(
                lax.dynamic_slice_in_dim(
                    cot_special, tp_place * specials.shape[0], specials.shape[0]
                ),
                GROUP,
            ),
        ],
        axis=0,
    ).astype(f32)

    stream, stream_own, normed, query, pack, key_own, value_own = call(
        functools.partial(embed_kernel, (tp_count, quarter, special, images)),
        [
            ((total, width), f32),
            ((block, width), f32),
            ((total, width), bf16),
            ((total, LANES), bf16),
            ((total, 384), bf16),
            ((total, LANES), bf16),
            ((total, LANES), bf16),
        ],
        [place, *x_parts, pos_rows, w_cat, b_cat, ln_gain[:1], ln_bias[:1], all_image],
    )
    w_outs = from_group(after(w_out_pad, x_parts))

    buffer_rows = (slot_count + images) * BAND + WINDOW
    pairs = from_bands(pack[:rows])
    keys, values, attended, attended_b, query = call(
        functools.partial(attend_kernel, (len(pairs), bands, images, rows)),
        [
            ((buffer_rows, LANES), bf16),
            ((buffer_rows, LANES), bf16),
            ((total, LANES), f32),
            ((total, LANES), bf16),
            ((total, LANES), bf16),
        ],
        [slots, windows, *pairs, key_own, value_own, query],
    )
    attended_all = from_group(attended_b)
    queries = from_bands(query[:rows])

    feed = call(
        functools.partial(feed_kernel, (tp_count, quarter, special)),
        [
            ((block, width), f32),
            ((block, width), f32),
            ((total, width), bf16),
            ((total, w_up.shape[1]), bf16),
            ((total, w_up.shape[1]), bf16),
            ((block, width), f32),
        ]
        + [((block, width), bf16)] * (tp_count - 1),
        [
            place,
            *attended_all,
            *w_outs,
            stream,
            layer_scale,
            branch_bias,
            ln_gain[1:],
            ln_bias[1:],
            w_up,
            up_bias[None],
            grad_hidden,
        ],
        [pltpu.VMEM((total, width), f32), pltpu.VMEM((total, width), f32)],
    )
    mid_own, one_own, normed_two, hidden, grad_pre = feed[:5]
    two_parts = to_group(feed[5:])

    back = call(
        functools.partial(mid_back_kernel, tp_count),
        [((block, width), f32), ((block, width), bf16), ((8, width), f32)]
        + [((block, LANES), bf16)] * tp_count,
        [
            *two_parts,
            mid_own,
            one_own,
            grad_result,
            own_weight,
            layer_scale,
            branch_bias,
            ln_gain[1:],
            *w_outs,
        ],
    )
    grad_mid, grad_one, early = back[:3]
    attn_parts = to_group(back[3:])
    (grad_attn,) = call(
        functools.partial(delta_kernel, (tp_count, quarter, special)),
        [((total, LANES), bf16)],
        [place, *attn_parts, attended],
        [pltpu.VMEM((total, LANES), f32)],
    )
    grads = from_bands(grad_attn[:rows])

    grad_two_w = grad_two * weight_b
    grad_pre_w = grad_pre * weight_b
    down_grad = dot_tn(hidden, grad_two_w)
    up_grad = dot_tn(normed_two, grad_pre_w)
    up_bias_grad = jnp.sum(grad_pre_w.astype(f32), axis=0)
    feed_sums = lax.psum(
        jnp.concatenate(
            [down_grad, up_grad, jnp.pad(up_bias_grad[None], ((0, 15), (0, 0)))], axis=0
        ).astype(bf16),
        "seq",
    ).astype(f32)
    ff = w_up.shape[1]
    down_grad, up_grad, up_bias_grad = (
        feed_sums[:ff],
        feed_sums[ff : ff + width],
        feed_sums[ff + width],
    )
    two_partial = after(dot(hidden, w_down).astype(bf16), attn_parts)
    two_blocks = []
    for k in range(tp_count):
        spot = lax.rem(tp_place + k, tp_count)
        two_blocks.append(
            jnp.concatenate(
                [
                    lax.dynamic_slice_in_dim(two_partial, spot * quarter, quarter),
                    lax.dynamic_slice_in_dim(two_partial, rows + spot * special, special),
                ],
                axis=0,
            )
        )
    branch_two = sum(b.astype(f32) for b in to_group(two_blocks)) + branch_bias[1]
    result = (mid_own + layer_scale[1] * branch_two).astype(bf16)
    weighted_result = grad_result * own_weight
    scale_grad_two = jnp.sum(weighted_result * branch_two, axis=0)
    bias_grad_two = jnp.sum(weighted_result, axis=0) * layer_scale[1]
    early_rows = jnp.concatenate(
        [jnp.zeros((2, width), f32), early[:4], scale_grad_two[None], bias_grad_two[None]], axis=0
    )
    grad_one_all = from_group(after(grad_one, attn_parts))

    (grad_query,) = call(
        functools.partial(query_grad_kernel, (bands, images, rows)),
        [((total, LANES), bf16)],
        [windows, query, grad_attn, keys, values],
    )
    pair = call(
        functools.partial(
            pair_grad_kernel, (len(grads), bands, images, tp_count, quarter, special)
        ),
        [((total, 640), bf16), ((block, width), f32)]
        + [((block, width), bf16)] * (tp_count - 1),
        [
            place,
            slots,
            windows,
            *queries,
            *grads,
            query,
            grad_attn,
            key_own,
            value_own,
            grad_query,
            w_cat,
        ],
        [
            pltpu.VMEM((buffer_rows, LANES), bf16),
            pltpu.VMEM((buffer_rows, LANES), bf16),
            pltpu.VMEM((total, width), f32),
        ],
        outside=(3, 4) if len(grads) == 1 else (),
    )
    joined = pair[0]
    normed_parts = to_group(pair[1:])

    joined_w = joined * weight_b
    qkv_grad = dot_tn(normed, joined_w)
    joined_bias = jnp.sum(joined_w.astype(f32), axis=0)
    out_grad = jnp.zeros((LANES, width), f32)
    for k in range(tp_count):
        spot = lax.rem(tp_place - k + tp_count, tp_count)
        piece = jnp.concatenate(
            [
                lax.dynamic_slice_in_dim(attended_b, spot * quarter, quarter),
                lax.dynamic_slice_in_dim(attended_b, rows + spot * special, special),
            ],
            axis=0,
        )
        out_grad = out_grad + dot_tn(piece, grad_one_all[k] * own_weight.astype(bf16))
    qkv_sums = lax.psum(
        jnp.concatenate([qkv_grad, jnp.pad(joined_bias[None], ((0, 15), (0, 0)))], axis=0).astype(
            bf16
        ),
        "seq",
    ).astype(f32)
    out_sums = lax.psum(out_grad.astype(bf16), "seq").astype(f32)
    out_grad = jnp.concatenate([out_sums[: 2 * DH], out_sums[3 * DH :]], axis=0)
    qkv_grad = jnp.stack(split_columns(qkv_sums[:width]))
    bias_q, _, bias_v = split_columns(qkv_sums[width : width + 1])
    qv_bias_grad = jnp.concatenate([bias_q, bias_v], axis=0)

    grad_stream, send, small = call(
        functools.partial(stream_back_kernel, (tp_count, quarter)),
        [((block, width), f32), ((quarter + 16, width), bf16), ((8, width), f32)],
        [*normed_parts, stream_own, grad_mid, own_weight, ln_gain[:1], early_rows],
    )
    if seq_count == 8:
        (sent,) = call(
            functools.partial(join_kernel, (tp_count, quarter)),
            [((rows + 16 * tp_count, width), bf16)],
            [place, *from_group(send)],
        )
        sent_all = from_bands(sent)
        images_at = jnp.concatenate(
            [band_starts * BAND, (image_length == PATCH_BIG).astype(jnp.int32)]
        ).astype(jnp.int32)
        pos_grad, small = call(
            functools.partial(position_kernel, (len(sent_all), images, rows, tp_count)),
            [((pos_table.shape[0], width), f32), ((8, width), f32)],
            [slots, images_at, origin, *sent_all],
            [
                pltpu.VMEM((slot_count * BAND, width), f32),
                pltpu.VMEM((seq_count * tp_count * 16, width), f32),
                pltpu.VMEM((BIG_BANDS * BAND, width), f32),
                pltpu.VMEM((-(-(pos_table.shape[0] - PATCH_BIG) // BAND) * BAND, width), f32),
            ],
        )
    else:
        mine = lax.dynamic_slice_in_dim(position, tp_place * quarter, quarter)
        used_mine = lax.dynamic_slice_in_dim(row_used.reshape(-1, 1), tp_place * quarter, quarter)
        local = jax.ops.segment_sum(
            jnp.where(used_mine, grad_stream[:quarter], 0.0),
            mine,
            num_segments=pos_table.shape[0],
        )
        pos_grad, small = lax.psum((local, small), ("seq", "tp"))
    return (
        result[:quarter],
        cut_special(result[quarter:]),
        grad_stream[:quarter],
        cut_special(grad_stream[quarter:]),
        pos_grad,
        qkv_grad,
        qv_bias_grad,
        out_grad,
        jnp.stack([small[5], small[7]]),
        jnp.stack([small[0], small[2]]),
        jnp.stack([small[1], small[3]]),
        jnp.stack([small[4], small[6]]),
        up_grad,
        up_bias_grad,
        down_grad,
    )


def solution(mesh):
    in_specs = (
        P(("seq", "tp"), None),
        P("tp", None),
        P(),
        P(),
        P(),
        P(None, None, "tp"),
        P(None, "tp"),
        P("tp", None),
        P(),
        P(),
        P(),
        P(),
        P(None, "tp"),
        P("tp"),
        P("tp", None),
        P("seq", None),
        P(),
    )
    out_specs = (
        P(("seq", "tp"), None),
        P("tp", None),
        P(("seq", "tp"), None),
        P("tp", None),
        P(),
        P(None, None, "tp"),
        P(None, "tp"),
        P("tp", None),
        P(),
        P(),
        P(),
        P(),
        P(None, "tp"),
        P("tp"),
        P("tp", None),
    )
    return jax.shard_map(
        on_device, mesh=mesh, in_specs=in_specs, out_specs=out_specs, check_vma=False
    )
```

```python
import functools

import jax
import jax.numpy as jnp
from jax import lax
from jax.experimental import pallas as pl
from jax.experimental.pallas import tpu as pltpu
from jax.sharding import PartitionSpec as P

DH = 64
SPECIALS = 5
PATCH_BIG = 1369
BAND = 64

GROUP = 16
LANES = 256
FAR = 1e30
EPS = 1e-06
BIG_BANDS = (PATCH_BIG + BAND - 1) // BAND
WINDOW = -(-(BIG_BANDS + 1) * BAND // 256) * 256
VMEM_LIMIT = 60 * 1024 * 1024

bf16 = jnp.bfloat16
f32 = jnp.float32


def dot(a, b):
    return jnp.dot(a, b, preferred_element_type=f32)


def dot_nt(a, b):
    return lax.dot_general(a, b, (((1,), (1,)), ((), ())), preferred_element_type=f32)


def dot_tn(a, b):
    return lax.dot_general(a, b, (((0,), (0,)), ((), ())), preferred_element_type=f32)


def lanes_of(shape):
    return lax.broadcasted_iota(jnp.int32, shape, len(shape) - 1)


def norm_parts(values):
    centre = jnp.mean(values, axis=-1, keepdims=True)
    centred = values - centre
    spread = jnp.mean(centred * centred, axis=-1, keepdims=True)
    scale = lax.rsqrt(spread + EPS)
    return centred * scale, scale


def norm_back(unit, scale, eg):
    first = jnp.mean(eg, axis=-1, keepdims=True)
    second = jnp.mean(eg * unit, axis=-1, keepdims=True)
    return scale * (eg - first - unit * second)


def key_head(lane, h):
    return (lane >= h * DH) & (lane < (h + 1) * DH)


def value_head(lane, h):
    start = (0, DH, 3 * DH)[h]
    return (lane >= start) & (lane < start + DH)


def key_side(lane, h, images):
    image_lane = (lane >= 3 * DH) & (lane <= 3 * DH + images)
    lse_start = 3 * DH + images + 1 + 3 * h
    return key_head(lane, h) | image_lane | ((lane >= lse_start) & (lane < lse_start + 3))


DELTA_LANE = 50


def value_side(lane, h):
    start = 2 * DH + DELTA_LANE + 3 * h
    return value_head(lane, h) | ((lane >= start) & (lane < start + 3))


def three_pieces(x):
    high = x.astype(bf16).astype(f32)
    rest = x - high
    middle = rest.astype(bf16).astype(f32)
    return high, middle, (rest - middle).astype(bf16).astype(f32)


def stacked(rows, picks):
    zero = jnp.zeros_like(rows)
    return jnp.concatenate([jnp.where(pick, rows, zero) for pick in picks], axis=0)


def spread_sum(stack, picks):
    count = stack.shape[0] // len(picks)
    total = None
    for h, pick in enumerate(picks):
        part = jnp.where(pick, stack[h * count : (h + 1) * count], 0.0)
        total = part if total is None else total + part
    return total


def call(body, outs, ins, scratch=(), outside=(), cost=2):
    spaces = []
    for i, item in enumerate(ins):
        smem = item.dtype == jnp.int32 and item.ndim == 1
        space = pl.ANY if i in outside else pltpu.SMEM if smem else pltpu.VMEM
        spaces.append(pl.BlockSpec(memory_space=space))
    out_spaces = [
        pl.BlockSpec(memory_space=pltpu.SMEM if d == jnp.int32 and len(s) == 1 else pltpu.VMEM)
        for s, d in outs
    ]
    return pl.pallas_call(
        body,
        out_shape=[jax.ShapeDtypeStruct(s, d) for s, d in outs],
        in_specs=spaces,
        out_specs=out_spaces,
        scratch_shapes=list(scratch),
        cost_estimate=pl.CostEstimate(
            flops=int(cost * 1e9), bytes_accessed=0, transcendentals=0
        ),
        compiler_params=pltpu.CompilerParams(vmem_limit_bytes=VMEM_LIMIT),
    )(*ins)


def for_each(count, body):
    if count <= 8:
        for i in range(count):
            body(i)
    else:

        def step(i, carry):
            body(i)
            return carry

        lax.fori_loop(0, count, step, 0)


def image_starts(images, length, held):
    def begin(i, start):
        held[i] = start
        return start + (length[i] + BAND - 1) // BAND

    return lax.fori_loop(0, images, begin, jnp.int32(0))


def band_facts(images, length, slot_band, held, used, slot):
    band = slot_band[slot]

    def look(i, state):
        image, first = state
        inside = band >= held[i]
        return jnp.where(inside, i, image), jnp.where(inside, held[i], first)

    state = (jnp.int32(0), jnp.int32(0))
    if images <= 8:
        for i in range(images):
            state = look(i, state)
    else:
        state = lax.fori_loop(0, images, look, state)
    image, first = state
    left = jnp.minimum(jnp.maximum(length[image] - (band - first) * BAND, 0), BAND)
    return band, image, first, jnp.where(band < used, left, 0)


def plan_kernel(sizes, length, slot_band, place, windows, spots, own, row_image, position, held):
    seq_count, bands, images, rows = sizes
    used = image_starts(images, length, held)

    def image_facts(i, carry):
        spots[i] = held[i] * BAND
        spots[images + i] = (length[i] == PATCH_BIG).astype(jnp.int32)
        windows[bands + i] = (held[i] + i) * BAND
        return carry

    lax.fori_loop(0, images, image_facts, 0)
    windows[bands + images] = (used + images) * BAND
    in_band = lax.broadcasted_iota(jnp.int32, (BAND, 1), 0)
    for u in range(bands):
        band, image, first, valid = band_facts(
            images, length, slot_band, held, used, place[1] * bands + u
        )
        windows[u] = jnp.where(valid > 0, (first + image) * BAND, 0)
        own[u] = jnp.where(valid > 0, (band - first) * BAND, 0)
        own[bands + u] = (length[image] == PATCH_BIG).astype(jnp.int32)
        good = in_band < valid
        row_image[u * BAND : (u + 1) * BAND] = jnp.where(good, image, -1)
        offset = jnp.where(length[image] == PATCH_BIG, 0, PATCH_BIG) + (band - first) * BAND
        position[u * BAND : (u + 1) * BAND] = jnp.where(good, offset + in_band, 0)
    group = lax.broadcasted_iota(jnp.int32, (images * GROUP, 1), 0)
    row_image[rows:] = jnp.where(group % GROUP < SPECIALS, group // GROUP, -1)


def slots_kernel(sizes, length, slot_band, place, slots, held):
    seq_count, bands, images = sizes
    slot_count = seq_count * bands
    used = image_starts(images, length, held)

    def put(i, carry):
        source = i // bands
        if seq_count == 8:
            source = jnp.bitwise_xor(source, place[1])
        band, image, _, valid = band_facts(
            images, length, slot_band, held, used, source * bands + i % bands
        )
        slots[i] = jnp.where(valid > 0, (band + image + 1) * BAND, 0)
        slots[slot_count + i] = image
        slots[2 * slot_count + i] = valid
        slots[3 * slot_count + i] = band * BAND
        return carry

    lax.fori_loop(0, slot_count, put, 0)


def gather_rows_kernel(patches, specials, out):
    quarter = patches.shape[0]
    out[:quarter] = patches[...]
    padding = jnp.zeros((GROUP - SPECIALS, patches.shape[1]), f32)
    for g in range(specials.shape[0] // SPECIALS):
        group = specials[g * SPECIALS : (g + 1) * SPECIALS].astype(f32)
        out[quarter + g * GROUP : quarter + (g + 1) * GROUP] = jnp.concatenate(
            [group, padding], axis=0
        ).astype(bf16)


def row_weight(count, patch_rows, seq):
    row = lax.broadcasted_iota(jnp.int32, (count, 1), 0)
    special = ((row - patch_rows) % GROUP < SPECIALS) & (seq == 0)
    return jnp.where((row < patch_rows) | special, 1.0, 0.0)


def embed_kernel(sizes, place, at_table, *refs):
    tp_count, quarter, special, images = sizes
    xs = refs[:tp_count]
    table, w_cat, b_cat, gain, shift, row_image = refs[tp_count : tp_count + 6]
    stream, own, normed, query, query_patch, pack, key_own, value_own, pos, low = refs[tp_count + 6 :]
    low[...] = table[PATCH_BIG:].astype(f32)
    bands = quarter * tp_count // BAND
    for u in range(bands):
        at = pl.multiple_of(at_table[u], BAND)
        good = row_image[u * BAND : (u + 1) * BAND] >= 0

        @pl.when(at_table[bands + u] > 0)
        def _(u=u, at=at, good=good):
            pos[u * BAND : (u + 1) * BAND] = jnp.where(
                good, table[pl.ds(at, BAND)].astype(f32), 0.0
            )

        @pl.when(at_table[bands + u] == 0)
        def _(u=u, at=at, good=good):
            pos[u * BAND : (u + 1) * BAND] = jnp.where(good, low[pl.ds(at, BAND)], 0.0)

    rows = quarter * tp_count
    me = place[0]
    for k in range(tp_count):
        spot = lax.rem(me - k + tp_count, tp_count)
        patch_at = pl.multiple_of(spot * quarter, 16)
        special_at = pl.multiple_of(rows + spot * special, 16)
        part = xs[k][:quarter].astype(f32) + pos[pl.ds(patch_at, quarter)]
        stream[pl.ds(patch_at, quarter)] = part
        tail = xs[k][quarter:].astype(f32)
        stream[pl.ds(special_at, special)] = tail
        if k == 0:
            own[:quarter] = part
            own[quarter:] = tail
    unit, _ = norm_parts(stream[...])
    rounded = (unit * gain[...] + shift[...]).astype(bf16)
    normed[...] = rounded
    projected = (dot_nt(rounded, w_cat[...]) + b_cat[...]).astype(bf16)
    image = row_image[...]
    total = image.shape[0]
    lane = lanes_of((total, LANES))
    image_lane = (lane >= 3 * DH) & (lane <= 3 * DH + images)
    scaled = projected[:, :LANES].astype(f32) * (DH**-0.5)
    far = jnp.where(image_lane & (lane != 3 * DH + image), FAR, 0.0)
    query[...] = jnp.where(lane < 3 * DH, scaled, far).astype(bf16)
    query_patch[...] = query[:rows]
    pack[...] = projected[:rows, LANES:]
    own_lane = 3 * DH + jnp.where(image < 0, images, image)
    lse_lane = (lane > 3 * DH + images) & (lane <= 3 * DH + images + 9)
    aux = jnp.where((lane == own_lane) | lse_lane, -1.0, 0.0)
    key_own[...] = jnp.where(
        lane < 3 * DH, projected[:, LANES : 2 * LANES].astype(f32), aux
    ).astype(bf16)
    half = lanes_of((total, 128))
    value_own[:, :128] = projected[:, 512:640]
    value_own[:, 128:] = jnp.where(
        half < DH,
        jnp.where((half >= DELTA_LANE) & (half < DELTA_LANE + 9), -1.0, 0.0),
        projected[:, 384:512].astype(f32),
    ).astype(bf16)


def clear_unused(clear, windows, bands, images, buffer_rows):
    lax.fori_loop(0, images, lambda i, c: clear(windows[bands + i], c), 0)
    lax.fori_loop(
        windows[bands + images] // BAND,
        windows[bands + images - 1] // BAND + WINDOW // BAND,
        lambda i, c: clear(i * BAND, c),
        0,
    )


def assemble_kernel(tp_count, place, whole, out):
    heads = 3 * DH
    for k in range(tp_count):
        at = pl.multiple_of(lax.rem(place[0] - k + tp_count, tp_count) * heads, DH)
        out[k, : 2 * DH] = whole[pl.ds(at, 2 * DH)]
        out[k, 2 * DH : 3 * DH] = jnp.zeros((DH, whole.shape[1]), bf16)
        out[k, 3 * DH : 4 * DH] = whole[pl.ds(pl.multiple_of(at + 2 * DH, DH), DH)]
        out[k, 4 * DH :] = jnp.zeros((DH, whole.shape[1]), bf16)


def out_grad_kernel(sizes, place, *refs):
    tp_count, quarter, special = sizes
    parts = refs[:tp_count]
    attended, out, whole = refs[tp_count:]
    rows = quarter * tp_count
    for k in range(tp_count):
        spot = lax.rem(place[0] - k + tp_count, tp_count)
        whole[pl.ds(pl.multiple_of(spot * quarter, 16), quarter)] = parts[k][:quarter]
        whole[pl.ds(pl.multiple_of(rows + spot * special, 16), special)] = parts[k][quarter : quarter + special]
    product = dot_tn(attended[...], whole[...]).astype(bf16)
    out[: 2 * DH] = product[: 2 * DH]
    out[2 * DH :] = product[3 * DH :]


def attend_kernel(sizes, slots, windows, *refs):
    blocks_count, bands, images, rows = sizes
    blocks = refs[:blocks_count]
    key_own, value_own, query = refs[blocks_count : blocks_count + 3]
    keys, values, attended, attended_b, packed, query_out = refs[blocks_count + 3 :]
    lane = lanes_of((1, LANES))
    lse_lane = (lane > 3 * DH + images) & (lane <= 3 * DH + images + 9)
    empty = jnp.where((lane == 3 * DH + images) | lse_lane, -1.0, 0.0)
    buffer_rows = keys.shape[0]

    def clear(at, carry):
        at = pl.multiple_of(at, BAND)
        keys[pl.ds(at, BAND)] = jnp.broadcast_to(empty, (BAND, LANES)).astype(bf16)
        values[pl.ds(at, BAND)] = jnp.zeros((BAND, LANES), bf16)
        return carry

    clear_unused(clear, windows, bands, images, buffer_rows)
    band_lane = lanes_of((BAND, LANES))
    half = lanes_of((BAND, 128))
    in_band = lax.broadcasted_iota(jnp.int32, (BAND, LANES), 0)
    band_lse = (band_lane > 3 * DH + images) & (band_lane <= 3 * DH + images + 9)
    delta_aux = jnp.where((half >= DELTA_LANE) & (half < DELTA_LANE + 9), -1.0, 0.0)
    per_block = blocks[0].shape[0] // BAND
    slot_count = blocks_count * per_block
    for b in range(blocks_count):

        def place(j, b=b):
            slot = b * per_block + j
            valid = slots[2 * slot_count + slot]

            @pl.when(valid > 0)
            def _():
                at = pl.multiple_of(slots[slot], BAND)
                image = slots[slot_count + slot]
                source = blocks[b][pl.ds(pl.multiple_of(j * BAND, BAND), BAND)]
                own_lane = 3 * DH + jnp.where(in_band < valid, image, images)
                aux = jnp.where((band_lane == own_lane) | band_lse, -1.0, 0.0)
                keys[pl.ds(at, BAND)] = jnp.where(
                    band_lane < 3 * DH, source[:, :LANES].astype(f32), aux
                ).astype(bf16)
                values[pl.ds(at, BAND), :128] = source[:, 256:384]
                values[pl.ds(at, BAND), 128:] = jnp.where(
                    half < DH, delta_aux, source[:, 128:256].astype(f32)
                ).astype(bf16)

        for_each(per_block, place)

    def place_special(i):
        at = pl.multiple_of(windows[bands + i], BAND)
        source = pl.ds(pl.multiple_of(rows + i * GROUP, GROUP), GROUP)
        keys[pl.ds(at, GROUP)] = key_own[source]
        values[pl.ds(at, GROUP)] = value_own[source]

    for_each(images, place_special)
    key_picks = [key_side(lane, h, images) for h in range(3)]
    value_picks = [value_head(lane, h) for h in range(3)]

    def unit(window, start, count):
        at = pl.multiple_of(windows[window], BAND)
        spot = pl.ds(start, count)
        own = query[spot]
        key_part = keys[pl.ds(at, WINDOW)]
        value_part = values[pl.ds(at, WINDOW)]
        scores = dot_nt(stacked(own, key_picks), key_part)
        top = jnp.maximum(jnp.max(scores, axis=-1, keepdims=True), -0.1 * FAR)
        weights = jnp.exp(scores - top)
        total = jnp.sum(weights, axis=-1, keepdims=True)
        usable = total > 0.0
        safe = jnp.where(usable, total, 1.0)
        summed = dot(weights.astype(bf16), value_part) / safe
        result = spread_sum(summed, value_picks)
        attended[spot] = result
        attended_b[spot] = result.astype(bf16)
        lse = jnp.where(usable, top + jnp.log(safe), 0.0)
        row = own.astype(f32)
        for h in range(3):
            for piece, part in enumerate(three_pieces(lse[h * count : (h + 1) * count])):
                row = jnp.where(lane == 3 * DH + images + 1 + 3 * h + piece, part, row)
        query_out[spot] = row.astype(bf16)

    for u in range(bands):
        unit(u, u * BAND, BAND)
    for_each(
        images,
        lambda i: unit(bands + i, pl.multiple_of(rows + i * GROUP, GROUP), GROUP),
    )
    total = query.shape[0]
    packed[:total] = attended_b[:, :128]
    upper = pltpu.roll(attended[: total // 2, 128:], DH, 1)
    lower = attended[total // 2 :, 128:]
    packed[total:] = jnp.where(lanes_of((1, 128)) < DH, upper, lower).astype(bf16)


def feed_kernel(sizes, place, *refs):
    tp_count, quarter, special = sizes
    attended = refs[:tp_count]
    w_outs, stream, scale, bias, gain, shift, w_up, up_bias, grad_hidden = refs[
        tp_count : tp_count + 9
    ]
    mid_own, one_own, normed, hidden_out, grad_pre_out, bias_out = refs[
        tp_count + 9 : tp_count + 15
    ]
    parts = refs[tp_count + 15 : 2 * tp_count + 15]
    mid, partial = refs[2 * tp_count + 15 :]
    rows = quarter * tp_count
    me = place[0]
    total = stream.shape[0]
    one = 0.0
    upper, lower = 0.0, 0.0
    for k in range(tp_count):
        one += dot(attended[k][:total], w_outs[k, : 2 * DH])
        upper += dot(attended[k][total:], w_outs[k, 3 * DH :])
        lower += dot(attended[k][total:], w_outs[k, 2 * DH : 4 * DH])
    one = one + jnp.concatenate([upper, lower], axis=0)
    partial[...] = one
    value = stream[...] + scale[0:1] * (one + bias[0:1])
    mid[...] = value
    own_patch = pl.ds(pl.multiple_of(me * quarter, 16), quarter)
    own_special = pl.ds(pl.multiple_of(rows + me * special, 16), special)
    mid_own[:quarter] = mid[own_patch]
    mid_own[quarter:] = mid[own_special]
    one_own[:quarter] = partial[own_patch]
    one_own[quarter:] = partial[own_special]
    unit, _ = norm_parts(value)
    rounded = (unit * gain[...] + shift[...]).astype(bf16)
    normed[...] = rounded
    pre = dot(rounded, w_up[...]) + up_bias[...]
    share = 0.5 * (1.0 + lax.erf(pre * (0.5**0.5)))
    hidden_out[...] = (pre * share).astype(bf16)
    slope = share + pre * jnp.exp(-0.5 * pre * pre) * (0.5 / jnp.pi) ** 0.5
    grad_pre = (grad_hidden[...] * slope).astype(bf16)
    weight = row_weight(value.shape[0], rows, place[1])
    weighted = grad_pre.astype(f32) * weight
    grad_pre_out[...] = weighted.astype(bf16)
    bias_out[...] = jnp.broadcast_to(jnp.sum(weighted, axis=0, keepdims=True), bias_out.shape).astype(bf16)
    partial[...] = dot_nt(grad_pre, w_up[...])
    send_blocks(me, parts, partial, quarter, special)


def feed_grad_kernel(sizes, place, *refs):
    tp_count, quarter, special = sizes
    hidden, normed, grad_two, grad_pre, w_down, grad_result, out, sums = refs[:8]
    two_blocks = refs[8 : 8 + tp_count]
    partial = refs[-1]
    ff, width = hidden.shape[1], normed.shape[1]
    out[:ff] = dot_tn(hidden[...], grad_two[...]).astype(bf16)
    out[ff : ff + width] = dot_tn(normed[...], grad_pre[...]).astype(bf16)
    two = dot(hidden[...], w_down[...])
    sums[...] = jnp.broadcast_to(
        jnp.sum(two * grad_result[...].astype(f32), axis=0, keepdims=True), sums.shape
    )
    partial[...] = two
    send_blocks(place[0], two_blocks, partial, quarter, special)


def proj_grad_kernel(parts, place, normed, joined, bias, out_grad, up_bias, keep, send, whole):
    columns = joined.shape[1]
    whole[:columns] = dot_tn(joined[...], normed[...])
    whole[columns : columns + 16, :columns] = bias[...].astype(f32)
    whole[columns : columns + 16, columns:] = jnp.zeros((16, normed.shape[1] - columns), f32)
    start = columns + 16 + out_grad.shape[0]
    whole[columns + 16 : start] = out_grad[...].astype(f32)
    whole[start : start + 16] = up_bias[...].astype(f32)
    whole[start + 16 :] = jnp.zeros((whole.shape[0] - start - 16, normed.shape[1]), f32)
    half = keep.shape[0]
    core = lax.rem(place[1], parts) if parts == 2 else 0
    keep[...] = whole[pl.ds(pl.multiple_of(core * half, 16), half)]
    send[...] = whole[pl.ds(pl.multiple_of((1 - core) * half if parts == 2 else 0, 16), half)].astype(bf16)


def chip_parts_kernel(place, keep, received, mine, *sends_and_whole):
    *sends, whole = sends_and_whole
    whole[...] = keep[...] + received[...].astype(f32)
    part = mine.shape[0]
    chip = place[1] // 2
    mine[...] = whole[pl.ds(pl.multiple_of(chip * part, 16), part)]
    for i, send in enumerate(sends):
        at = pl.multiple_of(jnp.bitwise_xor(chip, i + 1) * part, 16)
        send[...] = whole[pl.ds(at, part)].astype(bf16)


def add_parts_kernel(mine, first, second, third, out):
    total = mine[...] + first[...].astype(f32) + second[...].astype(f32) + third[...].astype(f32)
    out[...] = total.astype(bf16)


def split_kernel(place, *refs):
    *blocks, out, bias, out_w, up_bias, sums = refs
    part = blocks[0].shape[0]
    if len(blocks) == 1:
        sums[...] = blocks[0][...]
    else:
        for k, block in enumerate(blocks):
            source = jnp.bitwise_xor(place[1], k)
            at = (lax.rem(source, 2) * (len(blocks) // 2) + source // 2) * part
            sums[pl.ds(pl.multiple_of(at, 16), part)] = block[...]
    out[0] = sums[: 3 * DH].astype(f32)
    out[1] = sums[4 * DH : 7 * DH].astype(f32)
    out[2, : 2 * DH] = sums[8 * DH : 10 * DH].astype(f32)
    out[2, 2 * DH :] = sums[7 * DH : 8 * DH].astype(f32)
    tail = sums[10 * DH : 10 * DH + 8].astype(f32)
    third = pltpu.roll(tail[:, 384:512], DH, 1)
    bias[0:1] = tail[0:1, : 3 * DH]
    bias[1:2, :128] = tail[0:1, 512:640]
    bias[1:2, 128:] = third[0:1, :DH]
    start = 10 * DH + 16
    out_w[...] = sums[start : start + out_w.shape[0]].astype(f32)
    start += out_w.shape[0]
    up_bias[...] = sums[start : start + 8].astype(f32)


def send_blocks(me, parts, partial, quarter, special):
    tp_count = len(parts)
    rows = quarter * tp_count
    for k in range(tp_count):
        spot = lax.rem(me + k, tp_count)
        patch_at = pl.ds(pl.multiple_of(spot * quarter, 16), quarter)
        special_at = pl.ds(pl.multiple_of(rows + spot * special, 16), special)
        parts[k][:quarter] = partial[patch_at].astype(parts[k].dtype)
        parts[k][quarter:] = partial[special_at].astype(parts[k].dtype)


def mid_back_kernel(sizes, place, *refs):
    tp_count, quarter = sizes
    parts = refs[:tp_count]
    mid, one, grad_result, scale, bias, gain, w_outs = refs[tp_count : tp_count + 7]
    grad_mid_out, grad_one_out, small = refs[tp_count + 7 : tp_count + 10]
    sends = refs[tp_count + 10 :]
    weight = row_weight(mid.shape[0], quarter, place[1])
    incoming = parts[0][...]
    for k in range(1, tp_count):
        incoming += parts[k][...].astype(f32)
    unit, scaling = norm_parts(mid[...])
    grad_mid = grad_result[...] + norm_back(unit, scaling, incoming * gain[...])
    weighted = incoming * weight
    weighted_mid = grad_mid * weight
    small[0:1] = jnp.sum(weighted * unit, axis=0, keepdims=True)
    small[1:2] = jnp.sum(weighted, axis=0, keepdims=True)
    small[2:3] = jnp.sum(weighted_mid * (one[...] + bias[0:1]), axis=0, keepdims=True)
    small[3:4] = jnp.sum(weighted_mid, axis=0, keepdims=True) * scale[0:1]
    small[4:8] = jnp.zeros((4, small.shape[1]), f32)
    grad_mid_out[...] = grad_mid
    grad_one = (grad_mid * scale[0:1]).astype(bf16)
    grad_one_out[...] = (grad_one.astype(f32) * weight).astype(bf16)
    for k in range(tp_count):
        sends[k][...] = dot_nt(grad_one, w_outs[(tp_count - k) % tp_count, :LANES]).astype(bf16)


def delta_kernel(sizes, place, *refs):
    tp_count, quarter, special, images = sizes
    parts = refs[:tp_count]
    attended, query, out, out_patch, whole = refs[tp_count:]
    rows = quarter * tp_count
    me = place[0]
    for k in range(tp_count):
        spot = lax.rem(me - k + tp_count, tp_count)
        whole[pl.ds(pl.multiple_of(spot * quarter, 16), quarter)] = parts[k][:quarter].astype(f32)
        whole[pl.ds(pl.multiple_of(rows + spot * special, 16), special)] = parts[k][
            quarter:
        ].astype(f32)
    value = whole[...]
    total = value.shape[0]
    product = value * attended[...]
    lane = lanes_of(value.shape)
    for h in range(3):
        delta = jnp.sum(jnp.where(value_head(lane, h), product, 0.0), axis=-1, keepdims=True)
        for piece, part in enumerate(three_pieces(delta)):
            value = jnp.where(lane == 2 * DH + DELTA_LANE + 3 * h + piece, part, value)
    lse = jnp.concatenate(
        [jnp.zeros((total, 128), f32), pltpu.roll(query[:, 128:].astype(f32), DH, 1)], axis=1
    )
    lse_lane = (lane > 2 * DH + images) & (lane <= 2 * DH + images + 9)
    value = jnp.where(lse_lane, lse, value)
    out[...] = value.astype(bf16)
    out_patch[...] = value[:rows].astype(bf16)


def query_grad_kernel(sizes, windows, query, grad, keys, values, out):
    bands, images, rows = sizes
    lane = lanes_of((1, LANES))
    key_picks = [key_side(lane, h, images) for h in range(3)]
    value_picks = [value_side(lane, h) for h in range(3)]
    head_picks = [key_head(lane, h) for h in range(3)]

    def unit(window, start, count):
        at = pl.multiple_of(windows[window], BAND)
        spot = pl.ds(start, count)
        key_part = keys[pl.ds(at, WINDOW)]
        probs = jnp.exp(dot_nt(stacked(query[spot], key_picks), key_part))
        pulled = dot_nt(stacked(grad[spot], value_picks), values[pl.ds(at, WINDOW)])
        scores = (probs * pulled).astype(bf16)
        result = spread_sum(dot(scores, key_part), head_picks) * DH**-0.5
        out[spot] = result.astype(bf16)

    for u in range(bands):
        unit(u, u * BAND, BAND)
    for_each(
        images,
        lambda i: unit(bands + i, pl.multiple_of(rows + i * GROUP, GROUP), GROUP),
    )


def pair_grad_kernel(sizes, place, slots, windows, *refs):
    blocks_count, bands, images, tp_count, quarter, special = sizes
    query_blocks = refs[:blocks_count]
    grad_blocks = refs[blocks_count : 2 * blocks_count]
    rest = refs[2 * blocks_count :]
    query_own, grad_own, key_own, value_own, grad_query, w_cat, joined_out, bias_out = rest[:8]
    parts = rest[8 : 8 + tp_count]
    queries, grads, joined, partial = rest[8 + tp_count :]
    rows = quarter * tp_count
    lane = lanes_of((1, LANES))
    image_lane = (lane >= 3 * DH) & (lane <= 3 * DH + images)
    empty = jnp.where(image_lane, FAR, 0.0)
    half_lane = lanes_of((1, 128))
    lse_half = (half_lane > DH + images) & (half_lane <= DH + images + 9)

    def clear(at, carry):
        at = pl.multiple_of(at, BAND)
        queries[pl.ds(at, BAND)] = jnp.broadcast_to(empty, (BAND, LANES)).astype(bf16)
        grads[pl.ds(at, BAND)] = jnp.zeros((BAND, LANES), bf16)
        return carry

    clear_unused(clear, windows, bands, images, queries.shape[0])
    per_block = query_blocks[0].shape[0] // BAND
    slot_count = blocks_count * per_block
    for b in range(blocks_count):

        def put(j, b=b):
            slot = b * per_block + j

            @pl.when(slots[2 * slot_count + slot] > 0)
            def _():
                at = pl.multiple_of(slots[slot], BAND)
                source = pl.ds(pl.multiple_of(j * BAND, BAND), BAND)
                if blocks_count == 1:
                    pltpu.sync_copy(query_blocks[b].at[source], queries.at[pl.ds(at, BAND)])
                    pltpu.sync_copy(grad_blocks[b].at[source], grads.at[pl.ds(at, BAND)])
                    taken = grads[pl.ds(at, BAND), 128:]
                    held = queries[pl.ds(at, BAND), 128:]
                else:
                    grads[pl.ds(at, BAND)] = grad_blocks[b][source]
                    queries[pl.ds(at, BAND), :128] = query_blocks[b][source, :128]
                    taken = grad_blocks[b][source, 128:]
                    held = query_blocks[b][source, 128:]
                lse = pltpu.roll(taken.astype(f32), DH, 1)
                queries[pl.ds(at, BAND), 128:] = jnp.where(
                    lse_half, lse, held.astype(f32)
                ).astype(bf16)

        for_each(per_block, put)

    def put_special(i):
        at = pl.multiple_of(windows[bands + i], BAND)
        source = pl.ds(pl.multiple_of(rows + i * GROUP, GROUP), GROUP)
        queries[pl.ds(at, GROUP)] = query_own[source]
        grads[pl.ds(at, GROUP)] = grad_own[source]

    for_each(images, put_special)
    key_picks = [key_side(lane, h, images) for h in range(3)]
    value_picks = [value_side(lane, h) for h in range(3)]
    key_heads = [key_head(lane, h) for h in range(3)]
    value_heads = [value_head(lane, h) for h in range(3)]

    def unit(window, start, count):
        at = pl.multiple_of(windows[window], BAND)
        spot = pl.ds(start, count)
        query_part = queries[pl.ds(at, WINDOW)]
        grad_part = grads[pl.ds(at, WINDOW)]
        probs = jnp.exp(dot_nt(stacked(key_own[spot], key_picks), query_part))
        pulled = dot_nt(stacked(value_own[spot], value_picks), grad_part)
        scores = (probs * pulled).astype(bf16)
        grad_key = spread_sum(dot(scores, query_part), key_heads)
        grad_value = spread_sum(dot(probs.astype(bf16), grad_part), value_heads)
        joined[spot, 256:384] = grad_key[:, :128].astype(bf16)
        half = lanes_of((count, 128))
        joined[spot, 384:512] = jnp.where(half < DH, grad_key[:, 128:], grad_value[:, 128:]).astype(
            bf16
        )
        joined[spot, 512:640] = grad_value[:, :128].astype(bf16)

    joined[:, :256] = grad_query[...]
    for u in range(bands):
        unit(u, u * BAND, BAND)
    for_each(
        images,
        lambda i: unit(bands + i, pl.multiple_of(rows + i * GROUP, GROUP), GROUP),
    )
    partial[...] = dot(joined[...], w_cat[...])
    send_blocks(place[0], parts, partial, quarter, special)
    weighted = joined[...].astype(f32) * row_weight(joined.shape[0], rows, place[1])
    joined_out[...] = weighted.astype(bf16)
    bias_out[...] = jnp.broadcast_to(jnp.sum(weighted, axis=0, keepdims=True), bias_out.shape).astype(bf16)


def stream_back_kernel(sizes, place, *refs):
    tp_count, quarter = sizes
    parts = refs[:tp_count]
    stream, grad_mid, gain, early = refs[tp_count : tp_count + 4]
    two_blocks = refs[tp_count + 4 : 2 * tp_count + 3]
    out, send, small = refs[2 * tp_count + 3 : 2 * tp_count + 6]
    merged = refs[2 * tp_count + 6 :]
    weight = row_weight(stream.shape[0], quarter, place[1])
    incoming = parts[0][...]
    for k in range(1, tp_count):
        incoming += parts[k][...].astype(f32)
    unit, scaling = norm_parts(stream[...])
    result = grad_mid[...] + norm_back(unit, scaling, incoming * gain[...])
    out[...] = result
    weighted = incoming * weight
    first = jnp.sum(weighted * unit, axis=0, keepdims=True)
    second = jnp.sum(weighted, axis=0, keepdims=True)
    sums = jnp.concatenate([first, second, early[2:8]], axis=0)
    small[...] = sums
    send[:quarter] = result[:quarter].astype(bf16)
    send[quarter:] = sums.astype(bf16)
    block = stream.shape[0]
    for target, two in zip(merged, two_blocks):
        target[:block] = two[...]
        target[block:] = send[...]


def position_kernel(sizes, place, slots, spots, *refs):
    seq_count, tp_count, images, rows = sizes
    blocks = refs[: tp_count * seq_count]
    out, *smalls, ordered, tiny = refs[tp_count * seq_count :]
    bands = rows // BAND
    slot_count = seq_count * bands
    quarter = rows // tp_count
    piece = 32
    in_piece = lax.broadcasted_iota(jnp.int32, (piece, 1), 0)
    for c in range(tp_count):
        tp = lax.rem(place[0] - c + tp_count, tp_count)
        for k in range(seq_count):
            block = blocks[c * seq_count + k]
            seq = jnp.bitwise_xor(place[1], k)
            tiny[pl.ds(pl.multiple_of((seq * tp_count + tp) * 8, 8), 8)] = block[
                quarter : quarter + 8
            ].astype(f32)
            for r in range(quarter // piece):
                spot = tp * (quarter // piece) + r
                slot = k * bands + spot // 2
                shift = (spot % 2) * piece
                at = pl.multiple_of(slots[3 * slot_count + slot] + shift, piece)
                valid = slots[2 * slot_count + slot] - shift
                ordered[pl.ds(at, piece)] = jnp.where(
                    in_piece < valid, block[r * piece : (r + 1) * piece].astype(f32), 0.0
                )
    total = tiny[0:8]
    for i in range(1, seq_count * tp_count):
        total += tiny[i * 8 : (i + 1) * 8]
    for out_small, first, second in zip(smalls, (5, 0, 1, 4), (7, 2, 3, 6)):
        out_small[0:1] = total[first : first + 1]
        out_small[1:2] = total[second : second + 1]
    low_rows = out.shape[0] - PATCH_BIG
    seen_big, seen_low = jnp.int32(0), jnp.int32(0)
    for i in range(images):
        at = pl.multiple_of(spots[i], BAND)
        is_big = spots[images + i]
        seen = jnp.where(is_big > 0, seen_big, seen_low)

        @pl.when((is_big > 0) & (seen == 0))
        def _():
            out[:PATCH_BIG] = ordered[pl.ds(at, BIG_BANDS * BAND)][:PATCH_BIG]

        @pl.when((is_big > 0) & (seen > 0))
        def _():
            out[:PATCH_BIG] += ordered[pl.ds(at, BIG_BANDS * BAND)][:PATCH_BIG]

        @pl.when((is_big == 0) & (seen == 0))
        def _():
            out[PATCH_BIG:] = ordered[pl.ds(at, low_rows)]

        @pl.when((is_big == 0) & (seen > 0))
        def _():
            out[PATCH_BIG:] += ordered[pl.ds(at, low_rows)]

        seen_big += is_big
        seen_low += 1 - is_big


def rotated(x, k):
    count = lax.axis_size("tp")
    return lax.ppermute(x, "tp", [(i, (i + k) % count) for i in range(count)])


def from_group(x):
    return [x] + [rotated(x, k) for k in range(1, lax.axis_size("tp"))]


def to_group(blocks):
    return [blocks[0]] + [rotated(blocks[k], k) for k in range(1, len(blocks))]


def partner(x, k):
    count = lax.axis_size("seq")
    return lax.ppermute(x, "seq", [(i, i ^ k) for i in range(count)])


def from_chips(x):
    if lax.axis_size("seq") != 8:
        return [lax.all_gather(x, "seq", axis=0, tiled=True)]
    return [x] + [partner(x, k) for k in (2, 4, 6)]


def with_other_core(blocks):
    if len(blocks) == 1:
        return blocks
    odd = [partner(block, 1) for block in blocks]
    return [block for pair in zip(blocks, odd) for block in pair]


def from_bands(x):
    return with_other_core(from_chips(x))


def after(value, *others):
    return lax.optimization_barrier((value,) + tuple(others))[0]


def pad_special(rows, group):
    width = rows.shape[1]
    grouped = rows.reshape(-1, SPECIALS, width)
    return jnp.pad(grouped, ((0, 0), (0, group - SPECIALS), (0, 0))).reshape(-1, width)


def cut_special(rows):
    width = rows.shape[1]
    return rows.reshape(-1, GROUP, width)[:, :SPECIALS].reshape(-1, width)


def joined_columns(query, key, value, axis):
    cut = functools.partial(lax.slice_in_dim, axis=axis)
    return jnp.concatenate(
        [
            query,
            jnp.zeros_like(cut(query, 0, DH)),
            key,
            cut(value, 2 * DH, 3 * DH),
            cut(value, 0, 2 * DH),
        ],
        axis=axis,
    )


def on_device(
    patches,
    specials,
    pos_table,
    image_length,
    slot_band,
    w_qkv,
    qv_bias,
    w_out,
    branch_bias,
    ln_gain,
    ln_bias,
    layer_scale,
    w_up,
    up_bias,
    w_down,
    cot_patch,
    cot_special,
):
    seq_count = lax.axis_size("seq")
    tp_count = lax.axis_size("tp")
    seq_place = lax.axis_index("seq")
    tp_place = lax.axis_index("tp")
    near = seq_count == 8
    quarter, width = patches.shape
    ff = w_up.shape[1]
    images = image_length.shape[0]
    rows = quarter * tp_count
    bands = rows // BAND
    slot_count = slot_band.shape[0]
    special = (specials.shape[0] // SPECIALS) * GROUP
    special_rows = special * tp_count
    total = rows + special_rows
    block = quarter + special
    place = jnp.stack([tp_place, seq_place]).astype(jnp.int32)

    (x_own,) = call(gather_rows_kernel, [((block, width), bf16)], [patches, specials], cost=1)
    x_parts = from_group(x_own)
    windows, spots, at_table, row_image, position = call(
        functools.partial(plan_kernel, (seq_count, bands, images, rows)),
        [
            ((bands + images + 1,), jnp.int32),
            ((2 * images,), jnp.int32),
            ((2 * bands,), jnp.int32),
            ((total, 1), jnp.int32),
            ((rows, 1), jnp.int32),
        ],
        [image_length, slot_band, place],
        [pltpu.SMEM((images,), jnp.int32)],
    )
    w_cat = joined_columns(*jnp.transpose(w_qkv, (0, 2, 1)), 0)
    b_cat = joined_columns(qv_bias[:1], jnp.zeros_like(qv_bias[:1]), qv_bias[1:], 1)
    stream, stream_own, normed, query, query_patch, pack, key_own, value_own = call(
        functools.partial(embed_kernel, (tp_count, quarter, special, images)),
        [
            ((total, width), f32),
            ((block, width), f32),
            ((total, width), bf16),
            ((total, LANES), bf16),
            ((rows, LANES), bf16),
            ((rows, 384), bf16),
            ((total, LANES), bf16),
            ((total, LANES), bf16),
        ],
        [place, at_table, *x_parts, pos_table, w_cat, b_cat, ln_gain[:1], ln_bias[:1], row_image],
        [
            pltpu.VMEM((rows, width), f32),
            pltpu.VMEM((pos_table.shape[0] - PATCH_BIG, width), f32),
        ],
        cost=4,
    )

    pair_chips = from_chips(pack)
    pairs = with_other_core(pair_chips)
    query_chips = from_chips(after(query_patch, *pair_chips)) if near else []
    queries = with_other_core(query_chips) if near else []
    (slots,) = call(
        functools.partial(slots_kernel, (seq_count, bands, images)),
        [((4 * slot_count,), jnp.int32)],
        [image_length, slot_band, after(place, pack)],
        [pltpu.SMEM((images,), jnp.int32)],
        cost=4,
    )
    w_all = lax.all_gather(after(w_out, *x_parts), "tp", axis=0, tiled=True)
    (w_outs,) = call(
        functools.partial(assemble_kernel, tp_count),
        [((tp_count, LANES + DH, width), bf16)],
        [place, w_all],
    )
    w_down_late, cot_patch_late, cot_special_late = lax.optimization_barrier(
        (w_down, cot_patch, cot_special, pack)
    )[:3]
    cot_all = jnp.concatenate([cot_patch_late, pad_special(cot_special_late, GROUP)], axis=0)
    grad_two = (cot_all.astype(f32) * layer_scale[1]).astype(bf16)
    grad_hidden = dot_nt(grad_two, w_down_late)
    special_first = (jnp.arange(special_rows) % GROUP < SPECIALS) & (seq_place == 0)
    weight = jnp.concatenate([jnp.ones((rows,), f32), special_first.astype(f32)])[:, None]
    cot_weighted = cot_all * weight.astype(bf16)
    grad_two_w = grad_two * weight.astype(bf16)
    grad_result = jnp.concatenate(
        [
            lax.dynamic_slice_in_dim(cot_patch_late, tp_place * quarter, quarter),
            lax.dynamic_slice_in_dim(cot_all, rows + tp_place * special, special),
        ],
        axis=0,
    ).astype(f32)

    buffer_rows = (slot_count + images) * BAND + WINDOW
    keys, values, attended, attended_b, packed, query = call(
        functools.partial(attend_kernel, (len(pairs), bands, images, rows)),
        [
            ((buffer_rows, LANES), bf16),
            ((buffer_rows, LANES), bf16),
            ((total, LANES), f32),
            ((total, LANES), bf16),
            ((total + total // 2, 128), bf16),
            ((total, LANES), bf16),
        ],
        [slots, windows, *pairs, key_own, value_own, query],
        cost=10,
    )
    attended_all = from_group(packed)

    feed = call(
        functools.partial(feed_kernel, (tp_count, quarter, special)),
        [
            ((block, width), f32),
            ((block, width), f32),
            ((total, width), bf16),
            ((total, ff), bf16),
            ((total, ff), bf16),
            ((16, ff), bf16),
            ((block, width), f32),
        ]
        + [((block, width), bf16)] * (tp_count - 1),
        [
            place,
            *attended_all,
            w_outs,
            after(stream, *query_chips),
            layer_scale,
            branch_bias,
            ln_gain[1:],
            ln_bias[1:],
            w_up,
            up_bias[None],
            grad_hidden,
        ],
        [pltpu.VMEM((total, width), f32), pltpu.VMEM((total, width), f32)],
        cost=7,
    )
    mid_own, one_own, normed_two, hidden, grad_pre, up_bias_grad = feed[:6]
    two_parts = to_group(feed[6:])
    feed_grads, two_sums, *two_blocks = call(
        functools.partial(feed_grad_kernel, (tp_count, quarter, special)),
        [((ff + width, width), bf16), ((8, width), f32), ((block, width), f32)]
        + [((block, width), bf16)] * (tp_count - 1),
        [place, after(hidden, two_parts[1]), normed_two, grad_two_w, grad_pre, w_down, cot_weighted],
        [pltpu.VMEM((total, width), f32)],
        cost=5,
    )
    feed_sums = lax.psum(feed_grads, "seq")

    back = call(
        functools.partial(mid_back_kernel, (tp_count, quarter)),
        [((block, width), f32), ((block, width), bf16), ((8, width), f32)]
        + [((block, LANES), bf16)] * tp_count,
        [
            place,
            *two_parts,
            after(mid_own, feed_grads, *queries),
            one_own,
            grad_result,
            layer_scale,
            branch_bias,
            ln_gain[1:],
            w_outs,
        ],
        cost=4,
    )
    grad_mid, grad_one, early = back[:3]
    attn_parts = to_group(back[3:])
    grad_attn, grad_patch = call(
        functools.partial(delta_kernel, (tp_count, quarter, special, images)),
        [((total, LANES), bf16), ((rows, LANES), bf16)],
        [place, *attn_parts, attended, query],
        [pltpu.VMEM((total, LANES), f32)],
    )
    grad_chips = from_chips(grad_patch) if near else []
    grad_one_all = [grad_one, rotated(after(grad_one, grad_patch), 1)]
    (grad_query,) = call(
        functools.partial(query_grad_kernel, (bands, images, rows)),
        [((total, LANES), bf16)],
        [windows, query, grad_attn, keys, values],
        cost=10,
    )

    one_late = after(grad_one, grad_query)
    grad_one_all += [rotated(one_late, k) for k in range(2, tp_count)]
    own_special_weight = ((jnp.arange(special) % GROUP < SPECIALS) & (seq_place == 0)).astype(f32)
    own_weight = jnp.concatenate([jnp.ones((quarter,), f32), own_special_weight])[:, None]
    weighted_result = grad_result * own_weight
    result_sum = jnp.sum(weighted_result, axis=0)
    scale_grad_two = two_sums[0] + result_sum * branch_bias[1]
    bias_grad_two = result_sum * layer_scale[1]
    early_rows = jnp.concatenate(
        [jnp.zeros((2, width), f32), early[:4], scale_grad_two[None], bias_grad_two[None]], axis=0
    )
    if near:
        grads = [grad_patch, partner(grad_patch, 1)] + with_other_core(
            [after(chip, grad_query) for chip in grad_chips[1:]]
        )
    else:
        queries = from_chips(after(query_patch, grad_query))
        grads = from_chips(after(grad_patch, grad_query))
    pair = call(
        functools.partial(
            pair_grad_kernel, (len(grads), bands, images, tp_count, quarter, special)
        ),
        [((total, 640), bf16), ((16, 640), bf16), ((block, width), f32)]
        + [((block, width), bf16)] * (tp_count - 1),
        [
            place,
            slots,
            windows,
            *queries,
            *grads,
            query,
            grad_attn,
            key_own,
            value_own,
            grad_query,
            w_cat,
        ],
        [
            pltpu.VMEM((buffer_rows, LANES), bf16),
            pltpu.VMEM((buffer_rows, LANES), bf16),
            pltpu.VMEM((total, 640), bf16),
            pltpu.VMEM((total, width), f32),
        ],
        outside=(3, 4) if len(grads) == 1 else (),
        cost=14,
    )
    joined, joined_bias = pair[:2]
    normed_parts = to_group(pair[2:])
    (out_grad,) = call(
        functools.partial(out_grad_kernel, (tp_count, quarter, special)),
        [((w_out.shape[0], width), bf16)],
        [place, *grad_one_all, after(attended_b, joined)],
        [pltpu.VMEM((total, width), bf16)],
    )
    last_rows = -(-(640 + 32 + w_out.shape[0]) // 128) * 128
    held = last_rows // 2 if near else last_rows
    keep_last, send_last = call(
        functools.partial(proj_grad_kernel, 2 if near else 1),
        [((held, width), f32), ((held, width), bf16)],
        [place, normed, joined, joined_bias, out_grad, up_bias_grad],
        [pltpu.VMEM((last_rows, width), f32)],
        cost=2,
    )
    if near:
        part = last_rows // 8
        mine, *sends = call(
            chip_parts_kernel,
            [((part, width), f32)] + [((part, width), bf16)] * 3,
            [place, keep_last, partner(after(send_last, feed_sums), 1)],
            [pltpu.VMEM((last_rows // 2, width), f32)],
            cost=1,
        )
        received = [partner(block, k) for block, k in zip(sends, (2, 4, 6))]
        (reduced,) = call(add_parts_kernel, [((part, width), bf16)], [mine, *received], cost=1)
        last_blocks = from_bands(reduced)
    else:
        last_blocks = [lax.psum(send_last, "seq")]

    grad_stream, send, small, *merged = call(
        functools.partial(stream_back_kernel, (tp_count, quarter)),
        [((block, width), f32), ((quarter + 8, width), bf16), ((8, width), f32)]
        + [((block + quarter + 8, width), bf16)] * (tp_count - 1),
        [
            place,
            *normed_parts,
            after(stream_own, keep_last),
            grad_mid,
            ln_gain[:1],
            early_rows,
            *two_blocks[1:],
        ],
        cost=3,
    )
    arrived = [rotated(part, k + 1) for k, part in enumerate(merged)]
    branch_two = two_blocks[0] + sum(part[:block].astype(f32) for part in arrived)
    result = (mid_own + layer_scale[1] * (branch_two + branch_bias[1])).astype(bf16)
    if near:
        sent = from_bands(send)
        for part in arrived:
            sent += from_bands(part[block:])
        pos_grad, *smalls = call(
            functools.partial(position_kernel, (seq_count, tp_count, images, rows)),
            [((pos_table.shape[0], width), f32)] + [((2, width), f32)] * 4,
            [place, slots, spots, *sent],
            [
                pltpu.VMEM((slot_count * BAND, width), f32),
                pltpu.VMEM((seq_count * tp_count * 8, width), f32),
            ],
            cost=7,
        )
    else:
        mine = lax.dynamic_slice_in_dim(position, tp_place * quarter, quarter)[:, 0]
        used = lax.dynamic_slice_in_dim(row_image, tp_place * quarter, quarter) >= 0
        local = jax.ops.segment_sum(
            jnp.where(used, grad_stream[:quarter], 0.0), mine, num_segments=pos_table.shape[0]
        )
        pos_grad, small = lax.psum((local, small), ("seq", "tp"))
        smalls = [jnp.stack([small[i], small[j]]) for i, j in ((5, 7), (0, 2), (1, 3), (4, 6))]
    qkv_grad, qv_bias_grad, out_grad, up_bias_grad = call(
        split_kernel,
        [((3, 3 * DH, width), f32), ((2, 3 * DH), f32), ((3 * DH, width), f32), ((8, width), f32)],
        [place, *last_blocks],
        [pltpu.VMEM((last_rows, width), bf16)],
    )
    return (
        result[:quarter],
        cut_special(result[quarter:]),
        grad_stream[:quarter],
        cut_special(grad_stream[quarter:]),
        pos_grad,
        jnp.transpose(qkv_grad, (0, 2, 1)),
        qv_bias_grad,
        out_grad,
        *smalls,
        feed_sums[ff:].astype(f32),
        up_bias_grad[0],
        feed_sums[:ff].astype(f32),
    )


def solution(mesh):
    in_specs = (
        P(("seq", "tp"), None),
        P("tp", None),
        P(),
        P(),
        P(),
        P(None, None, "tp"),
        P(None, "tp"),
        P("tp", None),
        P(),
        P(),
        P(),
        P(),
        P(None, "tp"),
        P("tp"),
        P("tp", None),
        P("seq", None),
        P(),
    )
    out_specs = (
        P(("seq", "tp"), None),
        P("tp", None),
        P(("seq", "tp"), None),
        P("tp", None),
        P(),
        P(None, None, "tp"),
        P(None, "tp"),
        P("tp", None),
        P(),
        P(),
        P(),
        P(),
        P(None, "tp"),
        P("tp"),
        P("tp", None),
    )
    return jax.shard_map(
        on_device, mesh=mesh, in_specs=in_specs, out_specs=out_specs, check_vma=False
    )
```

```python
import functools
import math

import jax
import jax.numpy as jnp
from jax import lax
from jax.experimental import pallas as pl
from jax.experimental.pallas import tpu as pltpu
from jax.sharding import PartitionSpec as P

DH = 64
SPECIALS = 5
PATCH_BIG = 1369
BAND = 64

GROUP = 16
LANES = 256
FAR = 1e30
EPS = 1e-06
BIG_BANDS = (PATCH_BIG + BAND - 1) // BAND
WINDOW = (BIG_BANDS + 1) * BAND
CHUNK = 1280
KEPT = 8
VMEM_LIMIT = 60 * 1024 * 1024

bf16 = jnp.bfloat16
f32 = jnp.float32


def dot(a, b):
    return jnp.dot(a, b, preferred_element_type=f32)


def dot_nt(a, b):
    return lax.dot_general(a, b, (((1,), (1,)), ((), ())), preferred_element_type=f32)


def dot_tn(a, b):
    return lax.dot_general(a, b, (((0,), (0,)), ((), ())), preferred_element_type=f32)


def lanes_of(shape):
    return lax.broadcasted_iota(jnp.int32, shape, len(shape) - 1)


def norm_parts(values):
    centre = jnp.mean(values, axis=-1, keepdims=True)
    centred = values - centre
    spread = jnp.mean(centred * centred, axis=-1, keepdims=True)
    scale = lax.rsqrt(spread + EPS)
    return centred * scale, scale


def norm_back(unit, scale, eg):
    first = jnp.mean(eg, axis=-1, keepdims=True)
    second = jnp.mean(eg * unit, axis=-1, keepdims=True)
    return scale * (eg - first - unit * second)


def key_head(lane, h):
    return (lane >= h * DH) & (lane < (h + 1) * DH)


def value_head(lane, h):
    start = (0, DH, 3 * DH)[h]
    return (lane >= start) & (lane < start + DH)


def key_side(lane, h, images):
    image_lane = (lane >= 3 * DH) & (lane <= 3 * DH + images)
    lse_start = 3 * DH + images + 1 + 3 * h
    return key_head(lane, h) | image_lane | ((lane >= lse_start) & (lane < lse_start + 3))


DELTA_LANE = 50


def value_side(lane, h):
    start = 2 * DH + DELTA_LANE + 3 * h
    return value_head(lane, h) | ((lane >= start) & (lane < start + 3))


def three_pieces(x):
    high = x.astype(bf16).astype(f32)
    rest = x - high
    middle = rest.astype(bf16).astype(f32)
    return high, middle, (rest - middle).astype(bf16).astype(f32)


def stacked(rows, picks):
    zero = jnp.zeros_like(rows)
    return jnp.concatenate([jnp.where(pick, rows, zero) for pick in picks], axis=0)


def spread_sum(stack, picks):
    count = stack.shape[0] // len(picks)
    total = None
    for h, pick in enumerate(picks):
        part = jnp.where(pick, stack[h * count : (h + 1) * count], 0.0)
        total = part if total is None else total + part
    return total


def held_bytes(shape, dtype):
    lanes = -(-shape[-1] // 128) * 128
    rows = -(-math.prod(shape[:-1]) // 16) * 16
    return rows * lanes * jnp.dtype(dtype).itemsize


def call(body, outs, ins, scratch=(), outside=(), cost=2, spare=6):
    spaces = []
    for i, item in enumerate(ins):
        smem = item.dtype == jnp.int32 and item.ndim == 1
        space = pl.ANY if i in outside else pltpu.SMEM if smem else pltpu.VMEM
        spaces.append(pl.BlockSpec(memory_space=space))
    need = sum(held_bytes(x.shape, x.dtype) for i, x in enumerate(ins) if i not in outside)
    need += sum(held_bytes(s, d) for s, d in outs)
    need += sum(held_bytes(x.shape, x.dtype) for x in scratch)
    out_spaces = [
        pl.BlockSpec(memory_space=pltpu.SMEM if d == jnp.int32 and len(s) == 1 else pltpu.VMEM)
        for s, d in outs
    ]
    return pl.pallas_call(
        body,
        out_shape=[jax.ShapeDtypeStruct(s, d) for s, d in outs],
        in_specs=spaces,
        out_specs=out_spaces,
        scratch_shapes=list(scratch),
        cost_estimate=pl.CostEstimate(
            flops=int(cost * 1e9), bytes_accessed=0, transcendentals=0
        ),
        compiler_params=pltpu.CompilerParams(
            vmem_limit_bytes=min(need + spare * 1024 * 1024, VMEM_LIMIT)
            if need < 2**24 + 2**23
            else VMEM_LIMIT
        ),
    )(*ins)


def for_each(count, body):
    def step(i, carry):
        body(i)
        return carry

    lax.fori_loop(0, count, step, 0)


def image_starts(images, length, held):
    def begin(i, start):
        held[i] = start
        return start + (length[i] + BAND - 1) // BAND

    return lax.fori_loop(0, images, begin, jnp.int32(0))


def band_facts(images, length, slot_band, held, used, slot):
    band = slot_band[slot]

    def look(i, state):
        image, first = state
        inside = band >= held[i]
        return jnp.where(inside, i, image), jnp.where(inside, held[i], first)

    state = (jnp.int32(0), jnp.int32(0))
    if images <= 8:
        for i in range(images):
            state = look(i, state)
    else:
        state = lax.fori_loop(0, images, look, state)
    image, first = state
    left = jnp.minimum(jnp.maximum(length[image] - (band - first) * BAND, 0), BAND)
    return band, image, first, jnp.where(band < used, left, 0)


def plan_kernel(sizes, length, slot_band, place, windows, spots, own, row_image, position, held):
    seq_count, bands, images, rows = sizes
    used = image_starts(images, length, held)

    def image_facts(i, carry):
        spots[i] = held[i] * BAND
        spots[images + i] = (length[i] == PATCH_BIG).astype(jnp.int32)
        windows[bands + i] = (held[i] + i) * BAND
        return carry

    lax.fori_loop(0, images, image_facts, 0)
    windows[bands + images] = (used + images) * BAND
    in_band = lax.broadcasted_iota(jnp.int32, (BAND, 1), 0)
    for u in range(bands):
        band, image, first, valid = band_facts(
            images, length, slot_band, held, used, place[1] * bands + u
        )
        windows[u] = jnp.where(valid > 0, (first + image) * BAND, 0)
        own[u] = jnp.where(valid > 0, (band - first) * BAND, 0)
        own[bands + u] = (length[image] == PATCH_BIG).astype(jnp.int32)
        good = in_band < valid
        row_image[u * BAND : (u + 1) * BAND] = jnp.where(good, image, -1)
        offset = jnp.where(length[image] == PATCH_BIG, 0, PATCH_BIG) + (band - first) * BAND
        position[u * BAND : (u + 1) * BAND] = jnp.where(good, offset + in_band, 0)
    group = lax.broadcasted_iota(jnp.int32, (images * GROUP, 1), 0)
    row_image[rows:] = jnp.where(group % GROUP < SPECIALS, group // GROUP, -1)


def slots_kernel(sizes, length, slot_band, place, slots, held):
    seq_count, bands, images = sizes
    slot_count = seq_count * bands
    used = image_starts(images, length, held)

    def put(i, carry):
        source = i // bands
        if seq_count == 8:
            source = jnp.bitwise_xor(source, place[1])
        band, image, _, valid = band_facts(
            images, length, slot_band, held, used, source * bands + i % bands
        )
        slots[i] = jnp.where(valid > 0, (band + image + 1) * BAND, 0)
        slots[slot_count + i] = image
        slots[2 * slot_count + i] = valid
        slots[3 * slot_count + i] = band * BAND
        return carry

    lax.fori_loop(0, slot_count, put, 0)


def gather_rows_kernel(patches, specials, out):
    quarter = patches.shape[0]
    out[:quarter] = patches[...]
    padding = jnp.zeros((GROUP - SPECIALS, patches.shape[1]), f32)
    for g in range(specials.shape[0] // SPECIALS):
        group = specials[g * SPECIALS : (g + 1) * SPECIALS].astype(f32)
        out[quarter + g * GROUP : quarter + (g + 1) * GROUP] = jnp.concatenate(
            [group, padding], axis=0
        ).astype(bf16)


def row_weight(count, patch_rows, seq):
    row = lax.broadcasted_iota(jnp.int32, (count, 1), 0)
    special = ((row - patch_rows) % GROUP < SPECIALS) & (seq == 0)
    return jnp.where((row < patch_rows) | special, 1.0, 0.0)


def embed_kernel(sizes, place, at_table, *refs):
    tp_count, quarter, special, images = sizes
    xs = refs[:tp_count]
    table, w_cat, b_cat, gain, shift, row_image = refs[tp_count : tp_count + 6]
    stream, own, normed, query, pack, key_own, value_own, pos, low = refs[tp_count + 6 :]
    low[...] = table[PATCH_BIG:].astype(f32)
    bands = quarter * tp_count // BAND
    for u in range(bands):
        at = pl.multiple_of(at_table[u], BAND)
        good = row_image[u * BAND : (u + 1) * BAND] >= 0

        @pl.when(at_table[bands + u] > 0)
        def _(u=u, at=at, good=good):
            pos[u * BAND : (u + 1) * BAND] = jnp.where(
                good, table[pl.ds(at, BAND)].astype(f32), 0.0
            )

        @pl.when(at_table[bands + u] == 0)
        def _(u=u, at=at, good=good):
            pos[u * BAND : (u + 1) * BAND] = jnp.where(good, low[pl.ds(at, BAND)], 0.0)

    rows = quarter * tp_count
    me = place[0]
    for k in range(tp_count):
        spot = lax.rem(me - k + tp_count, tp_count)
        patch_at = pl.multiple_of(spot * quarter, 16)
        special_at = pl.multiple_of(rows + spot * special, 16)
        part = xs[k][:quarter].astype(f32) + pos[pl.ds(patch_at, quarter)]
        stream[pl.ds(patch_at, quarter)] = part
        tail = xs[k][quarter:].astype(f32)
        stream[pl.ds(special_at, special)] = tail
        if k == 0:
            own[:quarter] = part
            own[quarter:] = tail
    unit, _ = norm_parts(stream[...])
    rounded = (unit * gain[...] + shift[...]).astype(bf16)
    normed[...] = rounded
    projected = (dot_nt(rounded, w_cat[...]) + b_cat[...]).astype(bf16)
    image = row_image[...]
    total = image.shape[0]
    lane = lanes_of((total, LANES))
    image_lane = (lane >= 3 * DH) & (lane <= 3 * DH + images)
    scaled = projected[:, :LANES].astype(f32) * (DH**-0.5)
    far = jnp.where(image_lane & (lane != 3 * DH + image), FAR, 0.0)
    query[...] = jnp.where(lane < 3 * DH, scaled, far).astype(bf16)
    pack[...] = projected[:rows, LANES:]
    own_lane = 3 * DH + jnp.where(image < 0, images, image)
    lse_lane = (lane > 3 * DH + images) & (lane <= 3 * DH + images + 9)
    aux = jnp.where((lane == own_lane) | lse_lane, -1.0, 0.0)
    key_own[...] = jnp.where(
        lane < 3 * DH, projected[:, LANES : 2 * LANES].astype(f32), aux
    ).astype(bf16)
    half = lanes_of((total, 128))
    value_own[:, :128] = projected[:, 512:640]
    value_own[:, 128:] = jnp.where(
        half < DH,
        jnp.where((half >= DELTA_LANE) & (half < DELTA_LANE + 9), -1.0, 0.0),
        projected[:, 384:512].astype(f32),
    ).astype(bf16)


def chunk_count(windows, bands, images):
    return (windows[bands + images] + CHUNK - 1) // CHUNK


def chunk_at(start, c):
    return pl.ds(pl.multiple_of(start + c * CHUNK, BAND), CHUNK)


def first_rows(rows):
    rows = rows.astype(f32)
    count = rows.shape[0] // GROUP
    return jnp.concatenate([rows[i * GROUP : i * GROUP + KEPT] for i in range(count)], axis=0).astype(
        bf16
    )


def put_first_rows(target, start, rows):
    padding = jnp.zeros((GROUP - KEPT, rows.shape[1]), f32)
    count = rows.shape[0] // KEPT
    rows = rows.astype(f32)
    target[pl.ds(start, count * GROUP)] = jnp.concatenate(
        [part for i in range(count) for part in (rows[i * KEPT : (i + 1) * KEPT], padding)], axis=0
    ).astype(target.dtype)


def clear_unused(clear, windows, bands, images, buffer_rows):
    lax.fori_loop(0, images, lambda i, c: clear(windows[bands + i], c), 0)
    lax.fori_loop(
        windows[bands + images] // BAND,
        jnp.maximum(
            windows[bands + images - 1] // BAND + -(-WINDOW // BAND),
            chunk_count(windows, bands, images) * (CHUNK // BAND),
        ),
        lambda i, c: clear(i * BAND, c),
        0,
    )


def half_kernel(place, rows, out):
    half = out.shape[0]
    out[...] = rows[pl.ds(pl.multiple_of(lax.rem(place[1], 2) * half, 16), half)]


def in_order_kernel(axis, bit, place, mine, other, out):
    count = mine.shape[0]
    side = lax.rem(place[axis] // bit, 2)
    out[pl.ds(pl.multiple_of(side * count, 16), count)] = mine[...]
    out[pl.ds(pl.multiple_of((1 - side) * count, 16), count)] = other[...]


def assemble_kernel(place, mine, other, out):
    count = out.shape[0]
    half = mine.shape[0] // count
    cut = 2 * DH - half
    for k in range(count):
        spot = lax.rem(place[0] - k + count, count) * half
        at = pl.multiple_of(spot, 16)
        late = pl.multiple_of(spot + cut, 16)
        out[k, 2 * DH : 3 * DH] = jnp.zeros((DH, out.shape[2]), bf16)
        out[k, 4 * DH :] = jnp.zeros((DH, out.shape[2]), bf16)

        def fill(low, high, k=k, at=at, late=late):
            out[k, :half] = low[pl.ds(at, half)]
            out[k, half : 2 * DH] = high[pl.ds(at, cut)]
            out[k, 3 * DH : 4 * DH] = high[pl.ds(late, half - cut)]

        @pl.when(place[1] % 2 == 0)
        def _(fill=fill):
            fill(mine, other)

        @pl.when(place[1] % 2 == 1)
        def _(fill=fill):
            fill(other, mine)


def attend_kernel(sizes, slots, windows, *refs):
    blocks_count, bands, images, rows = sizes
    blocks = refs[:blocks_count]
    key_own, value_own, query = refs[blocks_count : blocks_count + 3]
    keys, values, attended, attended_b, packed, query_out = refs[blocks_count + 3 :]
    lane = lanes_of((1, LANES))
    lse_lane = (lane > 3 * DH + images) & (lane <= 3 * DH + images + 9)
    empty = jnp.where((lane == 3 * DH + images) | lse_lane, -1.0, 0.0)
    buffer_rows = keys.shape[0]

    def clear(at, carry):
        at = pl.multiple_of(at, BAND)
        keys[pl.ds(at, BAND)] = jnp.broadcast_to(empty, (BAND, LANES)).astype(bf16)
        values[pl.ds(at, BAND)] = jnp.zeros((BAND, LANES), bf16)
        return carry

    clear_unused(clear, windows, bands, images, buffer_rows)
    band_lane = lanes_of((BAND, LANES))
    half = lanes_of((BAND, 128))
    in_band = lax.broadcasted_iota(jnp.int32, (BAND, LANES), 0)
    band_lse = (band_lane > 3 * DH + images) & (band_lane <= 3 * DH + images + 9)
    delta_aux = jnp.where((half >= DELTA_LANE) & (half < DELTA_LANE + 9), -1.0, 0.0)
    per_block = blocks[0].shape[0] // BAND
    slot_count = blocks_count * per_block
    for b in range(blocks_count):

        def place(j, b=b):
            slot = b * per_block + j
            valid = slots[2 * slot_count + slot]

            @pl.when(valid > 0)
            def _():
                at = pl.multiple_of(slots[slot], BAND)
                image = slots[slot_count + slot]
                source = blocks[b][pl.ds(pl.multiple_of(j * BAND, BAND), BAND)]
                own_lane = 3 * DH + jnp.where(in_band < valid, image, images)
                aux = jnp.where((band_lane == own_lane) | band_lse, -1.0, 0.0)
                keys[pl.ds(at, BAND)] = jnp.where(
                    band_lane < 3 * DH, source[:, :LANES].astype(f32), aux
                ).astype(bf16)
                values[pl.ds(at, BAND), :128] = source[:, 256:384]
                values[pl.ds(at, BAND), 128:] = jnp.where(
                    half < DH, delta_aux, source[:, 128:256].astype(f32)
                ).astype(bf16)

        for_each(per_block, place)

    def place_special(i):
        at = pl.multiple_of(windows[bands + i], BAND)
        source = pl.ds(pl.multiple_of(rows + i * GROUP, GROUP), GROUP)
        keys[pl.ds(at, GROUP)] = key_own[source]
        values[pl.ds(at, GROUP)] = value_own[source]

    for_each(images, place_special)
    key_picks = [key_side(lane, h, images) for h in range(3)]
    value_picks = [value_head(lane, h) for h in range(3)]

    chunks = chunk_count(windows, bands, images)

    def finish(count, own, top, total, summed):
        usable = total > 0.0
        safe = jnp.where(usable, total, 1.0)
        result = spread_sum(summed / safe, value_picks)
        lse = jnp.where(usable, top + jnp.log(safe), 0.0)
        row = own.astype(f32)
        for h in range(3):
            for piece, part in enumerate(three_pieces(lse[h * count : (h + 1) * count])):
                row = jnp.where(lane == 3 * DH + images + 1 + 3 * h + piece, part, row)
        return result, row

    for u in range(bands):
        window = pl.ds(pl.multiple_of(windows[u], BAND), WINDOW)
        spot = pl.ds(u * BAND, BAND)
        own = query[spot]
        scores = dot_nt(stacked(own, key_picks), keys[window])
        top = jnp.maximum(jnp.max(scores, axis=-1, keepdims=True), -0.1 * FAR)
        weights = jnp.exp(scores - top)
        total = jnp.sum(weights, axis=-1, keepdims=True)
        result, row = finish(BAND, own, top, total, dot(weights.astype(bf16), values[window]))
        attended[spot] = result
        attended_b[spot] = result.astype(bf16)
        query_out[spot] = row.astype(bf16)

    own = first_rows(query[rows:])
    stack = stacked(own, key_picks)
    count = stack.shape[0]

    def add(c, state):
        top, total, summed = state
        scores = dot_nt(stack, keys[chunk_at(0, c)])
        new_top = jnp.maximum(top, jnp.max(scores, axis=-1, keepdims=True))
        rescale = jnp.exp(top - new_top)
        weights = jnp.exp(scores - new_top)
        return (
            new_top,
            total * rescale + jnp.sum(weights, axis=-1, keepdims=True),
            summed * rescale + dot(weights.astype(bf16), values[chunk_at(0, c)]),
        )

    start = (
        jnp.full((count, 1), -0.1 * FAR, f32),
        jnp.zeros((count, 1), f32),
        jnp.zeros((count, LANES), f32),
    )
    result, row = finish(count // 3, own, *lax.fori_loop(0, chunks, add, start))
    put_first_rows(attended, rows, result)
    put_first_rows(attended_b, rows, result)
    put_first_rows(query_out, rows, row)
    total = query.shape[0]
    packed[:total] = attended_b[:, :128]
    upper = pltpu.roll(attended[: total // 2, 128:], DH, 1)
    lower = attended[total // 2 :, 128:]
    packed[total:] = jnp.where(lanes_of((1, 128)) < DH, upper, lower).astype(bf16)


def cotangent_kernel(
    sizes, place, patch, special_rows, scale, w_down, two_weighted, weighted, hidden, own, whole
):
    quarter, special = sizes
    rows = patch.shape[0]
    whole[:rows] = patch[...].astype(f32)
    padding = jnp.zeros((GROUP - SPECIALS, patch.shape[1]), f32)
    for g in range(special_rows.shape[0] // SPECIALS):
        group = special_rows[g * SPECIALS : (g + 1) * SPECIALS].astype(f32)
        whole[rows + g * GROUP : rows + (g + 1) * GROUP] = jnp.concatenate([group, padding], axis=0)
    value = whole[...]
    weight = row_weight(whole.shape[0], rows, place[1])
    grad_two = (value * scale[1:2]).astype(bf16)
    weighted[...] = (value * weight).astype(bf16)
    two_weighted[...] = (grad_two.astype(f32) * weight).astype(bf16)
    hidden[...] = dot_nt(grad_two, w_down[...])
    own[:quarter] = whole[pl.ds(pl.multiple_of(place[0] * quarter, 16), quarter)]
    own[quarter:] = whole[pl.ds(pl.multiple_of(rows + place[0] * special, 16), special)]


def result_kernel(sizes, mid, scale, bias, *refs):
    quarter, groups = sizes
    *parts, patch, special = refs
    two = parts[0][...]
    for part in parts[1:]:
        two += part[: two.shape[0]].astype(f32)
    result = (mid[...] + scale[1:2] * (two + bias[1:2])).astype(bf16)
    patch[...] = result[:quarter]
    cut_groups(special, result[quarter:].astype(f32), groups)


def cut_groups(target, rows, groups):
    for g in range(groups):
        target[g * SPECIALS : (g + 1) * SPECIALS] = rows[g * GROUP : g * GROUP + SPECIALS].astype(
            target.dtype
        )


def feed_kernel(sizes, place, *refs):
    tp_count, quarter, special = sizes
    attended = refs[:tp_count]
    w_outs, stream, scale, bias, gain, shift, w_up, up_bias, grad_hidden = refs[
        tp_count : tp_count + 9
    ]
    mid_own, one_own, normed, hidden_out, grad_pre_out, bias_out = refs[
        tp_count + 9 : tp_count + 15
    ]
    parts = refs[tp_count + 15 : 2 * tp_count + 15]
    mid, partial = refs[2 * tp_count + 15 :]
    rows = quarter * tp_count
    me = place[0]
    total = stream.shape[0]
    one = 0.0
    upper, lower = 0.0, 0.0
    for k in range(tp_count):
        one += dot(attended[k][:total], w_outs[k, : 2 * DH])
        upper += dot(attended[k][total:], w_outs[k, 3 * DH :])
        lower += dot(attended[k][total:], w_outs[k, 2 * DH : 4 * DH])
    one = one + jnp.concatenate([upper, lower], axis=0)
    partial[...] = one
    value = stream[...] + scale[0:1] * (one + bias[0:1])
    mid[...] = value
    own_patch = pl.ds(pl.multiple_of(me * quarter, 16), quarter)
    own_special = pl.ds(pl.multiple_of(rows + me * special, 16), special)
    mid_own[:quarter] = mid[own_patch]
    mid_own[quarter:] = mid[own_special]
    one_own[:quarter] = partial[own_patch]
    one_own[quarter:] = partial[own_special]
    unit, _ = norm_parts(value)
    rounded = (unit * gain[...] + shift[...]).astype(bf16)
    normed[...] = rounded
    pre = dot(rounded, w_up[...]) + up_bias[...]
    share = 0.5 * (1.0 + lax.erf(pre * (0.5**0.5)))
    hidden_out[...] = (pre * share).astype(bf16)
    slope = share + pre * jnp.exp(-0.5 * pre * pre) * (0.5 / jnp.pi) ** 0.5
    grad_pre = (grad_hidden[...] * slope).astype(bf16)
    weight = row_weight(value.shape[0], rows, place[1])
    weighted = grad_pre.astype(f32) * weight
    grad_pre_out[...] = weighted.astype(bf16)
    bias_out[...] = jnp.broadcast_to(jnp.sum(weighted, axis=0, keepdims=True), bias_out.shape).astype(bf16)
    partial[...] = dot_nt(grad_pre, w_up[...])
    send_blocks(me, parts, partial, quarter, special)


def feed_grad_kernel(sizes, place, *refs):
    tp_count, quarter, special, split = sizes
    hidden, normed, grad_two, grad_pre, w_down, grad_result, keep, send, sums = refs[:9]
    two_blocks = refs[9 : 9 + tp_count]
    partial = refs[-1]
    ff = hidden.shape[1]
    down = dot_tn(hidden[...], grad_two[...])
    up = dot_tn(normed[...], grad_pre[...])
    if split:

        @pl.when(place[1] % 2 == 0)
        def _():
            keep[...] = down
            send[...] = up.astype(bf16)

        @pl.when(place[1] % 2 == 1)
        def _():
            keep[...] = up
            send[...] = down.astype(bf16)

    else:
        keep[...] = down
        send[:ff] = down.astype(bf16)
        send[ff:] = up.astype(bf16)
    two = dot(hidden[...], w_down[...])
    sums[...] = jnp.broadcast_to(
        jnp.sum(two * grad_result[...].astype(f32), axis=0, keepdims=True), sums.shape
    )
    partial[...] = two
    send_blocks(place[0], two_blocks, partial, quarter, special)


def proj_grad_kernel(parts, place, normed, joined, bias, out_grad, up_bias, keep, send, whole):
    columns = joined.shape[1]
    whole[:columns] = dot_tn(joined[...], normed[...])
    whole[columns : columns + 16, :columns] = bias[...].astype(f32)
    whole[columns : columns + 16, columns:] = jnp.zeros((16, normed.shape[1] - columns), f32)
    start = columns + 16 + out_grad.shape[0]
    whole[columns + 16 : start] = out_grad[...].astype(f32)
    whole[start : start + 16] = up_bias[...].astype(f32)
    whole[start + 16 :] = jnp.zeros((whole.shape[0] - start - 16, normed.shape[1]), f32)
    half = keep.shape[0]
    core = lax.rem(place[1], parts) if parts == 2 else 0
    keep[...] = whole[pl.ds(pl.multiple_of(core * half, 16), half)]
    send[...] = whole[pl.ds(pl.multiple_of((1 - core) * half if parts == 2 else 0, 16), half)].astype(bf16)


def chip_parts_kernel(place, keep, received, mine, *sends_and_whole):
    *sends, whole = sends_and_whole
    whole[...] = keep[...] + received[...].astype(f32)
    part = mine.shape[0]
    chip = place[1] // 2
    mine[...] = whole[pl.ds(pl.multiple_of(chip * part, 16), part)]
    for i, send in enumerate(sends):
        at = pl.multiple_of(jnp.bitwise_xor(chip, i + 1) * part, 16)
        send[...] = whole[pl.ds(at, part)].astype(bf16)


def add_parts_kernel(mine, first, second, third, out):
    total = mine[...] + first[...].astype(f32) + second[...].astype(f32) + third[...].astype(f32)
    out[...] = total.astype(bf16)


def split_kernel(first, place, *refs):
    *blocks, out, bias, out_w, up_bias, sums = refs
    part = sums.shape[0] // len(blocks)
    start = first
    if len(blocks) == 1:
        sums[...] = blocks[0][...]
    else:
        for k, block in enumerate(blocks):
            source = jnp.bitwise_xor(place[1], k)
            at = (lax.rem(source, 2) * (len(blocks) // 2) + source // 2) * part
            sums[pl.ds(pl.multiple_of(at, 16), part)] = block[start : start + part]
    out[0] = sums[: 3 * DH].astype(f32)
    out[1] = sums[4 * DH : 7 * DH].astype(f32)
    out[2, : 2 * DH] = sums[8 * DH : 10 * DH].astype(f32)
    out[2, 2 * DH :] = sums[7 * DH : 8 * DH].astype(f32)
    tail = sums[10 * DH : 10 * DH + 8].astype(f32)
    third = pltpu.roll(tail[:, 384:512], DH, 1)
    bias[0:1] = tail[0:1, : 3 * DH]
    bias[1:2, :128] = tail[0:1, 512:640]
    bias[1:2, 128:] = third[0:1, :DH]
    start = 10 * DH + 16
    out_w[...] = sums[start : start + out_w.shape[0]].astype(f32)
    start += out_w.shape[0]
    up_bias[...] = sums[start : start + 8].astype(f32)


def half_parts_kernel(place, keep, received, p_keep, q_keep, p_send, q_send, whole):
    whole[...] = keep[...] + received[...].astype(f32)
    part = p_keep.shape[0]
    x, y = lax.rem(place[1] // 2, 2), place[1] // 4
    for start, side, mine, send in ((0, x, p_keep, p_send), (2 * part, y, q_keep, q_send)):
        mine[...] = whole[pl.ds(pl.multiple_of(start + side * part, 16), part)]
        send[...] = whole[pl.ds(pl.multiple_of(start + (1 - side) * part, 16), part)].astype(bf16)


def quarter_parts_kernel(place, p, q, p_in, q_in, p_keep, q_keep, p_send, q_send, p_all, q_all):
    part = p_keep.shape[0]
    x, y = lax.rem(place[1] // 2, 2), place[1] // 4
    p_all[...] = p[...] + p_in[...].astype(f32)
    q_all[...] = q[...] + q_in[...].astype(f32)
    for whole, side, mine, send in ((p_all, y, p_keep, p_send), (q_all, x, q_keep, q_send)):
        mine[...] = whole[pl.ds(pl.multiple_of(side * part, 16), part)]
        send[...] = whole[pl.ds(pl.multiple_of((1 - side) * part, 16), part)].astype(bf16)


def add_two_kernel(p, q, p_in, q_in, p_out, q_out):
    p_out[...] = (p[...] + p_in[...].astype(f32)).astype(bf16)
    q_out[...] = (q[...] + q_in[...].astype(f32)).astype(bf16)


def feed_out_kernel(place, *refs):
    *blocks, down, up = refs
    part = down.shape[0] // 8
    for k, block in enumerate(blocks):
        source = jnp.bitwise_xor(place[1], k)
        x, y = lax.rem(source // 2, 2), source // 4
        start = block.shape[0] - 2 * part
        spots = (2 * x + y) * part, (4 + 2 * y + x) * part

        def put(out, block=block, start=start, spots=spots):
            for i, spot in enumerate(spots):
                rows = block[start + i * part : start + (i + 1) * part]
                out[pl.ds(pl.multiple_of(spot, 16), part)] = rows.astype(f32)

        @pl.when(lax.rem(source, 2) == 0)
        def _(put=put):
            put(down)

        @pl.when(lax.rem(source, 2) == 1)
        def _(put=put):
            put(up)


def send_blocks(me, parts, partial, quarter, special):
    tp_count = len(parts)
    rows = quarter * tp_count
    for k in range(tp_count):
        spot = lax.rem(me + k, tp_count)
        patch_at = pl.ds(pl.multiple_of(spot * quarter, 16), quarter)
        special_at = pl.ds(pl.multiple_of(rows + spot * special, 16), special)
        parts[k][:quarter] = partial[patch_at].astype(parts[k].dtype)
        parts[k][quarter:] = partial[special_at].astype(parts[k].dtype)


def mid_back_kernel(sizes, place, *refs):
    tp_count, quarter = sizes
    parts = refs[:tp_count]
    mid, one, grad_result, two_sums, scale, bias, gain = refs[tp_count : tp_count + 7]
    grad_mid_out, grad_one_out, small = refs[tp_count + 7 :]
    weight = row_weight(mid.shape[0], quarter, place[1])
    incoming = parts[0][...]
    for k in range(1, tp_count):
        incoming += parts[k][...].astype(f32)
    unit, scaling = norm_parts(mid[...])
    grad_mid = grad_result[...] + norm_back(unit, scaling, incoming * gain[...])
    weighted = incoming * weight
    weighted_mid = grad_mid * weight
    result_sum = jnp.sum(grad_result[...] * weight, axis=0, keepdims=True)
    small[0:2] = jnp.zeros((2, small.shape[1]), f32)
    small[2:3] = jnp.sum(weighted * unit, axis=0, keepdims=True)
    small[3:4] = jnp.sum(weighted, axis=0, keepdims=True)
    small[4:5] = jnp.sum(weighted_mid * (one[...] + bias[0:1]), axis=0, keepdims=True)
    small[5:6] = jnp.sum(weighted_mid, axis=0, keepdims=True) * scale[0:1]
    small[6:7] = two_sums[0:1] + result_sum * bias[1:2]
    small[7:8] = result_sum * scale[1:2]
    grad_mid_out[...] = grad_mid
    grad_one = (grad_mid * scale[0:1]).astype(bf16)
    grad_one_out[...] = grad_one


def delta_kernel(sizes, place, *refs):
    tp_count, quarter, special = sizes
    parts = refs[:tp_count]
    attended, attended_b, w_outs, query, out, out_patch, out_grad, whole = refs[tp_count:]
    rows = quarter * tp_count
    me = place[0]
    for k in range(tp_count):
        spot = lax.rem(me - k + tp_count, tp_count)
        whole[pl.ds(pl.multiple_of(spot * quarter, 16), quarter)] = parts[k][:quarter]
        whole[pl.ds(pl.multiple_of(rows + spot * special, 16), special)] = parts[k][quarter:]
    value = dot_nt(whole[...], w_outs[0, :LANES]).astype(bf16).astype(f32)
    total = value.shape[0]
    product = value * attended[...]
    lane = lanes_of(value.shape)
    for h in range(3):
        delta = jnp.sum(jnp.where(value_head(lane, h), product, 0.0), axis=-1, keepdims=True)
        for piece, part in enumerate(three_pieces(delta)):
            value = jnp.where(lane == 2 * DH + DELTA_LANE + 3 * h + piece, part, value)
    out[...] = value.astype(bf16)
    out_patch[:, :LANES] = value[:rows].astype(bf16)
    out_patch[:, LANES:] = query[:rows]
    weighted = (whole[...].astype(f32) * row_weight(total, rows, place[1])).astype(bf16)
    product = dot_tn(attended_b[...], weighted).astype(bf16)
    out_grad[: 2 * DH] = product[: 2 * DH]
    out_grad[2 * DH :] = product[3 * DH :]


def query_grad_kernel(sizes, windows, query, grad, keys, values, out):
    bands, images, rows = sizes
    lane = lanes_of((1, LANES))
    key_picks = [key_side(lane, h, images) for h in range(3)]
    value_picks = [value_side(lane, h) for h in range(3)]
    head_picks = [key_head(lane, h) for h in range(3)]

    def part(own, pulled, chunk):
        key_part = keys[chunk]
        probs = jnp.exp(dot_nt(own, key_part))
        return dot((probs * dot_nt(pulled, values[chunk])).astype(bf16), key_part)

    for u in range(bands):
        window = pl.ds(pl.multiple_of(windows[u], BAND), WINDOW)
        spot = pl.ds(u * BAND, BAND)
        summed = part(stacked(query[spot], key_picks), stacked(grad[spot], value_picks), window)
        out[spot] = (spread_sum(summed, head_picks) * DH**-0.5).astype(bf16)

    own = stacked(first_rows(query[rows:]), key_picks)
    pulled = stacked(first_rows(grad[rows:]), value_picks)
    summed = lax.fori_loop(
        0,
        chunk_count(windows, bands, images),
        lambda c, summed: summed + part(own, pulled, chunk_at(0, c)),
        jnp.zeros((own.shape[0], LANES), f32),
    )
    put_first_rows(out, rows, spread_sum(summed, head_picks) * DH**-0.5)


def pair_grad_kernel(sizes, place, slots, windows, *refs):
    blocks_count, bands, images, tp_count, quarter, special = sizes
    blocks = refs[:blocks_count]
    rest = refs[blocks_count:]
    query_own, grad_own, key_own, value_own, grad_query, w_cat, joined_out, bias_out = rest[:8]
    parts = rest[8 : 8 + tp_count]
    queries, grads, joined, partial = rest[8 + tp_count :]
    rows = quarter * tp_count
    lane = lanes_of((1, LANES))
    image_lane = (lane >= 3 * DH) & (lane <= 3 * DH + images)
    empty = jnp.where(image_lane, FAR, 0.0)

    def clear(at, carry):
        at = pl.multiple_of(at, BAND)
        queries[pl.ds(at, BAND)] = jnp.broadcast_to(empty, (BAND, LANES)).astype(bf16)
        grads[pl.ds(at, BAND)] = jnp.zeros((BAND, LANES), bf16)
        return carry

    clear_unused(clear, windows, bands, images, queries.shape[0])
    per_block = blocks[0].shape[0] // BAND
    slot_count = blocks_count * per_block
    for b in range(blocks_count):

        def put(j, b=b):
            slot = b * per_block + j

            @pl.when(slots[2 * slot_count + slot] > 0)
            def _():
                at = pl.multiple_of(slots[slot], BAND)
                source = pl.ds(pl.multiple_of(j * BAND, BAND), BAND)
                if blocks_count == 1:
                    target = pl.ds(at, BAND)
                    pltpu.sync_copy(blocks[b].at[source, pl.ds(0, LANES)], grads.at[target])
                    pltpu.sync_copy(blocks[b].at[source, pl.ds(LANES, LANES)], queries.at[target])
                else:
                    grads[pl.ds(at, BAND)] = blocks[b][source, :LANES]
                    queries[pl.ds(at, BAND)] = blocks[b][source, LANES:]

        for_each(per_block, put)

    def put_special(i):
        at = pl.multiple_of(windows[bands + i], BAND)
        source = pl.ds(pl.multiple_of(rows + i * GROUP, GROUP), GROUP)
        queries[pl.ds(at, GROUP)] = query_own[source]
        grads[pl.ds(at, GROUP)] = grad_own[source]

    for_each(images, put_special)
    key_picks = [key_side(lane, h, images) for h in range(3)]
    value_picks = [value_side(lane, h) for h in range(3)]
    key_heads = [key_head(lane, h) for h in range(3)]
    value_heads = [value_head(lane, h) for h in range(3)]

    def part(own, held, chunk, state):
        grad_key, grad_value = state
        query_part, grad_part = queries[chunk], grads[chunk]
        probs = jnp.exp(dot_nt(own, query_part))
        scores = (probs * dot_nt(held, grad_part)).astype(bf16)
        return (
            grad_key + dot(scores, query_part),
            grad_value + dot(probs.astype(bf16), grad_part),
        )

    def finish(state):
        grad_key = spread_sum(state[0], key_heads)
        grad_value = spread_sum(state[1], value_heads)
        half = lanes_of((1, 128))
        last = jnp.where(half < DH, grad_key[:, 128:], grad_value[:, 128:])
        return jnp.concatenate([grad_key[:, :128], last, grad_value[:, :128]], axis=1)

    joined[:, :256] = grad_query[...]

    def band(u):
        window = pl.ds(pl.multiple_of(windows[u], BAND), WINDOW)
        spot = pl.ds(pl.multiple_of(u * BAND, BAND), BAND)
        own, held = stacked(key_own[spot], key_picks), stacked(value_own[spot], value_picks)
        joined[spot, 256:] = finish(part(own, held, window, (0.0, 0.0))).astype(bf16)

    for u in range(bands):
        band(u)
    own = stacked(first_rows(key_own[rows:]), key_picks)
    held = stacked(first_rows(value_own[rows:]), value_picks)
    blank = jnp.zeros((own.shape[0], LANES), f32)
    state = lax.fori_loop(
        0,
        chunk_count(windows, bands, images),
        lambda c, state: part(own, held, chunk_at(0, c), state),
        (blank, blank),
    )
    put_first_rows(joined.at[:, 256:], rows, finish(state))
    partial[...] = dot(joined[...], w_cat[...])
    send_blocks(place[0], parts, partial, quarter, special)
    weighted = joined[...].astype(f32) * row_weight(joined.shape[0], rows, place[1])
    joined_out[...] = weighted.astype(bf16)
    bias_out[...] = jnp.broadcast_to(jnp.sum(weighted, axis=0, keepdims=True), bias_out.shape).astype(bf16)


def stream_back_kernel(sizes, place, *refs):
    tp_count, quarter = sizes
    parts = refs[:tp_count]
    stream, grad_mid, gain, early = refs[tp_count : tp_count + 4]
    out, out_special, send, small = refs[tp_count + 4 :]
    weight = row_weight(stream.shape[0], quarter, place[1])
    incoming = parts[0][...]
    for k in range(1, tp_count):
        incoming += parts[k][...].astype(f32)
    unit, scaling = norm_parts(stream[...])
    result = grad_mid[...] + norm_back(unit, scaling, incoming * gain[...])
    out[...] = result[:quarter]
    cut_groups(out_special, result[quarter:], out_special.shape[0] // SPECIALS)
    weighted = incoming * weight
    first = jnp.sum(weighted * unit, axis=0, keepdims=True)
    second = jnp.sum(weighted, axis=0, keepdims=True)
    sums = jnp.concatenate([first, second, early[2:8]], axis=0)
    small[...] = sums
    send[:quarter] = result[:quarter].astype(bf16)
    send[quarter:] = sums.astype(bf16)


def join_kernel(*refs):
    *parts, out = refs
    start = 0
    for part in parts:
        out[start : start + part.shape[0]] = part[...]
        start += part.shape[0]


def pack_kernel(cut, x_first, y_first, second, to_y, to_x):
    to_y[:cut] = x_first[:cut]
    to_y[cut:] = second[...]
    rest = y_first.shape[0] - cut
    to_x[:rest] = y_first[cut:]
    to_x[rest:] = second[...]


def unpack_kernel(cut, cut_second, from_x, from_y, diagonal, x_second, y_second, to_y, to_x):
    rest = diagonal.shape[0] - cut
    diagonal[:cut] = from_y[:cut]
    diagonal[cut:] = from_x[:rest]
    x_second[...] = from_x[rest:]
    y_second[...] = from_y[cut:]
    to_y[...] = from_x[rest : rest + cut_second]
    to_x[...] = from_y[cut + cut_second :]


def position_kernel(sizes, place, slots, spots, *refs):
    seq_count, tp_count, images, rows = sizes
    blocks = refs[: 2 * seq_count]
    out, *smalls, ordered, tiny = refs[2 * seq_count :]
    bands = rows // BAND
    slot_count = seq_count * bands
    quarter = rows // tp_count
    piece = 32
    in_piece = lax.broadcasted_iota(jnp.int32, (piece, 1), 0)
    for c in range(tp_count):
        tp = lax.rem(place[0] - c + tp_count, tp_count)
        for k in range(seq_count):
            block = blocks[k] if c == 0 else blocks[seq_count + k]
            block = block.at[pl.ds(max(c - 1, 0) * (quarter + 8), quarter + 8)]
            seq = jnp.bitwise_xor(place[1], k)
            tiny[pl.ds(pl.multiple_of((seq * tp_count + tp) * 8, 8), 8)] = block[
                quarter : quarter + 8
            ].astype(f32)
            for r in range(quarter // piece):
                spot = tp * (quarter // piece) + r
                slot = k * bands + spot // 2
                shift = (spot % 2) * piece
                at = pl.multiple_of(slots[3 * slot_count + slot] + shift, piece)
                valid = slots[2 * slot_count + slot] - shift
                ordered[pl.ds(at, piece)] = jnp.where(
                    in_piece < valid, block[r * piece : (r + 1) * piece].astype(f32), 0.0
                )
    total = tiny[0:8]
    for i in range(1, seq_count * tp_count):
        total += tiny[i * 8 : (i + 1) * 8]
    for out_small, first, second in zip(smalls, (5, 0, 1, 4), (7, 2, 3, 6)):
        out_small[0:1] = total[first : first + 1]
        out_small[1:2] = total[second : second + 1]
    low_rows = out.shape[0] - PATCH_BIG
    seen_big, seen_low = jnp.int32(0), jnp.int32(0)
    for i in range(images):
        at = pl.multiple_of(spots[i], BAND)
        is_big = spots[images + i]
        seen = jnp.where(is_big > 0, seen_big, seen_low)

        @pl.when((is_big > 0) & (seen == 0))
        def _():
            out[:PATCH_BIG] = ordered[pl.ds(at, BIG_BANDS * BAND)][:PATCH_BIG]

        @pl.when((is_big > 0) & (seen > 0))
        def _():
            out[:PATCH_BIG] += ordered[pl.ds(at, BIG_BANDS * BAND)][:PATCH_BIG]

        @pl.when((is_big == 0) & (seen == 0))
        def _():
            out[PATCH_BIG:] = ordered[pl.ds(at, low_rows)]

        @pl.when((is_big == 0) & (seen > 0))
        def _():
            out[PATCH_BIG:] += ordered[pl.ds(at, low_rows)]

        seen_big += is_big
        seen_low += 1 - is_big


def rotated(x, k):
    count = lax.axis_size("tp")
    return lax.ppermute(x, "tp", [(i, (i + k) % count) for i in range(count)])


def from_group(x):
    return [x] + [rotated(x, k) for k in range(1, lax.axis_size("tp"))]


def to_group(blocks):
    return [blocks[0]] + [rotated(blocks[k], k) for k in range(1, len(blocks))]


def exchanged(x, k):
    count = lax.axis_size("tp")
    return lax.ppermute(x, "tp", [(i, i ^ k) for i in range(count)])


def partner(x, k):
    count = lax.axis_size("seq")
    return lax.ppermute(x, "seq", [(i, i ^ k) for i in range(count)])


def from_chips(x):
    if lax.axis_size("seq") != 8:
        return [lax.all_gather(x, "seq", axis=0, tiled=True)]
    return [x] + [partner(x, k) for k in (2, 4, 6)]


def from_ring(x, *late):
    rows = x.shape[0]
    cut = -(-rows // 32) * 16
    along_x, along_y = partner(x, 2), partner(x, 4)
    halves = [partner(after(along_x, *late)[:cut], 4), partner(after(along_y, *late)[cut:], 2)]
    (diagonal,) = call(join_kernel, [(x.shape, x.dtype)], halves, cost=1)
    return [x, along_x, along_y, diagonal]


def two_rings(first, second, ready, passed):
    cut, cut_second = -(-first.shape[0] // 32) * 16, -(-second.shape[0] // 32) * 16
    rest, rest_second = first.shape[0] - cut, second.shape[0] - cut_second
    width = first.shape[1]
    x_first, y_first = partner(first, 2), partner(first, 4)
    to_y, to_x = call(
        functools.partial(pack_kernel, cut),
        [((cut + second.shape[0], width), bf16), ((rest + second.shape[0], width), bf16)],
        [after(x_first, *ready), y_first, second],
        cost=1,
    )
    from_x, from_y = partner(to_x, 2), partner(to_y, 4)
    diagonal, x_second, y_second, to_y, to_x = call(
        functools.partial(unpack_kernel, cut, cut_second),
        [
            (first.shape, bf16),
            (second.shape, bf16),
            (second.shape, bf16),
            ((cut_second, width), bf16),
            ((rest_second, width), bf16),
        ],
        [after(from_x, *passed), from_y],
        cost=1,
    )
    (diagonal_second,) = call(
        join_kernel, [(second.shape, bf16)], [partner(to_y, 4), partner(to_x, 2)], cost=1
    )
    return (
        with_other_core([first, x_first, y_first, diagonal]),
        with_other_core([second, x_second, y_second, diagonal_second]),
    )


def with_other_core(blocks):
    if len(blocks) == 1:
        return blocks
    odd = [partner(block, 1) for block in blocks]
    return [block for pair in zip(blocks, odd) for block in pair]


def from_bands(x):
    return with_other_core(from_chips(x))


def after(value, *others):
    return lax.optimization_barrier((value,) + tuple(others))[0]


def pad_heads(rows):
    gap = jnp.zeros_like(rows[:DH])
    return jnp.concatenate([rows[: 2 * DH], gap, rows[2 * DH :], gap], axis=0)


def joined_columns(query, key, value, axis):
    cut = functools.partial(lax.slice_in_dim, axis=axis)
    return jnp.concatenate(
        [
            query,
            jnp.zeros_like(cut(query, 0, DH)),
            key,
            cut(value, 2 * DH, 3 * DH),
            cut(value, 0, 2 * DH),
        ],
        axis=axis,
    )


def on_device(
    patches,
    specials,
    pos_table,
    image_length,
    slot_band,
    w_qkv,
    qv_bias,
    w_out,
    branch_bias,
    ln_gain,
    ln_bias,
    layer_scale,
    w_up,
    up_bias,
    w_down,
    cot_patch,
    cot_special,
):
    seq_count = lax.axis_size("seq")
    tp_count = lax.axis_size("tp")
    seq_place = lax.axis_index("seq")
    tp_place = lax.axis_index("tp")
    near = seq_count == 8
    quarter, width = patches.shape
    ff = w_up.shape[1]
    images = image_length.shape[0]
    rows = quarter * tp_count
    bands = rows // BAND
    slot_count = slot_band.shape[0]
    special = (specials.shape[0] // SPECIALS) * GROUP
    special_rows = special * tp_count
    total = rows + special_rows
    block = quarter + special
    place = jnp.stack([tp_place, seq_place]).astype(jnp.int32)

    (x_own,) = call(
        gather_rows_kernel,
        [((block, width), bf16)],
        [patches, specials],
        cost=1,
        spare=58,
    )
    x_parts = from_group(x_own)
    windows, spots, at_table, row_image, position = call(
        functools.partial(plan_kernel, (seq_count, bands, images, rows)),
        [
            ((bands + images + 1,), jnp.int32),
            ((2 * images,), jnp.int32),
            ((2 * bands,), jnp.int32),
            ((total, 1), jnp.int32),
            ((rows, 1), jnp.int32),
        ],
        [image_length, slot_band, place],
        [pltpu.SMEM((images,), jnp.int32)],
    )
    half = w_out.shape[0] // 2
    if near:
        (mine,) = call(
            half_kernel, [((half, width), bf16)], [place, after(w_out, x_own)], cost=1
        )
    w_cat = joined_columns(*jnp.transpose(w_qkv, (0, 2, 1)), 0)
    b_cat = joined_columns(qv_bias[:1], jnp.zeros_like(qv_bias[:1]), qv_bias[1:], 1)
    stream, stream_own, normed, query, pack, key_own, value_own = call(
        functools.partial(embed_kernel, (tp_count, quarter, special, images)),
        [
            ((total, width), f32),
            ((block, width), f32),
            ((total, width), bf16),
            ((total, LANES), bf16),
            ((rows, 384), bf16),
            ((total, LANES), bf16),
            ((total, LANES), bf16),
        ],
        [place, at_table, *x_parts, pos_table, w_cat, b_cat, ln_gain[:1], ln_bias[:1], row_image],
        [
            pltpu.VMEM((rows, width), f32),
            pltpu.VMEM((pos_table.shape[0] - PATCH_BIG, width), f32),
        ],
        cost=4,
    )

    (slots,) = call(
        functools.partial(slots_kernel, (seq_count, bands, images)),
        [((4 * slot_count,), jnp.int32)],
        [image_length, slot_band, after(place, pack)],
        [pltpu.SMEM((images,), jnp.int32)],
        cost=4,
    )
    chips = from_chips(pack)
    if near:
        chips[3] = after(chips[3], slots)
        mine = after(mine, pack)
        (two_halves,) = call(
            functools.partial(in_order_kernel, 0, 1),
            [((2 * half, width), bf16)],
            [place, mine, exchanged(mine, 1)],
            cost=1,
        )
        (four_halves,) = call(
            functools.partial(in_order_kernel, 0, 2),
            [((4 * half, width), bf16)],
            [place, two_halves, exchanged(two_halves, 2)],
            cost=1,
        )
        query = after(query, four_halves)
    pairs = with_other_core(chips)
    if near:
        (w_outs,) = call(
            assemble_kernel,
            [((tp_count, LANES + DH, width), bf16)],
            [place, four_halves, partner(four_halves, 1)],
            cost=1,
        )
    else:
        w_outs = jnp.stack([pad_heads(part) for part in from_group(w_out)])
    grad_two_w, cot_weighted, grad_hidden, grad_result = call(
        functools.partial(cotangent_kernel, (quarter, special)),
        [
            ((total, width), bf16),
            ((total, width), bf16),
            ((total, ff), f32),
            ((block, width), f32),
        ],
        [place, cot_patch, cot_special, layer_scale, after(w_down, pack)],
        [pltpu.VMEM((total, width), f32)],
        cost=3,
    )

    buffer_rows = (slot_count + images) * BAND + WINDOW
    keys, values, attended, attended_b, packed, query = call(
        functools.partial(attend_kernel, (len(pairs), bands, images, rows)),
        [
            ((buffer_rows, LANES), bf16),
            ((buffer_rows, LANES), bf16),
            ((total, LANES), f32),
            ((total, LANES), bf16),
            ((total + total // 2, 128), bf16),
            ((total, LANES), bf16),
        ],
        [slots, windows, *pairs, key_own, value_own, query],
        cost=8,
        spare=8,
    )
    attended_all = from_group(packed)

    feed = call(
        functools.partial(feed_kernel, (tp_count, quarter, special)),
        [
            ((block, width), f32),
            ((block, width), f32),
            ((total, width), bf16),
            ((total, ff), bf16),
            ((total, ff), bf16),
            ((16, ff), bf16),
            ((block, width), f32),
        ]
        + [((block, width), bf16)] * (tp_count - 1),
        [
            place,
            *attended_all,
            w_outs,
            stream,
            layer_scale,
            branch_bias,
            ln_gain[1:],
            ln_bias[1:],
            w_up,
            up_bias[None],
            grad_hidden,
        ],
        [pltpu.VMEM((total, width), f32), pltpu.VMEM((total, width), f32)],
        cost=6,
        spare=8,
    )
    mid_own, one_own, normed_two, hidden, grad_pre, up_bias_grad = feed[:6]
    two_parts = to_group(feed[6:])
    keep, send, two_sums, *two_blocks = call(
        functools.partial(feed_grad_kernel, (tp_count, quarter, special, near)),
        [
            ((ff, width), f32),
            ((ff if near else ff + width, width), bf16),
            ((8, width), f32),
            ((block, width), f32),
        ]
        + [((block, width), bf16)] * (tp_count - 1),
        [
            place,
            hidden,
            normed_two,
            grad_two_w,
            grad_pre,
            w_down,
            cot_weighted,
        ],
        [pltpu.VMEM((total, width), f32)],
        cost=4,
        spare=8,
    )
    if near:
        p, q, p_send, q_send = call(
            half_parts_kernel,
            [((ff // 4, width), f32)] * 2 + [((ff // 4, width), bf16)] * 2,
            [place, keep, partner(send, 1)],
            [pltpu.VMEM((ff, width), f32)],
            cost=1,
        )
        first_done = []
    else:
        feed_all = lax.psum(send, "seq")
        first_done = []

    grad_mid, grad_one, early = call(
        functools.partial(mid_back_kernel, (tp_count, quarter)),
        [((block, width), f32), ((block, width), bf16), ((8, width), f32)],
        [
            place,
            *two_parts,
            after(mid_own, *first_done),
            one_own,
            grad_result,
            two_sums,
            layer_scale,
            branch_bias,
            ln_gain[1:],
        ],
        cost=2,
    )
    grad_one_all = from_group(grad_one)
    if near:
        p_in, q_in = partner(after(p_send, grad_one), 2), partner(after(q_send, grad_one), 4)
        p2, q2, p2_send, q2_send = call(
            quarter_parts_kernel,
            [((ff // 8, width), f32)] * 2 + [((ff // 8, width), bf16)] * 2,
            [place, p, q, p_in, q_in],
            [pltpu.VMEM((ff // 4, width), f32)] * 2,
            cost=1,
        )
    if near:
        attended = after(attended, p2)
    grad_attn, grad_patch, out_grad = call(
        functools.partial(delta_kernel, (tp_count, quarter, special)),
        [((total, LANES), bf16), ((rows, 2 * LANES), bf16), ((w_out.shape[0], width), bf16)],
        [place, *grad_one_all, attended, attended_b, w_outs, query],
        [pltpu.VMEM((total, width), bf16)],
        cost=2,
    )
    (grad_query,) = call(
        functools.partial(query_grad_kernel, (bands, images, rows)),
        [((total, LANES), bf16)],
        [windows, query, grad_attn, keys, values],
        cost=6,
        spare=8,
    )
    if near:
        grads = with_other_core(from_ring(grad_patch, grad_query))
    else:
        grads = from_chips(after(grad_patch, grad_query))
    pair = call(
        functools.partial(
            pair_grad_kernel, (len(grads), bands, images, tp_count, quarter, special)
        ),
        [((total, 640), bf16), ((16, 640), bf16), ((block, width), f32)]
        + [((block, width), bf16)] * (tp_count - 1),
        [
            place,
            slots,
            windows,
            *grads,
            query,
            grad_attn,
            key_own,
            value_own,
            grad_query,
            w_cat,
        ],
        [
            pltpu.VMEM((buffer_rows, LANES), bf16),
            pltpu.VMEM((buffer_rows, LANES), bf16),
            pltpu.VMEM((total, 640), bf16),
            pltpu.VMEM((total, width), f32),
        ],
        outside=(3,) if len(grads) == 1 else (),
        cost=8,
        spare=8,
    )
    joined, joined_bias = pair[:2]
    normed_parts = to_group(pair[2:])

    last_rows = -(-(640 + 32 + w_out.shape[0]) // 128) * 128
    held = last_rows // 2 if near else last_rows
    keep_last, send_last = call(
        functools.partial(proj_grad_kernel, 2 if near else 1),
        [((held, width), f32), ((held, width), bf16)],
        [place, normed, joined, joined_bias, out_grad, up_bias_grad],
        [pltpu.VMEM((last_rows, width), f32)],
        cost=2,
    )
    second_done = [keep_last]
    if near:
        p2_late, q2_late = after(p2_send, grad_query), after(q2_send, grad_query)
        p2_in, q2_in = partner(p2_late, 4), partner(q2_late, 2)
        p3, q3 = call(
            add_two_kernel, [((ff // 8, width), bf16)] * 2, [p2, q2, p2_in, q2_in], cost=1
        )
    patch_out, special_out, send, small = call(
        functools.partial(stream_back_kernel, (tp_count, quarter)),
        [
            ((quarter, width), f32),
            ((specials.shape[0], width), f32),
            ((quarter + 8, width), bf16),
            ((8, width), f32),
        ],
        [
            place,
            *normed_parts,
            after(stream_own, *second_done),
            grad_mid,
            ln_gain[:1],
            early,
        ],
        cost=1,
    )
    arrived = from_group(send)[1:]
    two_in = [rotated(after(two_blocks[k], *arrived), k) for k in range(1, tp_count)]
    if near:
        part = last_rows // 8
        mine, *sends = call(
            chip_parts_kernel,
            [((part, width), f32)] + [((part, width), bf16)] * 3,
            [place, keep_last, partner(send_last, 1)],
            [pltpu.VMEM((last_rows // 2, width), f32)],
            cost=1,
        )
        received = [partner(block, k) for block, k in zip(sends, (2, 4, 6))]
        (reduced,) = call(add_parts_kernel, [((part, width), bf16)], [mine, *received], cost=1)
    else:
        last_blocks = [lax.psum(send_last, "seq")]
        part = last_rows
        down_grad, up_grad = feed_all[:ff].astype(f32), feed_all[ff:].astype(f32)
    if near:
        (first_sent,) = call(
            join_kernel,
            [((quarter + 8 + ff // 4, width), bf16)],
            [send, p3, q3],
            cost=1,
        )
        (second_sent,) = call(
            join_kernel,
            [((3 * (quarter + 8) + part, width), bf16)],
            [*arrived, reduced],
            cost=1,
        )
        first_blocks, last_blocks = two_rings(first_sent, second_sent, arrived, two_in)
        sent = first_blocks + last_blocks
        down_grad, up_grad = call(
            feed_out_kernel,
            [((ff, width), f32)] * 2,
            [place, *first_blocks],
            cost=2,
        )
        qkv_grad, qv_bias_grad, out_grad, up_bias_grad = call(
            functools.partial(split_kernel, 3 * (quarter + 8) if near else 0),
            [((3, 3 * DH, width), f32), ((2, 3 * DH), f32), ((3 * DH, width), f32), ((8, width), f32)],
            [place, *last_blocks],
            [pltpu.VMEM((last_rows, width), bf16)],
            cost=2,
        )
        pos_grad, *smalls = call(
            functools.partial(position_kernel, (seq_count, tp_count, images, rows)),
            [((pos_table.shape[0], width), f32)] + [((2, width), f32)] * 4,
            [place, slots, after(spots, down_grad, qkv_grad), *sent],
            [
                pltpu.VMEM((slot_count * BAND, width), f32),
                pltpu.VMEM((seq_count * tp_count * 8, width), f32),
            ],
            cost=5,
            spare=4,
        )
    else:
        qkv_grad, qv_bias_grad, out_grad, up_bias_grad = call(
            functools.partial(split_kernel, 3 * (quarter + 8) if near else 0),
            [((3, 3 * DH, width), f32), ((2, 3 * DH), f32), ((3 * DH, width), f32), ((8, width), f32)],
            [place, *last_blocks],
            [pltpu.VMEM((last_rows, width), bf16)],
            cost=2,
        )
        mine = lax.dynamic_slice_in_dim(position, tp_place * quarter, quarter)[:, 0]
        used = lax.dynamic_slice_in_dim(row_image, tp_place * quarter, quarter) >= 0
        local = jax.ops.segment_sum(
            jnp.where(used, patch_out, 0.0), mine, num_segments=pos_table.shape[0]
        )
        pos_grad, small = lax.psum((local, small), ("seq", "tp"))
        smalls = [jnp.stack([small[i], small[j]]) for i, j in ((5, 7), (0, 2), (1, 3), (4, 6))]
    result, result_special = call(
        functools.partial(result_kernel, (quarter, specials.shape[0] // SPECIALS)),
        [((quarter, width), bf16), (specials.shape, bf16)],
        [mid_own, layer_scale, branch_bias, two_blocks[0], *two_in],
        cost=1,
    )
    return (
        result,
        result_special,
        patch_out,
        special_out,
        pos_grad,
        jnp.transpose(qkv_grad, (0, 2, 1)),
        qv_bias_grad,
        out_grad,
        *smalls,
        up_grad,
        up_bias_grad[0],
        down_grad,
    )


def solution(mesh):
    in_specs = (
        P(("seq", "tp"), None),
        P("tp", None),
        P(),
        P(),
        P(),
        P(None, None, "tp"),
        P(None, "tp"),
        P("tp", None),
        P(),
        P(),
        P(),
        P(),
        P(None, "tp"),
        P("tp"),
        P("tp", None),
        P("seq", None),
        P(),
    )
    out_specs = (
        P(("seq", "tp"), None),
        P("tp", None),
        P(("seq", "tp"), None),
        P("tp", None),
        P(),
        P(None, None, "tp"),
        P(None, "tp"),
        P("tp", None),
        P(),
        P(),
        P(),
        P(),
        P(None, "tp"),
        P("tp"),
        P("tp", None),
    )
    return jax.shard_map(
        on_device, mesh=mesh, in_specs=in_specs, out_specs=out_specs, check_vma=False
    )
```

```python
import functools
import math

import jax
import jax.numpy as jnp
from jax import lax
from jax.experimental import pallas as pl
from jax.experimental.pallas import tpu as pltpu
from jax.sharding import PartitionSpec as P

DH = 64
SPECIALS = 5
PATCH_BIG = 1369
BAND = 64

GROUP = 16
LANES = 256
FAR = 1e30
EPS = 1e-06
BIG_BANDS = (PATCH_BIG + BAND - 1) // BAND
WINDOW = (BIG_BANDS + 1) * BAND
CHUNK = 1280
KEPT = 8
VMEM_LIMIT = 60 * 1024 * 1024

bf16 = jnp.bfloat16
f32 = jnp.float32


def dot(a, b):
    return jnp.dot(a, b, preferred_element_type=f32)


def dot_nt(a, b):
    return lax.dot_general(a, b, (((1,), (1,)), ((), ())), preferred_element_type=f32)


def dot_tn(a, b):
    return lax.dot_general(a, b, (((0,), (0,)), ((), ())), preferred_element_type=f32)


def lanes_of(shape):
    return lax.broadcasted_iota(jnp.int32, shape, len(shape) - 1)


def norm_parts(values):
    centre = jnp.mean(values, axis=-1, keepdims=True)
    centred = values - centre
    spread = jnp.mean(centred * centred, axis=-1, keepdims=True)
    scale = lax.rsqrt(spread + EPS)
    return centred * scale, scale


def norm_back(unit, scale, eg):
    first = jnp.mean(eg, axis=-1, keepdims=True)
    second = jnp.mean(eg * unit, axis=-1, keepdims=True)
    return scale * (eg - first - unit * second)


def key_head(lane, h):
    return (lane >= h * DH) & (lane < (h + 1) * DH)


def value_head(lane, h):
    start = (0, DH, 3 * DH)[h]
    return (lane >= start) & (lane < start + DH)


def key_side(lane, h, images):
    image_lane = (lane >= 3 * DH) & (lane <= 3 * DH + images)
    lse_start = 3 * DH + images + 1 + 3 * h
    return key_head(lane, h) | image_lane | ((lane >= lse_start) & (lane < lse_start + 3))


DELTA_LANE = 50


def value_side(lane, h):
    start = 2 * DH + DELTA_LANE + 3 * h
    return value_head(lane, h) | ((lane >= start) & (lane < start + 3))


def three_pieces(x):
    high = x.astype(bf16).astype(f32)
    rest = x - high
    middle = rest.astype(bf16).astype(f32)
    return high, middle, (rest - middle).astype(bf16).astype(f32)


def stacked(rows, picks):
    zero = jnp.zeros_like(rows)
    return jnp.concatenate([jnp.where(pick, rows, zero) for pick in picks], axis=0)


def spread_sum(stack, picks):
    count = stack.shape[0] // len(picks)
    total = None
    for h, pick in enumerate(picks):
        part = jnp.where(pick, stack[h * count : (h + 1) * count], 0.0)
        total = part if total is None else total + part
    return total


def held_bytes(shape, dtype):
    lanes = -(-shape[-1] // 128) * 128
    rows = -(-math.prod(shape[:-1]) // 16) * 16
    return rows * lanes * jnp.dtype(dtype).itemsize


def call(body, outs, ins, scratch=(), outside=(), cost=2, spare=6):
    spaces = []
    for i, item in enumerate(ins):
        smem = item.dtype == jnp.int32 and item.ndim == 1
        space = pl.ANY if i in outside else pltpu.SMEM if smem else pltpu.VMEM
        spaces.append(pl.BlockSpec(memory_space=space))
    need = sum(held_bytes(x.shape, x.dtype) for i, x in enumerate(ins) if i not in outside)
    need += sum(held_bytes(s, d) for s, d in outs)
    need += sum(held_bytes(x.shape, x.dtype) for x in scratch)
    out_spaces = [
        pl.BlockSpec(memory_space=pltpu.SMEM if d == jnp.int32 and len(s) == 1 else pltpu.VMEM)
        for s, d in outs
    ]
    return pl.pallas_call(
        body,
        out_shape=[jax.ShapeDtypeStruct(s, d) for s, d in outs],
        in_specs=spaces,
        out_specs=out_spaces,
        scratch_shapes=list(scratch),
        cost_estimate=pl.CostEstimate(
            flops=int(cost * 10**9), bytes_accessed=0, transcendentals=0
        ),
        compiler_params=pltpu.CompilerParams(
            vmem_limit_bytes=min(need + spare * 1024 * 1024, VMEM_LIMIT)
            if need < 2**24 + 2**23
            else VMEM_LIMIT
        ),
    )(*ins)


def for_each(count, body):
    def step(i, carry):
        body(i)
        return carry

    lax.fori_loop(0, count, step, 0)


def image_starts(images, length, held):
    def begin(i, start):
        held[i] = start
        return start + (length[i] + BAND - 1) // BAND

    return lax.fori_loop(0, images, begin, jnp.int32(0))


def band_facts(images, length, slot_band, held, used, slot):
    band = slot_band[slot]

    def look(i, state):
        image, first = state
        inside = band >= held[i]
        return jnp.where(inside, i, image), jnp.where(inside, held[i], first)

    state = (jnp.int32(0), jnp.int32(0))
    if images <= 8:
        for i in range(images):
            state = look(i, state)
    else:
        state = lax.fori_loop(0, images, look, state)
    image, first = state
    left = jnp.minimum(jnp.maximum(length[image] - (band - first) * BAND, 0), BAND)
    return band, image, first, jnp.where(band < used, left, 0)


def plan_kernel(sizes, length, slot_band, place, windows, spots, own, row_image, position, held):
    seq_count, bands, images, rows = sizes
    used = image_starts(images, length, held)

    def image_facts(i, carry):
        spots[i] = held[i] * BAND
        spots[images + i] = (length[i] == PATCH_BIG).astype(jnp.int32)
        windows[bands + i] = (held[i] + i) * BAND
        return carry

    lax.fori_loop(0, images, image_facts, 0)
    windows[bands + images] = (used + images) * BAND
    in_band = lax.broadcasted_iota(jnp.int32, (BAND, 1), 0)
    for u in range(bands):
        band, image, first, valid = band_facts(
            images, length, slot_band, held, used, place[1] * bands + u
        )
        windows[u] = jnp.where(valid > 0, (first + image) * BAND, 0)
        own[u] = jnp.where(valid > 0, (band - first) * BAND, 0)
        own[bands + u] = (length[image] == PATCH_BIG).astype(jnp.int32)
        good = in_band < valid
        row_image[u * BAND : (u + 1) * BAND] = jnp.where(good, image, -1)
        offset = jnp.where(length[image] == PATCH_BIG, 0, PATCH_BIG) + (band - first) * BAND
        position[u * BAND : (u + 1) * BAND] = jnp.where(good, offset + in_band, 0)
    group = lax.broadcasted_iota(jnp.int32, (images * GROUP, 1), 0)
    row_image[rows:] = jnp.where(group % GROUP < SPECIALS, group // GROUP, -1)


def slots_kernel(sizes, length, slot_band, place, slots, held):
    seq_count, bands, images = sizes
    slot_count = seq_count * bands
    used = image_starts(images, length, held)

    def put(i, carry):
        source = i // bands
        if seq_count == 8:
            source = jnp.bitwise_xor(source, place[1])
        band, image, _, valid = band_facts(
            images, length, slot_band, held, used, source * bands + i % bands
        )
        slots[i] = jnp.where(valid > 0, (band + image + 1) * BAND, 0)
        slots[slot_count + i] = image
        slots[2 * slot_count + i] = valid
        slots[3 * slot_count + i] = band * BAND
        return carry

    lax.fori_loop(0, slot_count, put, 0)


def gather_rows_kernel(patches, specials, out):
    quarter = patches.shape[0]
    out[:quarter] = patches[...]
    padding = jnp.zeros((GROUP - SPECIALS, patches.shape[1]), f32)
    for g in range(specials.shape[0] // SPECIALS):
        group = specials[g * SPECIALS : (g + 1) * SPECIALS].astype(f32)
        out[quarter + g * GROUP : quarter + (g + 1) * GROUP] = jnp.concatenate(
            [group, padding], axis=0
        ).astype(bf16)


def row_weight(count, patch_rows, seq):
    row = lax.broadcasted_iota(jnp.int32, (count, 1), 0)
    special = ((row - patch_rows) % GROUP < SPECIALS) & (seq == 0)
    return jnp.where((row < patch_rows) | special, 1.0, 0.0)


def embed_kernel(sizes, place, at_table, *refs):
    tp_count, quarter, special, images = sizes
    xs = refs[:tp_count]
    table, w_cat, b_cat, gain, shift, row_image = refs[tp_count : tp_count + 6]
    stream, own, normed, query, pack, key_own, value_own, pos, low = refs[tp_count + 6 :]
    low[...] = table[PATCH_BIG:].astype(f32)
    bands = quarter * tp_count // BAND
    for u in range(bands):
        at = pl.multiple_of(at_table[u], BAND)
        good = row_image[u * BAND : (u + 1) * BAND] >= 0

        @pl.when(at_table[bands + u] > 0)
        def _(u=u, at=at, good=good):
            pos[u * BAND : (u + 1) * BAND] = jnp.where(
                good, table[pl.ds(at, BAND)].astype(f32), 0.0
            )

        @pl.when(at_table[bands + u] == 0)
        def _(u=u, at=at, good=good):
            pos[u * BAND : (u + 1) * BAND] = jnp.where(good, low[pl.ds(at, BAND)], 0.0)

    rows = quarter * tp_count
    me = place[0]
    for k in range(tp_count):
        spot = lax.rem(me - k + tp_count, tp_count)
        patch_at = pl.multiple_of(spot * quarter, 16)
        special_at = pl.multiple_of(rows + spot * special, 16)
        part = xs[k][:quarter].astype(f32) + pos[pl.ds(patch_at, quarter)]
        stream[pl.ds(patch_at, quarter)] = part
        tail = xs[k][quarter:].astype(f32)
        stream[pl.ds(special_at, special)] = tail
        if k == 0:
            own[:quarter] = part
            own[quarter:] = tail
    unit, _ = norm_parts(stream[...])
    rounded = (unit * gain[...] + shift[...]).astype(bf16)
    normed[...] = rounded
    projected = (dot_nt(rounded, w_cat[...]) + b_cat[...]).astype(bf16)
    image = row_image[...]
    total = image.shape[0]
    lane = lanes_of((total, LANES))
    image_lane = (lane >= 3 * DH) & (lane <= 3 * DH + images)
    scaled = projected[:, :LANES].astype(f32) * (DH**-0.5)
    far = jnp.where(image_lane & (lane != 3 * DH + image), FAR, 0.0)
    query[...] = jnp.where(lane < 3 * DH, scaled, far).astype(bf16)
    pack[...] = projected[:rows, LANES:]
    own_lane = 3 * DH + jnp.where(image < 0, images, image)
    lse_lane = (lane > 3 * DH + images) & (lane <= 3 * DH + images + 9)
    aux = jnp.where((lane == own_lane) | lse_lane, -1.0, 0.0)
    key_own[...] = jnp.where(
        lane < 3 * DH, projected[:, LANES : 2 * LANES].astype(f32), aux
    ).astype(bf16)
    half = lanes_of((total, 128))
    value_own[:, :128] = projected[:, 512:640]
    value_own[:, 128:] = jnp.where(
        half < DH,
        jnp.where((half >= DELTA_LANE) & (half < DELTA_LANE + 9), -1.0, 0.0),
        projected[:, 384:512].astype(f32),
    ).astype(bf16)


def chunk_count(windows, bands, images):
    return (windows[bands + images] + CHUNK - 1) // CHUNK


def chunk_at(start, c):
    return pl.ds(pl.multiple_of(start + c * CHUNK, BAND), CHUNK)


def first_rows(rows):
    rows = rows.astype(f32)
    count = rows.shape[0] // GROUP
    return jnp.concatenate([rows[i * GROUP : i * GROUP + KEPT] for i in range(count)], axis=0).astype(
        bf16
    )


def put_first_rows(target, start, rows):
    padding = jnp.zeros((GROUP - KEPT, rows.shape[1]), f32)
    count = rows.shape[0] // KEPT
    rows = rows.astype(f32)
    target[pl.ds(start, count * GROUP)] = jnp.concatenate(
        [part for i in range(count) for part in (rows[i * KEPT : (i + 1) * KEPT], padding)], axis=0
    ).astype(target.dtype)


def clear_unused(clear, windows, bands, images, buffer_rows):
    lax.fori_loop(0, images, lambda i, c: clear(windows[bands + i], c), 0)
    lax.fori_loop(
        windows[bands + images] // BAND,
        jnp.maximum(
            windows[bands + images - 1] // BAND + -(-WINDOW // BAND),
            chunk_count(windows, bands, images) * (CHUNK // BAND),
        ),
        lambda i, c: clear(i * BAND, c),
        0,
    )


def half_kernel(place, rows, out):
    half = out.shape[0]
    out[...] = rows[pl.ds(pl.multiple_of(lax.rem(place[1], 2) * half, 16), half)]


def in_order_kernel(axis, bit, place, mine, other, out):
    count = mine.shape[0]
    side = lax.rem(place[axis] // bit, 2)
    out[pl.ds(pl.multiple_of(side * count, 16), count)] = mine[...]
    out[pl.ds(pl.multiple_of((1 - side) * count, 16), count)] = other[...]


def assemble_kernel(place, mine, other, out):
    count = out.shape[0]
    half = mine.shape[0] // count
    cut = 2 * DH - half
    for k in range(count):
        spot = lax.rem(place[0] - k + count, count) * half
        at = pl.multiple_of(spot, 16)
        late = pl.multiple_of(spot + cut, 16)
        out[k, 2 * DH : 3 * DH] = jnp.zeros((DH, out.shape[2]), bf16)
        out[k, 4 * DH :] = jnp.zeros((DH, out.shape[2]), bf16)

        def fill(low, high, k=k, at=at, late=late):
            out[k, :half] = low[pl.ds(at, half)]
            out[k, half : 2 * DH] = high[pl.ds(at, cut)]
            out[k, 3 * DH : 4 * DH] = high[pl.ds(late, half - cut)]

        @pl.when(place[1] % 2 == 0)
        def _(fill=fill):
            fill(mine, other)

        @pl.when(place[1] % 2 == 1)
        def _(fill=fill):
            fill(other, mine)


def attend_kernel(sizes, slots, windows, *refs):
    blocks_count, bands, images, rows = sizes
    blocks = refs[:blocks_count]
    key_own, value_own, query = refs[blocks_count : blocks_count + 3]
    keys, values, attended, attended_b, packed, query_out, query_patch = refs[blocks_count + 3 :]
    lane = lanes_of((1, LANES))
    lse_lane = (lane > 3 * DH + images) & (lane <= 3 * DH + images + 9)
    empty = jnp.where((lane == 3 * DH + images) | lse_lane, -1.0, 0.0)
    buffer_rows = keys.shape[0]

    def clear(at, carry):
        at = pl.multiple_of(at, BAND)
        keys[pl.ds(at, BAND)] = jnp.broadcast_to(empty, (BAND, LANES)).astype(bf16)
        values[pl.ds(at, BAND)] = jnp.zeros((BAND, LANES), bf16)
        return carry

    clear_unused(clear, windows, bands, images, buffer_rows)
    band_lane = lanes_of((BAND, LANES))
    half = lanes_of((BAND, 128))
    in_band = lax.broadcasted_iota(jnp.int32, (BAND, LANES), 0)
    band_lse = (band_lane > 3 * DH + images) & (band_lane <= 3 * DH + images + 9)
    delta_aux = jnp.where((half >= DELTA_LANE) & (half < DELTA_LANE + 9), -1.0, 0.0)
    per_block = blocks[0].shape[0] // BAND
    slot_count = blocks_count * per_block
    for b in range(blocks_count):

        def place(j, b=b):
            slot = b * per_block + j
            valid = slots[2 * slot_count + slot]

            @pl.when(valid > 0)
            def _():
                at = pl.multiple_of(slots[slot], BAND)
                image = slots[slot_count + slot]
                source = blocks[b][pl.ds(pl.multiple_of(j * BAND, BAND), BAND)]
                own_lane = 3 * DH + jnp.where(in_band < valid, image, images)
                aux = jnp.where((band_lane == own_lane) | band_lse, -1.0, 0.0)
                keys[pl.ds(at, BAND)] = jnp.where(
                    band_lane < 3 * DH, source[:, :LANES].astype(f32), aux
                ).astype(bf16)
                values[pl.ds(at, BAND), :128] = source[:, 256:384]
                values[pl.ds(at, BAND), 128:] = jnp.where(
                    half < DH, delta_aux, source[:, 128:256].astype(f32)
                ).astype(bf16)

        for_each(per_block, place)

    def place_special(i):
        at = pl.multiple_of(windows[bands + i], BAND)
        source = pl.ds(pl.multiple_of(rows + i * GROUP, GROUP), GROUP)
        keys[pl.ds(at, GROUP)] = key_own[source]
        values[pl.ds(at, GROUP)] = value_own[source]

    for_each(images, place_special)
    key_picks = [key_side(lane, h, images) for h in range(3)]
    value_picks = [value_head(lane, h) for h in range(3)]

    chunks = chunk_count(windows, bands, images)

    def finish(count, own, top, total, summed):
        usable = total > 0.0
        safe = jnp.where(usable, total, 1.0)
        result = spread_sum(summed / safe, value_picks)
        lse = jnp.where(usable, top + jnp.log(safe), 0.0)
        row = own.astype(f32)
        for h in range(3):
            for piece, part in enumerate(three_pieces(lse[h * count : (h + 1) * count])):
                row = jnp.where(lane == 3 * DH + images + 1 + 3 * h + piece, part, row)
        return result, row

    for u in range(bands):
        window = pl.ds(pl.multiple_of(windows[u], BAND), WINDOW)
        spot = pl.ds(u * BAND, BAND)
        own = query[spot]
        scores = dot_nt(stacked(own, key_picks), keys[window])
        top = jnp.maximum(jnp.max(scores, axis=-1, keepdims=True), -0.1 * FAR)
        weights = jnp.exp(scores - top)
        total = jnp.sum(weights, axis=-1, keepdims=True)
        result, row = finish(BAND, own, top, total, dot(weights.astype(bf16), values[window]))
        attended[spot] = result
        attended_b[spot] = result.astype(bf16)
        query_out[spot] = row.astype(bf16)

    own = first_rows(query[rows:])
    stack = stacked(own, key_picks)
    count = stack.shape[0]

    def add(c, state):
        top, total, summed = state
        scores = dot_nt(stack, keys[chunk_at(0, c)])
        new_top = jnp.maximum(top, jnp.max(scores, axis=-1, keepdims=True))
        rescale = jnp.exp(top - new_top)
        weights = jnp.exp(scores - new_top)
        return (
            new_top,
            total * rescale + jnp.sum(weights, axis=-1, keepdims=True),
            summed * rescale + dot(weights.astype(bf16), values[chunk_at(0, c)]),
        )

    start = (
        jnp.full((count, 1), -0.1 * FAR, f32),
        jnp.zeros((count, 1), f32),
        jnp.zeros((count, LANES), f32),
    )
    result, row = finish(count // 3, own, *lax.fori_loop(0, chunks, add, start))
    put_first_rows(attended, rows, result)
    put_first_rows(attended_b, rows, result)
    put_first_rows(query_out, rows, row)
    query_patch[...] = query_out[:rows]
    total = query.shape[0]
    packed[:total] = attended_b[:, :128]
    upper = pltpu.roll(attended[: total // 2, 128:], DH, 1)
    lower = attended[total // 2 :, 128:]
    packed[total:] = jnp.where(lanes_of((1, 128)) < DH, upper, lower).astype(bf16)


def cotangent_kernel(
    sizes, place, patch, special_rows, scale, w_down, two_weighted, weighted, hidden, own, whole
):
    quarter, special = sizes
    rows = patch.shape[0]
    whole[:rows] = patch[...].astype(f32)
    padding = jnp.zeros((GROUP - SPECIALS, patch.shape[1]), f32)
    for g in range(special_rows.shape[0] // SPECIALS):
        group = special_rows[g * SPECIALS : (g + 1) * SPECIALS].astype(f32)
        whole[rows + g * GROUP : rows + (g + 1) * GROUP] = jnp.concatenate([group, padding], axis=0)
    value = whole[...]
    weight = row_weight(whole.shape[0], rows, place[1])
    grad_two = (value * scale[1:2]).astype(bf16)
    weighted[...] = (value * weight).astype(bf16)
    two_weighted[...] = (grad_two.astype(f32) * weight).astype(bf16)
    hidden[...] = dot_nt(grad_two, w_down[...])
    own[:quarter] = whole[pl.ds(pl.multiple_of(place[0] * quarter, 16), quarter)]
    own[quarter:] = whole[pl.ds(pl.multiple_of(rows + place[0] * special, 16), special)]


def result_kernel(sizes, mid, scale, bias, *refs):
    quarter, groups = sizes
    *parts, patch, special = refs
    two = parts[0][...]
    for part in parts[1:]:
        two += part[: two.shape[0]].astype(f32)
    result = (mid[...] + scale[1:2] * (two + bias[1:2])).astype(bf16)
    patch[...] = result[:quarter]
    cut_groups(special, result[quarter:].astype(f32), groups)


def cut_groups(target, rows, groups):
    for g in range(groups):
        target[g * SPECIALS : (g + 1) * SPECIALS] = rows[g * GROUP : g * GROUP + SPECIALS].astype(
            target.dtype
        )


def feed_kernel(sizes, place, *refs):
    tp_count, quarter, special = sizes
    attended = refs[:tp_count]
    w_outs, stream, scale, bias, gain, shift, w_up, up_bias, grad_hidden = refs[
        tp_count : tp_count + 9
    ]
    mid_own, one_own, normed, hidden_out, grad_pre_out, bias_out = refs[
        tp_count + 9 : tp_count + 15
    ]
    parts = refs[tp_count + 15 : 2 * tp_count + 15]
    mid, partial = refs[2 * tp_count + 15 :]
    rows = quarter * tp_count
    me = place[0]
    total = stream.shape[0]
    one = 0.0
    upper, lower = 0.0, 0.0
    for k in range(tp_count):
        one += dot(attended[k][:total], w_outs[k, : 2 * DH])
        upper += dot(attended[k][total:], w_outs[k, 3 * DH :])
        lower += dot(attended[k][total:], w_outs[k, 2 * DH : 4 * DH])
    one = one + jnp.concatenate([upper, lower], axis=0)
    partial[...] = one
    value = stream[...] + scale[0:1] * (one + bias[0:1])
    mid[...] = value
    own_patch = pl.ds(pl.multiple_of(me * quarter, 16), quarter)
    own_special = pl.ds(pl.multiple_of(rows + me * special, 16), special)
    mid_own[:quarter] = mid[own_patch]
    mid_own[quarter:] = mid[own_special]
    one_own[:quarter] = partial[own_patch]
    one_own[quarter:] = partial[own_special]
    unit, _ = norm_parts(value)
    rounded = (unit * gain[...] + shift[...]).astype(bf16)
    normed[...] = rounded
    pre = dot(rounded, w_up[...]) + up_bias[...]
    share = 0.5 * (1.0 + lax.erf(pre * (0.5**0.5)))
    hidden_out[...] = (pre * share).astype(bf16)
    slope = share + pre * jnp.exp(-0.5 * pre * pre) * (0.5 / jnp.pi) ** 0.5
    grad_pre = (grad_hidden[...] * slope).astype(bf16)
    weight = row_weight(value.shape[0], rows, place[1])
    weighted = grad_pre.astype(f32) * weight
    grad_pre_out[...] = weighted.astype(bf16)
    bias_out[...] = jnp.broadcast_to(jnp.sum(weighted, axis=0, keepdims=True), bias_out.shape).astype(bf16)
    partial[...] = dot_nt(grad_pre, w_up[...])
    send_blocks(me, parts, partial, quarter, special)


def feed_grad_kernel(sizes, place, *refs):
    tp_count, quarter, special, split = sizes
    hidden, normed, grad_two, grad_pre, w_down, grad_result, keep, send, sums = refs[:9]
    two_blocks = refs[9 : 9 + tp_count]
    partial = refs[-1]
    ff = hidden.shape[1]
    down = dot_tn(hidden[...], grad_two[...])
    up = dot_tn(normed[...], grad_pre[...])
    if split:

        @pl.when(place[1] % 2 == 0)
        def _():
            keep[...] = down
            send[...] = up.astype(bf16)

        @pl.when(place[1] % 2 == 1)
        def _():
            keep[...] = up
            send[...] = down.astype(bf16)

    else:
        keep[...] = down
        send[:ff] = down.astype(bf16)
        send[ff:] = up.astype(bf16)
    two = dot(hidden[...], w_down[...])
    sums[...] = jnp.broadcast_to(
        jnp.sum(two * grad_result[...].astype(f32), axis=0, keepdims=True), sums.shape
    )
    partial[...] = two
    send_blocks(place[0], two_blocks, partial, quarter, special)


def proj_grad_kernel(parts, place, normed, joined, bias, out_grad, up_bias, keep, send, whole):
    columns = joined.shape[1]
    whole[:columns] = dot_tn(joined[...], normed[...])
    whole[columns : columns + 16, :columns] = bias[...].astype(f32)
    whole[columns : columns + 16, columns:] = jnp.zeros((16, normed.shape[1] - columns), f32)
    start = columns + 16 + out_grad.shape[0]
    whole[columns + 16 : start] = out_grad[...].astype(f32)
    whole[start : start + 16] = up_bias[...].astype(f32)
    whole[start + 16 :] = jnp.zeros((whole.shape[0] - start - 16, normed.shape[1]), f32)
    half = keep.shape[0]
    core = lax.rem(place[1], parts) if parts == 2 else 0
    keep[...] = whole[pl.ds(pl.multiple_of(core * half, 16), half)]
    send[...] = whole[pl.ds(pl.multiple_of((1 - core) * half if parts == 2 else 0, 16), half)].astype(bf16)


def chip_parts_kernel(place, keep, received, mine, *sends_and_whole):
    *sends, whole = sends_and_whole
    whole[...] = keep[...] + received[...].astype(f32)
    part = mine.shape[0]
    chip = place[1] // 2
    mine[...] = whole[pl.ds(pl.multiple_of(chip * part, 16), part)]
    for i, send in enumerate(sends):
        at = pl.multiple_of(jnp.bitwise_xor(chip, i + 1) * part, 16)
        send[...] = whole[pl.ds(at, part)].astype(bf16)


def add_parts_kernel(mine, first, second, third, out):
    total = mine[...] + first[...].astype(f32) + second[...].astype(f32) + third[...].astype(f32)
    out[...] = total.astype(bf16)


def split_kernel(first, place, *refs):
    *blocks, out, bias, out_w, up_bias, sums = refs
    part = sums.shape[0] // len(blocks)
    start = first
    if len(blocks) == 1:
        sums[...] = blocks[0][...]
    else:
        for k, block in enumerate(blocks):
            source = jnp.bitwise_xor(place[1], k)
            at = (lax.rem(source, 2) * (len(blocks) // 2) + source // 2) * part
            sums[pl.ds(pl.multiple_of(at, 16), part)] = block[start : start + part]
    out[0] = sums[: 3 * DH].astype(f32)
    out[1] = sums[4 * DH : 7 * DH].astype(f32)
    out[2, : 2 * DH] = sums[8 * DH : 10 * DH].astype(f32)
    out[2, 2 * DH :] = sums[7 * DH : 8 * DH].astype(f32)
    tail = sums[10 * DH : 10 * DH + 8].astype(f32)
    third = pltpu.roll(tail[:, 384:512], DH, 1)
    bias[0:1] = tail[0:1, : 3 * DH]
    bias[1:2, :128] = tail[0:1, 512:640]
    bias[1:2, 128:] = third[0:1, :DH]
    start = 10 * DH + 16
    out_w[...] = sums[start : start + out_w.shape[0]].astype(f32)
    start += out_w.shape[0]
    up_bias[...] = sums[start : start + 8].astype(f32)


def half_parts_kernel(place, keep, received, p_keep, q_keep, p_send, q_send, whole):
    whole[...] = keep[...] + received[...].astype(f32)
    part = p_keep.shape[0]
    x, y = lax.rem(place[1] // 2, 2), place[1] // 4
    for start, side, mine, send in ((0, x, p_keep, p_send), (2 * part, y, q_keep, q_send)):
        mine[...] = whole[pl.ds(pl.multiple_of(start + side * part, 16), part)]
        send[...] = whole[pl.ds(pl.multiple_of(start + (1 - side) * part, 16), part)].astype(bf16)


def quarter_parts_kernel(place, p, q, p_in, q_in, p_keep, q_keep, p_send, q_send, p_all, q_all):
    part = p_keep.shape[0]
    x, y = lax.rem(place[1] // 2, 2), place[1] // 4
    p_all[...] = p[...] + p_in[...].astype(f32)
    q_all[...] = q[...] + q_in[...].astype(f32)
    for whole, side, mine, send in ((p_all, y, p_keep, p_send), (q_all, x, q_keep, q_send)):
        mine[...] = whole[pl.ds(pl.multiple_of(side * part, 16), part)]
        send[...] = whole[pl.ds(pl.multiple_of((1 - side) * part, 16), part)].astype(bf16)


def add_two_kernel(p, q, p_in, q_in, p_out, q_out):
    p_out[...] = (p[...] + p_in[...].astype(f32)).astype(bf16)
    q_out[...] = (q[...] + q_in[...].astype(f32)).astype(bf16)


def feed_out_kernel(place, *refs):
    *blocks, down, up = refs
    part = down.shape[0] // 8
    for k, block in enumerate(blocks):
        source = jnp.bitwise_xor(place[1], k)
        x, y = lax.rem(source // 2, 2), source // 4
        start = block.shape[0] - 2 * part
        spots = (2 * x + y) * part, (4 + 2 * y + x) * part

        def put(out, block=block, start=start, spots=spots):
            for i, spot in enumerate(spots):
                rows = block[start + i * part : start + (i + 1) * part]
                out[pl.ds(pl.multiple_of(spot, 16), part)] = rows.astype(f32)

        @pl.when(lax.rem(source, 2) == 0)
        def _(put=put):
            put(down)

        @pl.when(lax.rem(source, 2) == 1)
        def _(put=put):
            put(up)


def send_blocks(me, parts, partial, quarter, special):
    tp_count = len(parts)
    rows = quarter * tp_count
    for k in range(tp_count):
        spot = lax.rem(me + k, tp_count)
        patch_at = pl.ds(pl.multiple_of(spot * quarter, 16), quarter)
        special_at = pl.ds(pl.multiple_of(rows + spot * special, 16), special)
        parts[k][:quarter] = partial[patch_at].astype(parts[k].dtype)
        parts[k][quarter:] = partial[special_at].astype(parts[k].dtype)


def mid_back_kernel(sizes, place, *refs):
    (quarter,) = sizes
    parts, mid, one, grad_result, two_sums, scale, bias, gain = refs[:8]
    grad_mid_out, grad_one_out, small = refs[8:]
    weight = row_weight(mid.shape[0], quarter, place[1])
    incoming = parts[...]
    unit, scaling = norm_parts(mid[...])
    grad_mid = grad_result[...] + norm_back(unit, scaling, incoming * gain[...])
    weighted = incoming * weight
    weighted_mid = grad_mid * weight
    result_sum = jnp.sum(grad_result[...] * weight, axis=0, keepdims=True)
    small[0:2] = jnp.zeros((2, small.shape[1]), f32)
    small[2:3] = jnp.sum(weighted * unit, axis=0, keepdims=True)
    small[3:4] = jnp.sum(weighted, axis=0, keepdims=True)
    small[4:5] = jnp.sum(weighted_mid * (one[...] + bias[0:1]), axis=0, keepdims=True)
    small[5:6] = jnp.sum(weighted_mid, axis=0, keepdims=True) * scale[0:1]
    small[6:7] = two_sums[0:1] + result_sum * bias[1:2]
    small[7:8] = result_sum * scale[1:2]
    grad_mid_out[...] = grad_mid
    grad_one = (grad_mid * scale[0:1]).astype(bf16)
    grad_one_out[...] = grad_one


def delta_kernel(sizes, place, *refs):
    tp_count, quarter, special = sizes
    parts = refs[:tp_count]
    attended, attended_b, w_outs, out, out_patch, out_grad, whole = refs[tp_count:]
    rows = quarter * tp_count
    me = place[0]
    for k in range(tp_count):
        spot = lax.rem(me - k + tp_count, tp_count)
        whole[pl.ds(pl.multiple_of(spot * quarter, 16), quarter)] = parts[k][:quarter]
        whole[pl.ds(pl.multiple_of(rows + spot * special, 16), special)] = parts[k][quarter:]
    value = dot_nt(whole[...], w_outs[0, :LANES]).astype(bf16).astype(f32)
    total = value.shape[0]
    product = value * attended[...]
    lane = lanes_of(value.shape)
    for h in range(3):
        delta = jnp.sum(jnp.where(value_head(lane, h), product, 0.0), axis=-1, keepdims=True)
        for piece, part in enumerate(three_pieces(delta)):
            value = jnp.where(lane == 2 * DH + DELTA_LANE + 3 * h + piece, part, value)
    out[...] = value.astype(bf16)
    out_patch[...] = value[:rows].astype(bf16)
    weighted = (whole[...].astype(f32) * row_weight(total, rows, place[1])).astype(bf16)
    product = dot_tn(attended_b[...], weighted).astype(bf16)
    out_grad[: 2 * DH] = product[: 2 * DH]
    out_grad[2 * DH :] = product[3 * DH :]


def query_grad_kernel(sizes, windows, query, grad, keys, values, out):
    bands, images, rows = sizes
    lane = lanes_of((1, LANES))
    key_picks = [key_side(lane, h, images) for h in range(3)]
    value_picks = [value_side(lane, h) for h in range(3)]
    head_picks = [key_head(lane, h) for h in range(3)]

    def part(own, pulled, chunk):
        key_part = keys[chunk]
        probs = jnp.exp(dot_nt(own, key_part))
        return dot((probs * dot_nt(pulled, values[chunk])).astype(bf16), key_part)

    for u in range(bands):
        window = pl.ds(pl.multiple_of(windows[u], BAND), WINDOW)
        spot = pl.ds(u * BAND, BAND)
        summed = part(stacked(query[spot], key_picks), stacked(grad[spot], value_picks), window)
        out[spot] = (spread_sum(summed, head_picks) * DH**-0.5).astype(bf16)

    own = stacked(first_rows(query[rows:]), key_picks)
    pulled = stacked(first_rows(grad[rows:]), value_picks)
    summed = lax.fori_loop(
        0,
        chunk_count(windows, bands, images),
        lambda c, summed: summed + part(own, pulled, chunk_at(0, c)),
        jnp.zeros((own.shape[0], LANES), f32),
    )
    put_first_rows(out, rows, spread_sum(summed, head_picks) * DH**-0.5)


def pair_grad_kernel(sizes, place, slots, windows, *refs):
    blocks_count, bands, images, tp_count, quarter, special = sizes
    query_blocks = refs[:blocks_count]
    blocks = refs[blocks_count : 2 * blocks_count]
    rest = refs[2 * blocks_count :]
    query_own, grad_own, key_own, value_own, grad_query, w_cat, joined_out, bias_out = rest[:8]
    parts = rest[8 : 8 + tp_count]
    queries, grads, joined, partial = rest[8 + tp_count :]
    rows = quarter * tp_count
    lane = lanes_of((1, LANES))
    image_lane = (lane >= 3 * DH) & (lane <= 3 * DH + images)
    empty = jnp.where(image_lane, FAR, 0.0)

    def clear(at, carry):
        at = pl.multiple_of(at, BAND)
        queries[pl.ds(at, BAND)] = jnp.broadcast_to(empty, (BAND, LANES)).astype(bf16)
        grads[pl.ds(at, BAND)] = jnp.zeros((BAND, LANES), bf16)
        return carry

    clear_unused(clear, windows, bands, images, queries.shape[0])
    per_block = blocks[0].shape[0] // BAND
    slot_count = blocks_count * per_block
    for b in range(blocks_count):

        def put(j, b=b):
            slot = b * per_block + j

            @pl.when(slots[2 * slot_count + slot] > 0)
            def _():
                at = pl.multiple_of(slots[slot], BAND)
                source = pl.ds(pl.multiple_of(j * BAND, BAND), BAND)
                if blocks_count == 1:
                    target = pl.ds(at, BAND)
                    pltpu.sync_copy(blocks[b].at[source], grads.at[target])
                    pltpu.sync_copy(query_blocks[b].at[source], queries.at[target])
                else:
                    grads[pl.ds(at, BAND)] = blocks[b][source]
                    queries[pl.ds(at, BAND)] = query_blocks[b][source]

        for_each(per_block, put)

    def put_special(i):
        at = pl.multiple_of(windows[bands + i], BAND)
        source = pl.ds(pl.multiple_of(rows + i * GROUP, GROUP), GROUP)
        queries[pl.ds(at, GROUP)] = query_own[source]
        grads[pl.ds(at, GROUP)] = grad_own[source]

    for_each(images, put_special)
    key_picks = [key_side(lane, h, images) for h in range(3)]
    value_picks = [value_side(lane, h) for h in range(3)]
    key_heads = [key_head(lane, h) for h in range(3)]
    value_heads = [value_head(lane, h) for h in range(3)]

    def part(own, held, chunk, state):
        grad_key, grad_value = state
        query_part, grad_part = queries[chunk], grads[chunk]
        probs = jnp.exp(dot_nt(own, query_part))
        scores = (probs * dot_nt(held, grad_part)).astype(bf16)
        return (
            grad_key + dot(scores, query_part),
            grad_value + dot(probs.astype(bf16), grad_part),
        )

    def finish(state):
        grad_key = spread_sum(state[0], key_heads)
        grad_value = spread_sum(state[1], value_heads)
        half = lanes_of((1, 128))
        last = jnp.where(half < DH, grad_key[:, 128:], grad_value[:, 128:])
        return jnp.concatenate([grad_key[:, :128], last, grad_value[:, :128]], axis=1)

    joined[:, :256] = grad_query[...]

    def band(u):
        window = pl.ds(pl.multiple_of(windows[u], BAND), WINDOW)
        spot = pl.ds(pl.multiple_of(u * BAND, BAND), BAND)
        own, held = stacked(key_own[spot], key_picks), stacked(value_own[spot], value_picks)
        joined[spot, 256:] = finish(part(own, held, window, (0.0, 0.0))).astype(bf16)

    for u in range(bands):
        band(u)
    own = stacked(first_rows(key_own[rows:]), key_picks)
    held = stacked(first_rows(value_own[rows:]), value_picks)
    blank = jnp.zeros((own.shape[0], LANES), f32)
    state = lax.fori_loop(
        0,
        chunk_count(windows, bands, images),
        lambda c, state: part(own, held, chunk_at(0, c), state),
        (blank, blank),
    )
    put_first_rows(joined.at[:, 256:], rows, finish(state))
    partial[...] = dot(joined[...], w_cat[...])
    send_blocks(place[0], parts, partial, quarter, special)
    weighted = joined[...].astype(f32) * row_weight(joined.shape[0], rows, place[1])
    joined_out[...] = weighted.astype(bf16)
    bias_out[...] = jnp.broadcast_to(jnp.sum(weighted, axis=0, keepdims=True), bias_out.shape).astype(bf16)


def sum_kernel(*refs):
    *parts, out = refs
    total = parts[0][...]
    for part in parts[1:]:
        total += part[...].astype(f32)
    out[...] = total


def stream_back_kernel(sizes, place, *refs):
    quarter, = sizes
    parts, stream, grad_mid, gain, early, out, out_special, send, small = refs
    weight = row_weight(stream.shape[0], quarter, place[1])
    incoming = parts[...]
    unit, scaling = norm_parts(stream[...])
    result = grad_mid[...] + norm_back(unit, scaling, incoming * gain[...])
    out[...] = result[:quarter]
    cut_groups(out_special, result[quarter:], out_special.shape[0] // SPECIALS)
    weighted = incoming * weight
    first = jnp.sum(weighted * unit, axis=0, keepdims=True)
    second = jnp.sum(weighted, axis=0, keepdims=True)
    sums = jnp.concatenate([first, second, early[2:8]], axis=0)
    small[...] = sums
    send[:quarter] = result[:quarter].astype(bf16)
    send[quarter:] = sums.astype(bf16)


def join_kernel(*refs):
    *parts, out = refs
    start = 0
    for part in parts:
        out[start : start + part.shape[0]] = part[...]
        start += part.shape[0]


def pack_kernel(cut, x_first, y_first, second, to_y, to_x):
    to_y[:cut] = x_first[:cut]
    to_y[cut:] = second[...]
    rest = y_first.shape[0] - cut
    to_x[:rest] = y_first[cut:]
    to_x[rest:] = second[...]


def unpack_kernel(cut, cut_second, from_x, from_y, diagonal, x_second, y_second, to_y, to_x):
    rest = diagonal.shape[0] - cut
    diagonal[:cut] = from_y[:cut]
    diagonal[cut:] = from_x[:rest]
    x_second[...] = from_x[rest:]
    y_second[...] = from_y[cut:]
    to_y[...] = from_x[rest : rest + cut_second]
    to_x[...] = from_y[cut + cut_second :]


def position_kernel(sizes, place, slots, spots, *refs):
    seq_count, tp_count, images, rows = sizes
    blocks = refs[: 2 * seq_count]
    out, *smalls, ordered, tiny = refs[2 * seq_count :]
    bands = rows // BAND
    slot_count = seq_count * bands
    quarter = rows // tp_count
    piece = 32
    in_piece = lax.broadcasted_iota(jnp.int32, (piece, 1), 0)
    for c in range(tp_count):
        tp = lax.rem(place[0] - c + tp_count, tp_count)
        for k in range(seq_count):
            block = blocks[k] if c == 0 else blocks[seq_count + k]
            block = block.at[pl.ds(max(c - 1, 0) * (quarter + 8), quarter + 8)]
            seq = jnp.bitwise_xor(place[1], k)
            tiny[pl.ds(pl.multiple_of((seq * tp_count + tp) * 8, 8), 8)] = block[
                quarter : quarter + 8
            ].astype(f32)
            for r in range(quarter // piece):
                spot = tp * (quarter // piece) + r
                slot = k * bands + spot // 2
                shift = (spot % 2) * piece
                at = pl.multiple_of(slots[3 * slot_count + slot] + shift, piece)
                valid = slots[2 * slot_count + slot] - shift
                ordered[pl.ds(at, piece)] = jnp.where(
                    in_piece < valid, block[r * piece : (r + 1) * piece].astype(f32), 0.0
                )
    total = tiny[0:8]
    for i in range(1, seq_count * tp_count):
        total += tiny[i * 8 : (i + 1) * 8]
    for out_small, first, second in zip(smalls, (5, 0, 1, 4), (7, 2, 3, 6)):
        out_small[0:1] = total[first : first + 1]
        out_small[1:2] = total[second : second + 1]
    low_rows = out.shape[0] - PATCH_BIG
    seen_big, seen_low = jnp.int32(0), jnp.int32(0)
    for i in range(images):
        at = pl.multiple_of(spots[i], BAND)
        is_big = spots[images + i]
        seen = jnp.where(is_big > 0, seen_big, seen_low)

        @pl.when((is_big > 0) & (seen == 0))
        def _():
            out[:PATCH_BIG] = ordered[pl.ds(at, BIG_BANDS * BAND)][:PATCH_BIG]

        @pl.when((is_big > 0) & (seen > 0))
        def _():
            out[:PATCH_BIG] += ordered[pl.ds(at, BIG_BANDS * BAND)][:PATCH_BIG]

        @pl.when((is_big == 0) & (seen == 0))
        def _():
            out[PATCH_BIG:] = ordered[pl.ds(at, low_rows)]

        @pl.when((is_big == 0) & (seen > 0))
        def _():
            out[PATCH_BIG:] += ordered[pl.ds(at, low_rows)]

        seen_big += is_big
        seen_low += 1 - is_big


def rotated(x, k):
    count = lax.axis_size("tp")
    return lax.ppermute(x, "tp", [(i, (i + k) % count) for i in range(count)])


def from_group(x):
    return [x] + [rotated(x, k) for k in range(1, lax.axis_size("tp"))]


def to_group(blocks):
    return [blocks[0]] + [rotated(blocks[k], k) for k in range(1, len(blocks))]


def exchanged(x, k):
    count = lax.axis_size("tp")
    return lax.ppermute(x, "tp", [(i, i ^ k) for i in range(count)])


def partner(x, k):
    count = lax.axis_size("seq")
    return lax.ppermute(x, "seq", [(i, i ^ k) for i in range(count)])


def from_chips(x):
    if lax.axis_size("seq") != 8:
        return [lax.all_gather(x, "seq", axis=0, tiled=True)]
    return [x] + [partner(x, k) for k in (2, 4, 6)]


def from_ring(x, *late):
    rows = x.shape[0]
    cut = -(-rows // 32) * 16
    along_x, along_y = partner(x, 2), partner(x, 4)
    halves = [partner(after(along_x, *late)[:cut], 4), partner(after(along_y, *late)[cut:], 2)]
    (diagonal,) = call(join_kernel, [(x.shape, x.dtype)], halves, cost=1)
    return [x, along_x, along_y, diagonal]


def two_rings(first, second, ready, passed, use_first):
    cut, cut_second = -(-first.shape[0] // 32) * 16, -(-second.shape[0] // 32) * 16
    rest, rest_second = first.shape[0] - cut, second.shape[0] - cut_second
    width = first.shape[1]
    x_first, y_first = partner(first, 2), partner(first, 4)
    to_y, to_x = call(
        functools.partial(pack_kernel, cut),
        [((cut + second.shape[0], width), bf16), ((rest + second.shape[0], width), bf16)],
        [after(x_first, *ready), y_first, second],
        cost=1,
    )
    from_x, from_y = partner(to_x, 2), partner(to_y, 4)
    diagonal, x_second, y_second, to_y, to_x = call(
        functools.partial(unpack_kernel, cut, cut_second),
        [
            (first.shape, bf16),
            (second.shape, bf16),
            (second.shape, bf16),
            ((cut_second, width), bf16),
            ((rest_second, width), bf16),
        ],
        [after(from_x, *passed), from_y],
        cost=1,
    )
    first_blocks = with_other_core([first, x_first, y_first, diagonal])
    used = use_first(first_blocks)
    low, high = partner(to_y, 4), partner(to_x, 2)
    (diagonal_second,) = call(
        join_kernel, [(second.shape, bf16)], [after(low, *used), high], cost=1
    )
    second_blocks = with_other_core([second, x_second, y_second, diagonal_second])
    return first_blocks, second_blocks, used


def with_other_core(blocks):
    if len(blocks) == 1:
        return blocks
    odd = [partner(block, 1) for block in blocks]
    return [block for pair in zip(blocks, odd) for block in pair]


def from_bands(x):
    return with_other_core(from_chips(x))


def after(value, *others):
    return lax.optimization_barrier((value,) + tuple(others))[0]


def pad_heads(rows):
    gap = jnp.zeros_like(rows[:DH])
    return jnp.concatenate([rows[: 2 * DH], gap, rows[2 * DH :], gap], axis=0)


def joined_columns(query, key, value, axis):
    cut = functools.partial(lax.slice_in_dim, axis=axis)
    return jnp.concatenate(
        [
            query,
            jnp.zeros_like(cut(query, 0, DH)),
            key,
            cut(value, 2 * DH, 3 * DH),
            cut(value, 0, 2 * DH),
        ],
        axis=axis,
    )


def on_device(
    patches,
    specials,
    pos_table,
    image_length,
    slot_band,
    w_qkv,
    qv_bias,
    w_out,
    branch_bias,
    ln_gain,
    ln_bias,
    layer_scale,
    w_up,
    up_bias,
    w_down,
    cot_patch,
    cot_special,
):
    seq_count = lax.axis_size("seq")
    tp_count = lax.axis_size("tp")
    seq_place = lax.axis_index("seq")
    tp_place = lax.axis_index("tp")
    near = seq_count == 8
    quarter, width = patches.shape
    ff = w_up.shape[1]
    images = image_length.shape[0]
    rows = quarter * tp_count
    bands = rows // BAND
    slot_count = slot_band.shape[0]
    special = (specials.shape[0] // SPECIALS) * GROUP
    special_rows = special * tp_count
    total = rows + special_rows
    block = quarter + special
    place = jnp.stack([tp_place, seq_place]).astype(jnp.int32)

    (x_own,) = call(
        gather_rows_kernel,
        [((block, width), bf16)],
        [patches, specials],
        cost=1,
        spare=58,
    )
    x_parts = from_group(x_own)
    windows, spots, at_table, row_image, position = call(
        functools.partial(plan_kernel, (seq_count, bands, images, rows)),
        [
            ((bands + images + 1,), jnp.int32),
            ((2 * images,), jnp.int32),
            ((2 * bands,), jnp.int32),
            ((total, 1), jnp.int32),
            ((rows, 1), jnp.int32),
        ],
        [image_length, slot_band, place],
        [pltpu.SMEM((images,), jnp.int32)],
    )
    half = w_out.shape[0] // 2
    if near:
        (mine,) = call(
            half_kernel, [((half, width), bf16)], [place, after(w_out, x_own)], cost=1
        )
    w_cat = joined_columns(*jnp.transpose(w_qkv, (0, 2, 1)), 0)
    b_cat = joined_columns(qv_bias[:1], jnp.zeros_like(qv_bias[:1]), qv_bias[1:], 1)
    stream, stream_own, normed, query, pack, key_own, value_own = call(
        functools.partial(embed_kernel, (tp_count, quarter, special, images)),
        [
            ((total, width), f32),
            ((block, width), f32),
            ((total, width), bf16),
            ((total, LANES), bf16),
            ((rows, 384), bf16),
            ((total, LANES), bf16),
            ((total, LANES), bf16),
        ],
        [place, at_table, *x_parts, pos_table, w_cat, b_cat, ln_gain[:1], ln_bias[:1], row_image],
        [
            pltpu.VMEM((rows, width), f32),
            pltpu.VMEM((pos_table.shape[0] - PATCH_BIG, width), f32),
        ],
        cost=4,
    )

    (slots,) = call(
        functools.partial(slots_kernel, (seq_count, bands, images)),
        [((4 * slot_count,), jnp.int32)],
        [image_length, slot_band, after(place, pack)],
        [pltpu.SMEM((images,), jnp.int32)],
        cost=4,
    )
    chips = from_chips(pack)
    if near:
        chips[3] = after(chips[3], slots)
        mine = after(mine, pack)
        (two_halves,) = call(
            functools.partial(in_order_kernel, 0, 1),
            [((2 * half, width), bf16)],
            [place, mine, exchanged(mine, 1)],
            cost=1,
        )
        (four_halves,) = call(
            functools.partial(in_order_kernel, 0, 2),
            [((4 * half, width), bf16)],
            [place, two_halves, exchanged(two_halves, 2)],
            cost=6,
        )
    pairs = with_other_core(chips)
    if near:
        (w_outs,) = call(
            assemble_kernel,
            [((tp_count, LANES + DH, width), bf16)],
            [place, four_halves, partner(four_halves, 1)],
            cost=1,
        )
    else:
        w_outs = jnp.stack([pad_heads(part) for part in from_group(w_out)])
    grad_two_w, cot_weighted, grad_hidden, grad_result = call(
        functools.partial(cotangent_kernel, (quarter, special)),
        [
            ((total, width), bf16),
            ((total, width), bf16),
            ((total, ff), f32),
            ((block, width), f32),
        ],
        [place, cot_patch, cot_special, layer_scale, after(w_down, pack)],
        [pltpu.VMEM((total, width), f32)],
        cost=3,
    )

    buffer_rows = (slot_count + images) * BAND + WINDOW
    keys, values, attended, attended_b, packed, query, query_patch = call(
        functools.partial(attend_kernel, (len(pairs), bands, images, rows)),
        [
            ((buffer_rows, LANES), bf16),
            ((buffer_rows, LANES), bf16),
            ((total, LANES), f32),
            ((total, LANES), bf16),
            ((total + total // 2, 128), bf16),
            ((total, LANES), bf16),
            ((rows, LANES), bf16),
        ],
        [slots, windows, *pairs, key_own, value_own, query],
        cost=8,
        spare=8,
    )
    attended_all = from_group(packed)
    query_chips = from_ring(query_patch, attended_all[1]) if near else []

    feed = call(
        functools.partial(feed_kernel, (tp_count, quarter, special)),
        [
            ((block, width), f32),
            ((block, width), f32),
            ((total, width), bf16),
            ((total, ff), bf16),
            ((total, ff), bf16),
            ((16, ff), bf16),
            ((block, width), f32),
        ]
        + [((block, width), bf16)] * (tp_count - 1),
        [
            place,
            *attended_all,
            w_outs,
            after(stream, *query_chips[1:3]),
            layer_scale,
            branch_bias,
            ln_gain[1:],
            ln_bias[1:],
            w_up,
            up_bias[None],
            grad_hidden,
        ],
        [pltpu.VMEM((total, width), f32), pltpu.VMEM((total, width), f32)],
        cost=6,
        spare=8,
    )
    mid_own, one_own, normed_two, hidden, grad_pre, up_bias_grad = feed[:6]
    two_parts = to_group(feed[6:])
    keep, send, two_sums, *two_blocks = call(
        functools.partial(feed_grad_kernel, (tp_count, quarter, special, near)),
        [
            ((ff, width), f32),
            ((ff if near else ff + width, width), bf16),
            ((8, width), f32),
            ((block, width), f32),
        ]
        + [((block, width), bf16)] * (tp_count - 1),
        [
            place,
            hidden,
            normed_two,
            grad_two_w,
            grad_pre,
            w_down,
            cot_weighted,
        ],
        [pltpu.VMEM((total, width), f32)],
        cost=0.5,
        spare=8,
    )
    if near:
        p, q, p_send, q_send = call(
            half_parts_kernel,
            [((ff // 4, width), f32)] * 2 + [((ff // 4, width), bf16)] * 2,
            [place, keep, partner(send, 1)],
            [pltpu.VMEM((ff, width), f32)],
            cost=0.1,
        )
        p2, q2, p2_send, q2_send = call(
            quarter_parts_kernel,
            [((ff // 8, width), f32)] * 2 + [((ff // 8, width), bf16)] * 2,
            [place, p, q, partner(p_send, 2), partner(q_send, 4)],
            [pltpu.VMEM((ff // 4, width), f32)] * 2,
            cost=0.1,
        )
        p3, q3 = call(
            add_two_kernel,
            [((ff // 8, width), bf16)] * 2,
            [p2, q2, partner(p2_send, 4), partner(q2_send, 2)],
            cost=0.1,
        )
    else:
        feed_all = lax.psum(send, "seq")

    (grad_two_normed,) = call(sum_kernel, [((block, width), f32)], two_parts, cost=20)
    grad_mid, grad_one, early = call(
        functools.partial(mid_back_kernel, (quarter,)),
        [((block, width), f32), ((block, width), bf16), ((8, width), f32)],
        [
            place,
            grad_two_normed,
            mid_own,
            one_own,
            grad_result,
            two_sums,
            layer_scale,
            branch_bias,
            ln_gain[1:],
        ],
        cost=2,
    )
    grad_one_all = from_group(grad_one)
    if near:
        attended = after(attended, query_chips[3], p3)
    grad_attn, grad_patch, out_grad = call(
        functools.partial(delta_kernel, (tp_count, quarter, special)),
        [((total, LANES), bf16), ((rows, LANES), bf16), ((w_out.shape[0], width), bf16)],
        [place, *grad_one_all, attended, attended_b, w_outs],
        [pltpu.VMEM((total, width), bf16)],
        cost=2,
    )
    (grad_query,) = call(
        functools.partial(query_grad_kernel, (bands, images, rows)),
        [((total, LANES), bf16)],
        [windows, query, grad_attn, keys, values],
        cost=6,
        spare=8,
    )
    if near:
        grads = with_other_core(from_ring(grad_patch, grad_query))
        queries = with_other_core(query_chips)
    else:
        queries = from_chips(after(query_patch, grad_query))
        grads = from_chips(after(grad_patch, grad_query))
    pair = call(
        functools.partial(
            pair_grad_kernel, (len(grads), bands, images, tp_count, quarter, special)
        ),
        [((total, 640), bf16), ((16, 640), bf16), ((block, width), f32)]
        + [((block, width), bf16)] * (tp_count - 1),
        [
            place,
            slots,
            windows,
            *queries,
            *grads,
            query,
            grad_attn,
            key_own,
            value_own,
            grad_query,
            w_cat,
        ],
        [
            pltpu.VMEM((buffer_rows, LANES), bf16),
            pltpu.VMEM((buffer_rows, LANES), bf16),
            pltpu.VMEM((total, 640), bf16),
            pltpu.VMEM((total, width), f32),
        ],
        outside=(3, 4) if len(grads) == 1 else (),
        cost=8,
        spare=8,
    )
    joined, joined_bias = pair[:2]
    normed_parts = to_group(pair[2:])

    last_rows = -(-(640 + 32 + w_out.shape[0]) // 128) * 128
    held = last_rows // 2 if near else last_rows
    keep_last, send_last = call(
        functools.partial(proj_grad_kernel, 2 if near else 1),
        [((held, width), f32), ((held, width), bf16)],
        [place, normed, joined, joined_bias, out_grad, up_bias_grad],
        [pltpu.VMEM((last_rows, width), f32)],
        cost=0.1,
    )
    second_done = [keep_last]
    if near:
        part = last_rows // 8
        mine, *sends = call(
            chip_parts_kernel,
            [((part, width), f32)] + [((part, width), bf16)] * 3,
            [place, keep_last, partner(send_last, 1)],
            [pltpu.VMEM((last_rows // 2, width), f32)],
            cost=0.1,
        )
        received = [partner(block, k) for block, k in zip(sends, (2, 4, 6))]
        (reduced,) = call(add_parts_kernel, [((part, width), bf16)], [mine, *received], cost=0.1)
        second_done.append(reduced)
    (grad_normed,) = call(sum_kernel, [((block, width), f32)], normed_parts, cost=20)
    patch_out, special_out, send, small = call(
        functools.partial(stream_back_kernel, (quarter,)),
        [
            ((quarter, width), f32),
            ((specials.shape[0], width), f32),
            ((quarter + 8, width), bf16),
            ((8, width), f32),
        ],
        [
            place,
            grad_normed,
            after(stream_own, *second_done),
            grad_mid,
            ln_gain[:1],
            early,
        ],
        cost=1,
    )
    arrived = from_group(send)[1:]
    two_in = [rotated(after(two_blocks[k], *arrived), k) for k in range(1, tp_count)]
    def split_sums(blocks, first):
        return call(
            functools.partial(split_kernel, first),
            [
                ((3, 3 * DH, width), f32),
                ((2, 3 * DH), f32),
                ((3 * DH, width), f32),
                ((8, width), f32),
            ],
            [place, *blocks],
            [pltpu.VMEM((last_rows, width), bf16)],
            cost=2,
        )

    if not near:
        last_blocks = [lax.psum(send_last, "seq")]
        part = last_rows
        down_grad, up_grad = feed_all[:ff].astype(f32), feed_all[ff:].astype(f32)
    if near:
        (first_sent,) = call(
            join_kernel,
            [((quarter + 8 + part + ff // 4, width), bf16)],
            [send, reduced, p3, q3],
            cost=1,
        )
        (second_sent,) = call(
            join_kernel,
            [((3 * (quarter + 8), width), bf16)],
            arrived,
            cost=1,
        )

        def use_first(blocks):
            out = call(feed_out_kernel, [((ff, width), f32)] * 2, [place, *blocks], cost=2)
            return out + split_sums(blocks, quarter + 8)

        first_blocks, second_blocks, used = two_rings(
            first_sent, second_sent, arrived, two_in, use_first
        )
        down_grad, up_grad, qkv_grad, qv_bias_grad, out_grad, up_bias_grad = used
        sent = first_blocks + second_blocks
        pos_grad, *smalls = call(
            functools.partial(position_kernel, (seq_count, tp_count, images, rows)),
            [((pos_table.shape[0], width), f32)] + [((2, width), f32)] * 4,
            [place, slots, after(spots, down_grad, qkv_grad), *sent],
            [
                pltpu.VMEM((slot_count * BAND, width), f32),
                pltpu.VMEM((seq_count * tp_count * 8, width), f32),
            ],
            cost=5,
            spare=4,
        )
    else:
        qkv_grad, qv_bias_grad, out_grad, up_bias_grad = split_sums(last_blocks, 0)
        mine = lax.dynamic_slice_in_dim(position, tp_place * quarter, quarter)[:, 0]
        used = lax.dynamic_slice_in_dim(row_image, tp_place * quarter, quarter) >= 0
        local = jax.ops.segment_sum(
            jnp.where(used, patch_out, 0.0), mine, num_segments=pos_table.shape[0]
        )
        pos_grad, small = lax.psum((local, small), ("seq", "tp"))
        smalls = [jnp.stack([small[i], small[j]]) for i, j in ((5, 7), (0, 2), (1, 3), (4, 6))]
    result, result_special = call(
        functools.partial(result_kernel, (quarter, specials.shape[0] // SPECIALS)),
        [((quarter, width), bf16), (specials.shape, bf16)],
        [mid_own, layer_scale, branch_bias, two_blocks[0], *two_in],
        cost=1,
    )
    return (
        result,
        result_special,
        patch_out,
        special_out,
        pos_grad,
        jnp.transpose(qkv_grad, (0, 2, 1)),
        qv_bias_grad,
        out_grad,
        *smalls,
        up_grad,
        up_bias_grad[0],
        down_grad,
    )


def solution(mesh):
    in_specs = (
        P(("seq", "tp"), None),
        P("tp", None),
        P(),
        P(),
        P(),
        P(None, None, "tp"),
        P(None, "tp"),
        P("tp", None),
        P(),
        P(),
        P(),
        P(),
        P(None, "tp"),
        P("tp"),
        P("tp", None),
        P("seq", None),
        P(),
    )
    out_specs = (
        P(("seq", "tp"), None),
        P("tp", None),
        P(("seq", "tp"), None),
        P("tp", None),
        P(),
        P(None, None, "tp"),
        P(None, "tp"),
        P("tp", None),
        P(),
        P(),
        P(),
        P(),
        P(None, "tp"),
        P("tp"),
        P("tp", None),
    )
    return jax.shard_map(
        on_device, mesh=mesh, in_specs=in_specs, out_specs=out_specs, check_vma=False
    )
```

```python
import functools
import math

import jax
import jax.numpy as jnp
from jax import lax
from jax.experimental import pallas as pl
from jax.experimental.pallas import tpu as pltpu
from jax.sharding import PartitionSpec as P

DH = 64
SPECIALS = 5
PATCH_BIG = 1369
BAND = 64

GROUP = 16
LANES = 256
FAR = 1e30
EPS = 1e-06
BIG_BANDS = (PATCH_BIG + BAND - 1) // BAND
WINDOW = (BIG_BANDS + 1) * BAND
CHUNK = 1280
KEPT = 8
VMEM_LIMIT = 60 * 1024 * 1024

bf16 = jnp.bfloat16
f32 = jnp.float32


def dot(a, b):
    return jnp.dot(a, b, preferred_element_type=f32)


def dot_nt(a, b):
    return lax.dot_general(a, b, (((1,), (1,)), ((), ())), preferred_element_type=f32)


def dot_tn(a, b):
    return lax.dot_general(a, b, (((0,), (0,)), ((), ())), preferred_element_type=f32)


def lanes_of(shape):
    return lax.broadcasted_iota(jnp.int32, shape, len(shape) - 1)


def norm_parts(values):
    centre = jnp.mean(values, axis=-1, keepdims=True)
    centred = values - centre
    spread = jnp.mean(centred * centred, axis=-1, keepdims=True)
    scale = lax.rsqrt(spread + EPS)
    return centred * scale, scale


def norm_back(unit, scale, eg):
    first = jnp.mean(eg, axis=-1, keepdims=True)
    second = jnp.mean(eg * unit, axis=-1, keepdims=True)
    return scale * (eg - first - unit * second)


def key_head(lane, h):
    return (lane >= h * DH) & (lane < (h + 1) * DH)


def value_head(lane, h):
    start = (0, DH, 3 * DH)[h]
    return (lane >= start) & (lane < start + DH)


def key_side(lane, h, images):
    image_lane = (lane >= 3 * DH) & (lane <= 3 * DH + images)
    lse_start = 3 * DH + images + 1 + 3 * h
    return key_head(lane, h) | image_lane | ((lane >= lse_start) & (lane < lse_start + 3))


DELTA_LANE = 50


def value_side(lane, h):
    start = 2 * DH + DELTA_LANE + 3 * h
    return value_head(lane, h) | ((lane >= start) & (lane < start + 3))


def three_pieces(x):
    high = x.astype(bf16).astype(f32)
    rest = x - high
    middle = rest.astype(bf16).astype(f32)
    return high, middle, (rest - middle).astype(bf16).astype(f32)


def stacked(rows, picks):
    zero = jnp.zeros_like(rows)
    return jnp.concatenate([jnp.where(pick, rows, zero) for pick in picks], axis=0)


def spread_sum(stack, picks):
    count = stack.shape[0] // len(picks)
    total = None
    for h, pick in enumerate(picks):
        part = jnp.where(pick, stack[h * count : (h + 1) * count], 0.0)
        total = part if total is None else total + part
    return total


def held_bytes(shape, dtype):
    lanes = -(-shape[-1] // 128) * 128
    rows = -(-math.prod(shape[:-1]) // 16) * 16
    return rows * lanes * jnp.dtype(dtype).itemsize


def call(body, outs, ins, scratch=(), outside=(), cost=2, spare=6):
    spaces = []
    for i, item in enumerate(ins):
        smem = item.dtype == jnp.int32 and item.ndim == 1
        space = pl.ANY if i in outside else pltpu.SMEM if smem else pltpu.VMEM
        spaces.append(pl.BlockSpec(memory_space=space))
    need = sum(held_bytes(x.shape, x.dtype) for i, x in enumerate(ins) if i not in outside)
    need += sum(held_bytes(s, d) for s, d in outs)
    need += sum(held_bytes(x.shape, x.dtype) for x in scratch)
    out_spaces = [
        pl.BlockSpec(memory_space=pltpu.SMEM if d == jnp.int32 and len(s) == 1 else pltpu.VMEM)
        for s, d in outs
    ]
    return pl.pallas_call(
        body,
        out_shape=[jax.ShapeDtypeStruct(s, d) for s, d in outs],
        in_specs=spaces,
        out_specs=out_spaces,
        scratch_shapes=list(scratch),
        cost_estimate=pl.CostEstimate(
            flops=int(cost * 10**9), bytes_accessed=0, transcendentals=0
        ),
        compiler_params=pltpu.CompilerParams(
            vmem_limit_bytes=min(need + spare * 1024 * 1024, VMEM_LIMIT)
            if need < 2**24 + 2**23
            else VMEM_LIMIT
        ),
    )(*ins)


def for_each(count, body):
    def step(i, carry):
        body(i)
        return carry

    lax.fori_loop(0, count, step, 0)


def image_starts(images, length, held):
    def begin(i, start):
        held[i] = start
        return start + (length[i] + BAND - 1) // BAND

    return lax.fori_loop(0, images, begin, jnp.int32(0))


def band_facts(images, length, slot_band, held, used, slot):
    band = slot_band[slot]

    def look(i, state):
        image, first = state
        inside = band >= held[i]
        return jnp.where(inside, i, image), jnp.where(inside, held[i], first)

    state = (jnp.int32(0), jnp.int32(0))
    if images <= 8:
        for i in range(images):
            state = look(i, state)
    else:
        state = lax.fori_loop(0, images, look, state)
    image, first = state
    left = jnp.minimum(jnp.maximum(length[image] - (band - first) * BAND, 0), BAND)
    return band, image, first, jnp.where(band < used, left, 0)


def plan_kernel(sizes, length, slot_band, place, windows, spots, own, row_image, position, held):
    seq_count, bands, images, rows = sizes
    used = image_starts(images, length, held)

    def image_facts(i, carry):
        spots[i] = held[i] * BAND
        spots[images + i] = (length[i] == PATCH_BIG).astype(jnp.int32)
        windows[bands + i] = (held[i] + i) * BAND
        return carry

    lax.fori_loop(0, images, image_facts, 0)
    windows[bands + images] = (used + images) * BAND
    in_band = lax.broadcasted_iota(jnp.int32, (BAND, 1), 0)
    for u in range(bands):
        band, image, first, valid = band_facts(
            images, length, slot_band, held, used, place[1] * bands + u
        )
        windows[u] = jnp.where(valid > 0, (first + image) * BAND, 0)
        own[u] = jnp.where(valid > 0, (band - first) * BAND, 0)
        own[bands + u] = (length[image] == PATCH_BIG).astype(jnp.int32)
        good = in_band < valid
        row_image[u * BAND : (u + 1) * BAND] = jnp.where(good, image, -1)
        offset = jnp.where(length[image] == PATCH_BIG, 0, PATCH_BIG) + (band - first) * BAND
        position[u * BAND : (u + 1) * BAND] = jnp.where(good, offset + in_band, 0)
    group = lax.broadcasted_iota(jnp.int32, (images * GROUP, 1), 0)
    row_image[rows:] = jnp.where(group % GROUP < SPECIALS, group // GROUP, -1)


def slots_kernel(sizes, length, slot_band, place, slots, held):
    seq_count, bands, images = sizes
    slot_count = seq_count * bands
    used = image_starts(images, length, held)

    def put(i, carry):
        source = i // bands
        if seq_count == 8:
            source = jnp.bitwise_xor(source, place[1])
        band, image, _, valid = band_facts(
            images, length, slot_band, held, used, source * bands + i % bands
        )
        slots[i] = jnp.where(valid > 0, (band + image + 1) * BAND, 0)
        slots[slot_count + i] = image
        slots[2 * slot_count + i] = valid
        slots[3 * slot_count + i] = band * BAND
        return carry

    lax.fori_loop(0, slot_count, put, 0)


def gather_rows_kernel(patches, specials, out):
    quarter = patches.shape[0]
    out[:quarter] = patches[...]
    padding = jnp.zeros((KEPT - SPECIALS, patches.shape[1]), f32)
    for g in range(specials.shape[0] // SPECIALS):
        group = specials[g * SPECIALS : (g + 1) * SPECIALS].astype(f32)
        out[quarter + g * KEPT : quarter + (g + 1) * KEPT] = jnp.concatenate(
            [group, padding], axis=0
        ).astype(bf16)


def kept_rows(whole, start, groups):
    at = [pl.ds(pl.multiple_of(start + g * GROUP, GROUP), KEPT) for g in range(groups)]
    return jnp.concatenate([whole[spot].astype(f32) for spot in at], axis=0)


def put_kept_rows(whole, start, rows):
    padding = jnp.zeros((GROUP - KEPT, rows.shape[1]), f32)
    rows = rows.astype(f32)
    for g in range(rows.shape[0] // KEPT):
        group = jnp.concatenate([rows[g * KEPT : (g + 1) * KEPT], padding], axis=0)
        whole[pl.ds(pl.multiple_of(start + g * GROUP, GROUP), GROUP)] = group.astype(whole.dtype)


def row_weight(count, patch_rows, seq, group=GROUP):
    row = lax.broadcasted_iota(jnp.int32, (count, 1), 0)
    special = ((row - patch_rows) % group < SPECIALS) & (seq == 0)
    return jnp.where((row < patch_rows) | special, 1.0, 0.0)


def embed_kernel(sizes, place, at_table, *refs):
    tp_count, quarter, special, images = sizes
    xs = refs[:tp_count]
    table, w_cat, b_cat, gain, shift, row_image = refs[tp_count : tp_count + 6]
    stream, own, normed, query, pack, key_own, value_own, pos, low = refs[tp_count + 6 :]
    low[...] = table[PATCH_BIG:].astype(f32)
    bands = quarter * tp_count // BAND
    for u in range(bands):
        at = pl.multiple_of(at_table[u], BAND)
        good = row_image[u * BAND : (u + 1) * BAND] >= 0

        @pl.when(at_table[bands + u] > 0)
        def _(u=u, at=at, good=good):
            pos[u * BAND : (u + 1) * BAND] = jnp.where(
                good, table[pl.ds(at, BAND)].astype(f32), 0.0
            )

        @pl.when(at_table[bands + u] == 0)
        def _(u=u, at=at, good=good):
            pos[u * BAND : (u + 1) * BAND] = jnp.where(good, low[pl.ds(at, BAND)], 0.0)

    rows = quarter * tp_count
    me = place[0]
    for k in range(tp_count):
        spot = lax.rem(me - k + tp_count, tp_count)
        patch_at = pl.multiple_of(spot * quarter, 16)
        special_at = rows + spot * special
        part = xs[k][:quarter].astype(f32) + pos[pl.ds(patch_at, quarter)]
        stream[pl.ds(patch_at, quarter)] = part
        tail = xs[k][quarter:].astype(f32)
        put_kept_rows(stream, special_at, tail)
        if k == 0:
            own[:quarter] = part
            own[quarter:] = tail
    unit, _ = norm_parts(stream[...])
    rounded = (unit * gain[...] + shift[...]).astype(bf16)
    normed[...] = rounded
    projected = (dot_nt(rounded, w_cat[...]) + b_cat[...]).astype(bf16)
    image = row_image[...]
    total = image.shape[0]
    lane = lanes_of((total, LANES))
    image_lane = (lane >= 3 * DH) & (lane <= 3 * DH + images)
    scaled = projected[:, :LANES].astype(f32) * (DH**-0.5)
    far = jnp.where(image_lane & (lane != 3 * DH + image), FAR, 0.0)
    query[...] = jnp.where(lane < 3 * DH, scaled, far).astype(bf16)
    pack[...] = projected[:rows, LANES:]
    own_lane = 3 * DH + jnp.where(image < 0, images, image)
    lse_lane = (lane > 3 * DH + images) & (lane <= 3 * DH + images + 9)
    aux = jnp.where((lane == own_lane) | lse_lane, -1.0, 0.0)
    key_own[...] = jnp.where(
        lane < 3 * DH, projected[:, LANES : 2 * LANES].astype(f32), aux
    ).astype(bf16)
    half = lanes_of((total, 128))
    value_own[:, :128] = projected[:, 512:640]
    value_own[:, 128:] = jnp.where(
        half < DH,
        jnp.where((half >= DELTA_LANE) & (half < DELTA_LANE + 9), -1.0, 0.0),
        projected[:, 384:512].astype(f32),
    ).astype(bf16)


def chunk_count(windows, bands, images):
    return (windows[bands + images] + CHUNK - 1) // CHUNK


def chunk_at(start, c):
    return pl.ds(pl.multiple_of(start + c * CHUNK, BAND), CHUNK)


def first_rows(rows):
    rows = rows.astype(f32)
    count = rows.shape[0] // GROUP
    return jnp.concatenate([rows[i * GROUP : i * GROUP + KEPT] for i in range(count)], axis=0).astype(
        bf16
    )


def put_first_rows(target, start, rows):
    padding = jnp.zeros((GROUP - KEPT, rows.shape[1]), f32)
    count = rows.shape[0] // KEPT
    rows = rows.astype(f32)
    target[pl.ds(start, count * GROUP)] = jnp.concatenate(
        [part for i in range(count) for part in (rows[i * KEPT : (i + 1) * KEPT], padding)], axis=0
    ).astype(target.dtype)


def clear_unused(clear, windows, bands, images, buffer_rows):
    lax.fori_loop(0, images, lambda i, c: clear(windows[bands + i], c), 0)
    lax.fori_loop(
        windows[bands + images] // BAND,
        jnp.maximum(
            windows[bands + images - 1] // BAND + -(-WINDOW // BAND),
            chunk_count(windows, bands, images) * (CHUNK // BAND),
        ),
        lambda i, c: clear(i * BAND, c),
        0,
    )


def half_kernel(place, rows, out):
    half = out.shape[0]
    out[...] = rows[pl.ds(pl.multiple_of(lax.rem(place[1], 2) * half, 16), half)]


def in_order_kernel(axis, bit, place, mine, other, out):
    count = mine.shape[0]
    side = lax.rem(place[axis] // bit, 2)
    out[pl.ds(pl.multiple_of(side * count, 16), count)] = mine[...]
    out[pl.ds(pl.multiple_of((1 - side) * count, 16), count)] = other[...]


def assemble_kernel(place, mine, other, out):
    count = out.shape[0]
    half = mine.shape[0] // count
    cut = 2 * DH - half
    for k in range(count):
        spot = lax.rem(place[0] - k + count, count) * half
        at = pl.multiple_of(spot, 16)
        late = pl.multiple_of(spot + cut, 16)
        out[k, 2 * DH : 3 * DH] = jnp.zeros((DH, out.shape[2]), bf16)
        out[k, 4 * DH :] = jnp.zeros((DH, out.shape[2]), bf16)

        def fill(low, high, k=k, at=at, late=late):
            out[k, :half] = low[pl.ds(at, half)]
            out[k, half : 2 * DH] = high[pl.ds(at, cut)]
            out[k, 3 * DH : 4 * DH] = high[pl.ds(late, half - cut)]

        @pl.when(place[1] % 2 == 0)
        def _(fill=fill):
            fill(mine, other)

        @pl.when(place[1] % 2 == 1)
        def _(fill=fill):
            fill(other, mine)


def attend_kernel(sizes, slots, windows, *refs):
    blocks_count, bands, images, rows = sizes
    blocks = refs[:blocks_count]
    key_own, value_own, query = refs[blocks_count : blocks_count + 3]
    keys, values, attended, attended_b, packed, query_out, query_patch = refs[blocks_count + 3 :]
    lane = lanes_of((1, LANES))
    lse_lane = (lane > 3 * DH + images) & (lane <= 3 * DH + images + 9)
    empty = jnp.where((lane == 3 * DH + images) | lse_lane, -1.0, 0.0)
    buffer_rows = keys.shape[0]

    def clear(at, carry):
        at = pl.multiple_of(at, BAND)
        keys[pl.ds(at, BAND)] = jnp.broadcast_to(empty, (BAND, LANES)).astype(bf16)
        values[pl.ds(at, BAND)] = jnp.zeros((BAND, LANES), bf16)
        return carry

    clear_unused(clear, windows, bands, images, buffer_rows)
    band_lane = lanes_of((BAND, LANES))
    half = lanes_of((BAND, 128))
    in_band = lax.broadcasted_iota(jnp.int32, (BAND, LANES), 0)
    band_lse = (band_lane > 3 * DH + images) & (band_lane <= 3 * DH + images + 9)
    delta_aux = jnp.where((half >= DELTA_LANE) & (half < DELTA_LANE + 9), -1.0, 0.0)
    per_block = blocks[0].shape[0] // BAND
    slot_count = blocks_count * per_block
    for b in range(blocks_count):

        def place(j, b=b):
            slot = b * per_block + j
            valid = slots[2 * slot_count + slot]

            @pl.when(valid > 0)
            def _():
                at = pl.multiple_of(slots[slot], BAND)
                image = slots[slot_count + slot]
                source = blocks[b][pl.ds(pl.multiple_of(j * BAND, BAND), BAND)]
                own_lane = 3 * DH + jnp.where(in_band < valid, image, images)
                aux = jnp.where((band_lane == own_lane) | band_lse, -1.0, 0.0)
                keys[pl.ds(at, BAND)] = jnp.where(
                    band_lane < 3 * DH, source[:, :LANES].astype(f32), aux
                ).astype(bf16)
                values[pl.ds(at, BAND), :128] = source[:, 256:384]
                values[pl.ds(at, BAND), 128:] = jnp.where(
                    half < DH, delta_aux, source[:, 128:256].astype(f32)
                ).astype(bf16)

        for_each(per_block, place)

    def place_special(i):
        at = pl.multiple_of(windows[bands + i], BAND)
        source = pl.ds(pl.multiple_of(rows + i * GROUP, GROUP), GROUP)
        keys[pl.ds(at, GROUP)] = key_own[source]
        values[pl.ds(at, GROUP)] = value_own[source]

    for_each(images, place_special)
    key_picks = [key_side(lane, h, images) for h in range(3)]
    value_picks = [value_head(lane, h) for h in range(3)]

    chunks = chunk_count(windows, bands, images)

    def finish(count, own, top, total, summed):
        usable = total > 0.0
        safe = jnp.where(usable, total, 1.0)
        result = spread_sum(summed / safe, value_picks)
        lse = jnp.where(usable, top + jnp.log(safe), 0.0)
        row = own.astype(f32)
        for h in range(3):
            for piece, part in enumerate(three_pieces(lse[h * count : (h + 1) * count])):
                row = jnp.where(lane == 3 * DH + images + 1 + 3 * h + piece, part, row)
        return result, row

    for u in range(bands):
        window = pl.ds(pl.multiple_of(windows[u], BAND), WINDOW)
        spot = pl.ds(u * BAND, BAND)
        own = query[spot]
        scores = dot_nt(stacked(own, key_picks), keys[window])
        top = jnp.maximum(jnp.max(scores, axis=-1, keepdims=True), -0.1 * FAR)
        weights = jnp.exp(scores - top)
        total = jnp.sum(weights, axis=-1, keepdims=True)
        result, row = finish(BAND, own, top, total, dot(weights.astype(bf16), values[window]))
        attended[spot] = result
        attended_b[spot] = result.astype(bf16)
        query_out[spot] = row.astype(bf16)

    own = first_rows(query[rows:])
    stack = stacked(own, key_picks)
    count = stack.shape[0]

    def add(c, state):
        top, total, summed = state
        scores = dot_nt(stack, keys[chunk_at(0, c)])
        new_top = jnp.maximum(top, jnp.max(scores, axis=-1, keepdims=True))
        rescale = jnp.exp(top - new_top)
        weights = jnp.exp(scores - new_top)
        return (
            new_top,
            total * rescale + jnp.sum(weights, axis=-1, keepdims=True),
            summed * rescale + dot(weights.astype(bf16), values[chunk_at(0, c)]),
        )

    start = (
        jnp.full((count, 1), -0.1 * FAR, f32),
        jnp.zeros((count, 1), f32),
        jnp.zeros((count, LANES), f32),
    )
    result, row = finish(count // 3, own, *lax.fori_loop(0, chunks, add, start))
    put_first_rows(attended, rows, result)
    put_first_rows(attended_b, rows, result)
    put_first_rows(query_out, rows, row)
    query_patch[...] = query_out[:rows]
    kept = rows + images * KEPT
    half = kept // 2
    tails = kept_rows(attended, rows, images)
    packed[:rows] = attended_b[:rows, :128]
    packed[rows:kept] = tails[:, :128].astype(bf16)
    third = jnp.concatenate([attended[:rows, 128:], tails[:, 128:]], axis=0)
    upper = pltpu.roll(third[:half], DH, 1)
    packed[kept:] = jnp.where(lanes_of((1, 128)) < DH, upper, third[half:]).astype(bf16)


def cotangent_kernel(
    sizes, place, patch, special_rows, scale, w_down, two_weighted, weighted, hidden, own, whole
):
    quarter, special = sizes
    rows = patch.shape[0]
    whole[:rows] = patch[...].astype(f32)
    padding = jnp.zeros((GROUP - SPECIALS, patch.shape[1]), f32)
    for g in range(special_rows.shape[0] // SPECIALS):
        group = special_rows[g * SPECIALS : (g + 1) * SPECIALS].astype(f32)
        whole[rows + g * GROUP : rows + (g + 1) * GROUP] = jnp.concatenate([group, padding], axis=0)
    value = whole[...]
    weight = row_weight(whole.shape[0], rows, place[1])
    grad_two = (value * scale[1:2]).astype(bf16)
    weighted[...] = (value * weight).astype(bf16)
    two_weighted[...] = (grad_two.astype(f32) * weight).astype(bf16)
    hidden[...] = dot_nt(grad_two, w_down[...])
    own[:quarter] = whole[pl.ds(pl.multiple_of(place[0] * quarter, 16), quarter)]
    own[quarter:] = kept_rows(whole, rows + place[0] * special, special // GROUP)


def result_kernel(sizes, mid, scale, bias, *refs):
    quarter, groups = sizes
    *parts, patch, special = refs
    two = parts[0][...]
    for part in parts[1:]:
        two += part[: two.shape[0]].astype(f32)
    result = (mid[...] + scale[1:2] * (two + bias[1:2])).astype(bf16)
    patch[...] = result[:quarter]
    cut_groups(special, result[quarter:].astype(f32), groups)


def cut_groups(target, rows, groups):
    for g in range(groups):
        target[g * SPECIALS : (g + 1) * SPECIALS] = rows[g * KEPT : g * KEPT + SPECIALS].astype(
            target.dtype
        )


def feed_kernel(sizes, place, *refs):
    tp_count, quarter, special = sizes
    attended = refs[:tp_count]
    w_outs, stream, scale, bias, gain, shift, w_up, up_bias, grad_hidden = refs[
        tp_count : tp_count + 9
    ]
    mid_own, one_own, normed, hidden_out, grad_pre_out, bias_out = refs[
        tp_count + 9 : tp_count + 15
    ]
    parts = refs[tp_count + 15 : 2 * tp_count + 15]
    mid, partial = refs[2 * tp_count + 15 :]
    rows = quarter * tp_count
    me = place[0]
    kept = attended[0].shape[0] * 2 // 3
    one = 0.0
    upper, lower = 0.0, 0.0
    for k in range(tp_count):
        one += dot(attended[k][:kept], w_outs[k, : 2 * DH])
        upper += dot(attended[k][kept:], w_outs[k, 3 * DH :])
        lower += dot(attended[k][kept:], w_outs[k, 2 * DH : 4 * DH])
    one = one + jnp.concatenate([upper, lower], axis=0)
    partial[:rows] = one[:rows]
    put_kept_rows(partial, rows, one[rows:])
    value = stream[...] + scale[0:1] * (partial[...] + bias[0:1])
    mid[...] = value
    own_patch = pl.ds(pl.multiple_of(me * quarter, 16), quarter)
    own_special = rows + me * special, special // GROUP
    mid_own[:quarter] = mid[own_patch]
    mid_own[quarter:] = kept_rows(mid, *own_special)
    one_own[:quarter] = partial[own_patch]
    one_own[quarter:] = kept_rows(partial, *own_special)
    unit, _ = norm_parts(value)
    rounded = (unit * gain[...] + shift[...]).astype(bf16)
    normed[...] = rounded
    pre = dot(rounded, w_up[...]) + up_bias[...]
    share = 0.5 * (1.0 + lax.erf(pre * (0.5**0.5)))
    hidden_out[...] = (pre * share).astype(bf16)
    slope = share + pre * jnp.exp(-0.5 * pre * pre) * (0.5 / jnp.pi) ** 0.5
    grad_pre = (grad_hidden[...] * slope).astype(bf16)
    weight = row_weight(value.shape[0], rows, place[1])
    weighted = grad_pre.astype(f32) * weight
    grad_pre_out[...] = weighted.astype(bf16)
    bias_out[...] = jnp.broadcast_to(jnp.sum(weighted, axis=0, keepdims=True), bias_out.shape).astype(bf16)
    partial[...] = dot_nt(grad_pre, w_up[...])
    send_blocks(me, parts, partial, quarter, special)


def feed_grad_kernel(sizes, place, *refs):
    tp_count, quarter, special, split = sizes
    hidden, normed, grad_two, grad_pre, w_down, grad_result, keep, send, sums = refs[:9]
    two_blocks = refs[9 : 9 + tp_count]
    partial = refs[-1]
    ff = hidden.shape[1]
    down = dot_tn(hidden[...], grad_two[...])
    up = dot_tn(normed[...], grad_pre[...])
    if split:

        @pl.when(place[1] % 2 == 0)
        def _():
            keep[...] = down
            send[...] = up.astype(bf16)

        @pl.when(place[1] % 2 == 1)
        def _():
            keep[...] = up
            send[...] = down.astype(bf16)

    else:
        keep[...] = down
        send[:ff] = down.astype(bf16)
        send[ff:] = up.astype(bf16)
    two = dot(hidden[...], w_down[...])
    sums[...] = jnp.broadcast_to(
        jnp.sum(two * grad_result[...].astype(f32), axis=0, keepdims=True), sums.shape
    )
    partial[...] = two
    send_blocks(place[0], two_blocks, partial, quarter, special)


def proj_grad_kernel(parts, place, normed, joined, bias, out_grad, up_bias, keep, send, whole):
    columns = joined.shape[1]
    whole[:columns] = dot_tn(joined[...], normed[...])
    whole[columns : columns + 16, :columns] = bias[...].astype(f32)
    whole[columns : columns + 16, columns:] = jnp.zeros((16, normed.shape[1] - columns), f32)
    start = columns + 16 + out_grad.shape[0]
    whole[columns + 16 : start] = out_grad[...].astype(f32)
    whole[start : start + 16] = up_bias[...].astype(f32)
    whole[start + 16 :] = jnp.zeros((whole.shape[0] - start - 16, normed.shape[1]), f32)
    half = keep.shape[0]
    core = lax.rem(place[1], parts) if parts == 2 else 0
    keep[...] = whole[pl.ds(pl.multiple_of(core * half, 16), half)]
    send[...] = whole[pl.ds(pl.multiple_of((1 - core) * half if parts == 2 else 0, 16), half)].astype(bf16)


def chip_parts_kernel(place, keep, received, mine, *sends_and_whole):
    *sends, whole = sends_and_whole
    whole[...] = keep[...] + received[...].astype(f32)
    part = mine.shape[0]
    chip = place[1] // 2
    mine[...] = whole[pl.ds(pl.multiple_of(chip * part, 16), part)]
    for i, send in enumerate(sends):
        at = pl.multiple_of(jnp.bitwise_xor(chip, i + 1) * part, 16)
        send[...] = whole[pl.ds(at, part)].astype(bf16)


def add_parts_kernel(mine, first, second, third, out):
    total = mine[...] + first[...].astype(f32) + second[...].astype(f32) + third[...].astype(f32)
    out[...] = total.astype(bf16)


def split_kernel(first, place, *refs):
    *blocks, out, bias, out_w, up_bias, sums = refs
    part = sums.shape[0] // len(blocks)
    start = first
    if len(blocks) == 1:
        sums[...] = blocks[0][...]
    else:
        for k, block in enumerate(blocks):
            source = jnp.bitwise_xor(place[1], k)
            at = (lax.rem(source, 2) * (len(blocks) // 2) + source // 2) * part
            sums[pl.ds(pl.multiple_of(at, 16), part)] = block[start : start + part]
    out[0] = sums[: 3 * DH].astype(f32)
    out[1] = sums[4 * DH : 7 * DH].astype(f32)
    out[2, : 2 * DH] = sums[8 * DH : 10 * DH].astype(f32)
    out[2, 2 * DH :] = sums[7 * DH : 8 * DH].astype(f32)
    tail = sums[10 * DH : 10 * DH + 8].astype(f32)
    third = pltpu.roll(tail[:, 384:512], DH, 1)
    bias[0:1] = tail[0:1, : 3 * DH]
    bias[1:2, :128] = tail[0:1, 512:640]
    bias[1:2, 128:] = third[0:1, :DH]
    start = 10 * DH + 16
    out_w[...] = sums[start : start + out_w.shape[0]].astype(f32)
    start += out_w.shape[0]
    up_bias[...] = sums[start : start + 8].astype(f32)


def half_parts_kernel(place, keep, received, p_keep, q_keep, p_send, q_send, whole):
    whole[...] = keep[...] + received[...].astype(f32)
    part = p_keep.shape[0]
    x, y = lax.rem(place[1] // 2, 2), place[1] // 4
    for start, side, mine, send in ((0, x, p_keep, p_send), (2 * part, y, q_keep, q_send)):
        mine[...] = whole[pl.ds(pl.multiple_of(start + side * part, 16), part)]
        send[...] = whole[pl.ds(pl.multiple_of(start + (1 - side) * part, 16), part)].astype(bf16)


def quarter_parts_kernel(place, p, q, p_in, q_in, p_keep, q_keep, p_send, q_send, p_all, q_all):
    part = p_keep.shape[0]
    x, y = lax.rem(place[1] // 2, 2), place[1] // 4
    p_all[...] = p[...] + p_in[...].astype(f32)
    q_all[...] = q[...] + q_in[...].astype(f32)
    for whole, side, mine, send in ((p_all, y, p_keep, p_send), (q_all, x, q_keep, q_send)):
        mine[...] = whole[pl.ds(pl.multiple_of(side * part, 16), part)]
        send[...] = whole[pl.ds(pl.multiple_of((1 - side) * part, 16), part)].astype(bf16)


def add_two_kernel(p, q, p_in, q_in, p_out, q_out):
    p_out[...] = (p[...] + p_in[...].astype(f32)).astype(bf16)
    q_out[...] = (q[...] + q_in[...].astype(f32)).astype(bf16)


def feed_out_kernel(place, *refs):
    *blocks, down, up = refs
    part = down.shape[0] // 8
    for k, block in enumerate(blocks):
        source = jnp.bitwise_xor(place[1], k)
        x, y = lax.rem(source // 2, 2), source // 4
        start = block.shape[0] - 2 * part
        spots = (2 * x + y) * part, (4 + 2 * y + x) * part

        def put(out, block=block, start=start, spots=spots):
            for i, spot in enumerate(spots):
                rows = block[start + i * part : start + (i + 1) * part]
                out[pl.ds(pl.multiple_of(spot, 16), part)] = rows.astype(f32)

        @pl.when(lax.rem(source, 2) == 0)
        def _(put=put):
            put(down)

        @pl.when(lax.rem(source, 2) == 1)
        def _(put=put):
            put(up)


def send_blocks(me, parts, partial, quarter, special):
    tp_count = len(parts)
    rows = quarter * tp_count
    for k in range(tp_count):
        spot = lax.rem(me + k, tp_count)
        patch_at = pl.ds(pl.multiple_of(spot * quarter, 16), quarter)
        tail = kept_rows(partial, rows + spot * special, special // GROUP)
        parts[k][:quarter] = partial[patch_at].astype(parts[k].dtype)
        parts[k][quarter:] = tail.astype(parts[k].dtype)


def mid_back_kernel(sizes, place, *refs):
    (quarter,) = sizes
    parts, mid, one, grad_result, two_sums, scale, bias, gain = refs[:8]
    grad_mid_out, grad_one_out, small = refs[8:]
    weight = row_weight(mid.shape[0], quarter, place[1], KEPT)
    incoming = parts[...]
    unit, scaling = norm_parts(mid[...])
    grad_mid = grad_result[...] + norm_back(unit, scaling, incoming * gain[...])
    weighted = incoming * weight
    weighted_mid = grad_mid * weight
    result_sum = jnp.sum(grad_result[...] * weight, axis=0, keepdims=True)
    small[0:2] = jnp.zeros((2, small.shape[1]), f32)
    small[2:3] = jnp.sum(weighted * unit, axis=0, keepdims=True)
    small[3:4] = jnp.sum(weighted, axis=0, keepdims=True)
    small[4:5] = jnp.sum(weighted_mid * (one[...] + bias[0:1]), axis=0, keepdims=True)
    small[5:6] = jnp.sum(weighted_mid, axis=0, keepdims=True) * scale[0:1]
    small[6:7] = two_sums[0:1] + result_sum * bias[1:2]
    small[7:8] = result_sum * scale[1:2]
    grad_mid_out[...] = grad_mid
    grad_one = (grad_mid * scale[0:1]).astype(bf16)
    grad_one_out[...] = grad_one


def delta_kernel(sizes, place, *refs):
    tp_count, quarter, special = sizes
    parts = refs[:tp_count]
    attended, attended_b, w_outs, out, out_patch, out_grad, whole = refs[tp_count:]
    rows = quarter * tp_count
    me = place[0]
    for k in range(tp_count):
        spot = lax.rem(me - k + tp_count, tp_count)
        whole[pl.ds(pl.multiple_of(spot * quarter, 16), quarter)] = parts[k][:quarter]
        put_kept_rows(whole, rows + spot * special, parts[k][quarter:])
    value = dot_nt(whole[...], w_outs[0, :LANES]).astype(bf16).astype(f32)
    total = value.shape[0]
    product = value * attended[...]
    lane = lanes_of(value.shape)
    for h in range(3):
        delta = jnp.sum(jnp.where(value_head(lane, h), product, 0.0), axis=-1, keepdims=True)
        for piece, part in enumerate(three_pieces(delta)):
            value = jnp.where(lane == 2 * DH + DELTA_LANE + 3 * h + piece, part, value)
    out[...] = value.astype(bf16)
    out_patch[...] = value[:rows].astype(bf16)
    weighted = (whole[...].astype(f32) * row_weight(total, rows, place[1])).astype(bf16)
    product = dot_tn(attended_b[...], weighted).astype(bf16)
    out_grad[: 2 * DH] = product[: 2 * DH]
    out_grad[2 * DH :] = product[3 * DH :]


def query_grad_kernel(sizes, windows, query, grad, keys, values, out):
    bands, images, rows = sizes
    lane = lanes_of((1, LANES))
    key_picks = [key_side(lane, h, images) for h in range(3)]
    value_picks = [value_side(lane, h) for h in range(3)]
    head_picks = [key_head(lane, h) for h in range(3)]

    def part(own, pulled, chunk):
        key_part = keys[chunk]
        probs = jnp.exp(dot_nt(own, key_part))
        return dot((probs * dot_nt(pulled, values[chunk])).astype(bf16), key_part)

    for u in range(bands):
        window = pl.ds(pl.multiple_of(windows[u], BAND), WINDOW)
        spot = pl.ds(u * BAND, BAND)
        summed = part(stacked(query[spot], key_picks), stacked(grad[spot], value_picks), window)
        out[spot] = (spread_sum(summed, head_picks) * DH**-0.5).astype(bf16)

    own = stacked(first_rows(query[rows:]), key_picks)
    pulled = stacked(first_rows(grad[rows:]), value_picks)
    summed = lax.fori_loop(
        0,
        chunk_count(windows, bands, images),
        lambda c, summed: summed + part(own, pulled, chunk_at(0, c)),
        jnp.zeros((own.shape[0], LANES), f32),
    )
    put_first_rows(out, rows, spread_sum(summed, head_picks) * DH**-0.5)


def pair_grad_kernel(sizes, place, slots, windows, *refs):
    blocks_count, bands, images, tp_count, quarter, special = sizes
    query_blocks = refs[:blocks_count]
    blocks = refs[blocks_count : 2 * blocks_count]
    rest = refs[2 * blocks_count :]
    query_own, grad_own, key_own, value_own, grad_query, w_cat, joined_out, bias_out = rest[:8]
    parts = rest[8 : 8 + tp_count]
    queries, grads, joined, partial = rest[8 + tp_count :]
    rows = quarter * tp_count
    lane = lanes_of((1, LANES))
    image_lane = (lane >= 3 * DH) & (lane <= 3 * DH + images)
    empty = jnp.where(image_lane, FAR, 0.0)

    def clear(at, carry):
        at = pl.multiple_of(at, BAND)
        queries[pl.ds(at, BAND)] = jnp.broadcast_to(empty, (BAND, LANES)).astype(bf16)
        grads[pl.ds(at, BAND)] = jnp.zeros((BAND, LANES), bf16)
        return carry

    clear_unused(clear, windows, bands, images, queries.shape[0])
    per_block = blocks[0].shape[0] // BAND
    slot_count = blocks_count * per_block
    for b in range(blocks_count):

        def put(j, b=b):
            slot = b * per_block + j

            @pl.when(slots[2 * slot_count + slot] > 0)
            def _():
                at = pl.multiple_of(slots[slot], BAND)
                source = pl.ds(pl.multiple_of(j * BAND, BAND), BAND)
                if blocks_count == 1:
                    target = pl.ds(at, BAND)
                    pltpu.sync_copy(blocks[b].at[source], grads.at[target])
                    pltpu.sync_copy(query_blocks[b].at[source], queries.at[target])
                else:
                    grads[pl.ds(at, BAND)] = blocks[b][source]
                    queries[pl.ds(at, BAND)] = query_blocks[b][source]

        for_each(per_block, put)

    def put_special(i):
        at = pl.multiple_of(windows[bands + i], BAND)
        source = pl.ds(pl.multiple_of(rows + i * GROUP, GROUP), GROUP)
        queries[pl.ds(at, GROUP)] = query_own[source]
        grads[pl.ds(at, GROUP)] = grad_own[source]

    for_each(images, put_special)
    key_picks = [key_side(lane, h, images) for h in range(3)]
    value_picks = [value_side(lane, h) for h in range(3)]
    key_heads = [key_head(lane, h) for h in range(3)]
    value_heads = [value_head(lane, h) for h in range(3)]

    def part(own, held, chunk, state):
        grad_key, grad_value = state
        query_part, grad_part = queries[chunk], grads[chunk]
        probs = jnp.exp(dot_nt(own, query_part))
        scores = (probs * dot_nt(held, grad_part)).astype(bf16)
        return (
            grad_key + dot(scores, query_part),
            grad_value + dot(probs.astype(bf16), grad_part),
        )

    def finish(state):
        grad_key = spread_sum(state[0], key_heads)
        grad_value = spread_sum(state[1], value_heads)
        half = lanes_of((1, 128))
        last = jnp.where(half < DH, grad_key[:, 128:], grad_value[:, 128:])
        return jnp.concatenate([grad_key[:, :128], last, grad_value[:, :128]], axis=1)

    joined[:, :256] = grad_query[...]

    def band(u):
        window = pl.ds(pl.multiple_of(windows[u], BAND), WINDOW)
        spot = pl.ds(pl.multiple_of(u * BAND, BAND), BAND)
        own, held = stacked(key_own[spot], key_picks), stacked(value_own[spot], value_picks)
        joined[spot, 256:] = finish(part(own, held, window, (0.0, 0.0))).astype(bf16)

    for u in range(bands):
        band(u)
    own = stacked(first_rows(key_own[rows:]), key_picks)
    held = stacked(first_rows(value_own[rows:]), value_picks)
    blank = jnp.zeros((own.shape[0], LANES), f32)
    state = lax.fori_loop(
        0,
        chunk_count(windows, bands, images),
        lambda c, state: part(own, held, chunk_at(0, c), state),
        (blank, blank),
    )
    put_first_rows(joined.at[:, 256:], rows, finish(state))
    partial[...] = dot(joined[...], w_cat[...])
    send_blocks(place[0], parts, partial, quarter, special)
    weighted = joined[...].astype(f32) * row_weight(joined.shape[0], rows, place[1])
    joined_out[...] = weighted.astype(bf16)
    bias_out[...] = jnp.broadcast_to(jnp.sum(weighted, axis=0, keepdims=True), bias_out.shape).astype(bf16)


def sum_kernel(*refs):
    *parts, out = refs
    total = parts[0][...]
    for part in parts[1:]:
        total += part[...].astype(f32)
    out[...] = total


def stream_back_kernel(sizes, place, *refs):
    quarter, = sizes
    parts, stream, grad_mid, gain, early, out, out_special, send, small = refs
    weight = row_weight(stream.shape[0], quarter, place[1], KEPT)
    incoming = parts[...]
    unit, scaling = norm_parts(stream[...])
    result = grad_mid[...] + norm_back(unit, scaling, incoming * gain[...])
    out[...] = result[:quarter]
    cut_groups(out_special, result[quarter:], out_special.shape[0] // SPECIALS)
    weighted = incoming * weight
    first = jnp.sum(weighted * unit, axis=0, keepdims=True)
    second = jnp.sum(weighted, axis=0, keepdims=True)
    sums = jnp.concatenate([first, second, early[2:8]], axis=0)
    small[...] = sums
    send[:quarter] = result[:quarter].astype(bf16)
    send[quarter:] = sums.astype(bf16)


def join_kernel(*refs):
    *parts, out = refs
    start = 0
    for part in parts:
        out[start : start + part.shape[0]] = part[...]
        start += part.shape[0]


def pack_kernel(cut, x_first, y_first, second, to_y, to_x):
    to_y[:cut] = x_first[:cut]
    to_y[cut:] = second[...]
    rest = y_first.shape[0] - cut
    to_x[:rest] = y_first[cut:]
    to_x[rest:] = second[...]


def unpack_kernel(cut, cut_second, from_x, from_y, diagonal, x_second, y_second, to_y, to_x):
    rest = diagonal.shape[0] - cut
    diagonal[:cut] = from_y[:cut]
    diagonal[cut:] = from_x[:rest]
    x_second[...] = from_x[rest:]
    y_second[...] = from_y[cut:]
    to_y[...] = from_x[rest : rest + cut_second]
    to_x[...] = from_y[cut + cut_second :]


def position_kernel(sizes, place, slots, spots, *refs):
    seq_count, tp_count, images, rows = sizes
    blocks = refs[: 2 * seq_count]
    out, *smalls, ordered, tiny = refs[2 * seq_count :]
    bands = rows // BAND
    slot_count = seq_count * bands
    quarter = rows // tp_count
    piece = 32
    in_piece = lax.broadcasted_iota(jnp.int32, (piece, 1), 0)
    for c in range(tp_count):
        tp = lax.rem(place[0] - c + tp_count, tp_count)
        for k in range(seq_count):
            block = blocks[k] if c == 0 else blocks[seq_count + k]
            block = block.at[pl.ds(max(c - 1, 0) * (quarter + 8), quarter + 8)]
            seq = jnp.bitwise_xor(place[1], k)
            tiny[pl.ds(pl.multiple_of((seq * tp_count + tp) * 8, 8), 8)] = block[
                quarter : quarter + 8
            ].astype(f32)
            for r in range(quarter // piece):
                spot = tp * (quarter // piece) + r
                slot = k * bands + spot // 2
                shift = (spot % 2) * piece
                at = pl.multiple_of(slots[3 * slot_count + slot] + shift, piece)
                valid = slots[2 * slot_count + slot] - shift
                ordered[pl.ds(at, piece)] = jnp.where(
                    in_piece < valid, block[r * piece : (r + 1) * piece].astype(f32), 0.0
                )
    total = tiny[0:8]
    for i in range(1, seq_count * tp_count):
        total += tiny[i * 8 : (i + 1) * 8]
    for out_small, first, second in zip(smalls, (5, 0, 1, 4), (7, 2, 3, 6)):
        out_small[0:1] = total[first : first + 1]
        out_small[1:2] = total[second : second + 1]
    low_rows = out.shape[0] - PATCH_BIG
    seen_big, seen_low = jnp.int32(0), jnp.int32(0)
    for i in range(images):
        at = pl.multiple_of(spots[i], BAND)
        is_big = spots[images + i]
        seen = jnp.where(is_big > 0, seen_big, seen_low)

        @pl.when((is_big > 0) & (seen == 0))
        def _():
            out[:PATCH_BIG] = ordered[pl.ds(at, BIG_BANDS * BAND)][:PATCH_BIG]

        @pl.when((is_big > 0) & (seen > 0))
        def _():
            out[:PATCH_BIG] += ordered[pl.ds(at, BIG_BANDS * BAND)][:PATCH_BIG]

        @pl.when((is_big == 0) & (seen == 0))
        def _():
            out[PATCH_BIG:] = ordered[pl.ds(at, low_rows)]

        @pl.when((is_big == 0) & (seen > 0))
        def _():
            out[PATCH_BIG:] += ordered[pl.ds(at, low_rows)]

        seen_big += is_big
        seen_low += 1 - is_big


def rotated(x, k):
    count = lax.axis_size("tp")
    return lax.ppermute(x, "tp", [(i, (i + k) % count) for i in range(count)])


def from_group(x):
    return [x] + [rotated(x, k) for k in range(1, lax.axis_size("tp"))]


def to_group(blocks):
    return [blocks[0]] + [rotated(blocks[k], k) for k in range(1, len(blocks))]


def exchanged(x, k):
    count = lax.axis_size("tp")
    return lax.ppermute(x, "tp", [(i, i ^ k) for i in range(count)])


def partner(x, k):
    count = lax.axis_size("seq")
    return lax.ppermute(x, "seq", [(i, i ^ k) for i in range(count)])


def from_chips(x):
    if lax.axis_size("seq") != 8:
        return [lax.all_gather(x, "seq", axis=0, tiled=True)]
    return [x] + [partner(x, k) for k in (2, 4, 6)]


def from_ring(x, *late):
    rows = x.shape[0]
    cut = -(-rows // 32) * 16
    along_x, along_y = partner(x, 2), partner(x, 4)
    halves = [partner(after(along_x, *late)[:cut], 4), partner(after(along_y, *late)[cut:], 2)]
    (diagonal,) = call(join_kernel, [(x.shape, x.dtype)], halves, cost=1)
    return [x, along_x, along_y, diagonal]


def two_rings(first, second, ready, passed, use_first):
    cut, cut_second = -(-first.shape[0] // 32) * 16, -(-second.shape[0] // 32) * 16
    rest, rest_second = first.shape[0] - cut, second.shape[0] - cut_second
    width = first.shape[1]
    x_first, y_first = partner(first, 2), partner(first, 4)
    to_y, to_x = call(
        functools.partial(pack_kernel, cut),
        [((cut + second.shape[0], width), bf16), ((rest + second.shape[0], width), bf16)],
        [after(x_first, *ready), y_first, second],
        cost=1,
    )
    from_x, from_y = partner(to_x, 2), partner(to_y, 4)
    diagonal, x_second, y_second, to_y, to_x = call(
        functools.partial(unpack_kernel, cut, cut_second),
        [
            (first.shape, bf16),
            (second.shape, bf16),
            (second.shape, bf16),
            ((cut_second, width), bf16),
            ((rest_second, width), bf16),
        ],
        [after(from_x, *passed), from_y],
        cost=1,
    )
    first_blocks = with_other_core([first, x_first, y_first, diagonal])
    used = use_first(first_blocks)
    low, high = partner(to_y, 4), partner(to_x, 2)
    (diagonal_second,) = call(
        join_kernel, [(second.shape, bf16)], [after(low, *used), high], cost=1
    )
    second_blocks = with_other_core([second, x_second, y_second, diagonal_second])
    return first_blocks, second_blocks, used


def with_other_core(blocks):
    if len(blocks) == 1:
        return blocks
    odd = [partner(block, 1) for block in blocks]
    return [block for pair in zip(blocks, odd) for block in pair]


def from_bands(x):
    return with_other_core(from_chips(x))


def after(value, *others):
    return lax.optimization_barrier((value,) + tuple(others))[0]


def pad_heads(rows):
    gap = jnp.zeros_like(rows[:DH])
    return jnp.concatenate([rows[: 2 * DH], gap, rows[2 * DH :], gap], axis=0)


def joined_columns(query, key, value, axis):
    cut = functools.partial(lax.slice_in_dim, axis=axis)
    return jnp.concatenate(
        [
            query,
            jnp.zeros_like(cut(query, 0, DH)),
            key,
            cut(value, 2 * DH, 3 * DH),
            cut(value, 0, 2 * DH),
        ],
        axis=axis,
    )


def on_device(
    patches,
    specials,
    pos_table,
    image_length,
    slot_band,
    w_qkv,
    qv_bias,
    w_out,
    branch_bias,
    ln_gain,
    ln_bias,
    layer_scale,
    w_up,
    up_bias,
    w_down,
    cot_patch,
    cot_special,
):
    seq_count = lax.axis_size("seq")
    tp_count = lax.axis_size("tp")
    seq_place = lax.axis_index("seq")
    tp_place = lax.axis_index("tp")
    near = seq_count == 8
    quarter, width = patches.shape
    ff = w_up.shape[1]
    images = image_length.shape[0]
    rows = quarter * tp_count
    bands = rows // BAND
    slot_count = slot_band.shape[0]
    special = (specials.shape[0] // SPECIALS) * GROUP
    special_rows = special * tp_count
    total = rows + special_rows
    block = quarter + special // GROUP * KEPT
    place = jnp.stack([tp_place, seq_place]).astype(jnp.int32)

    (x_own,) = call(
        gather_rows_kernel,
        [((block, width), bf16)],
        [patches, specials],
        cost=1,
        spare=58,
    )
    x_parts = from_group(x_own)
    windows, spots, at_table, row_image, position = call(
        functools.partial(plan_kernel, (seq_count, bands, images, rows)),
        [
            ((bands + images + 1,), jnp.int32),
            ((2 * images,), jnp.int32),
            ((2 * bands,), jnp.int32),
            ((total, 1), jnp.int32),
            ((rows, 1), jnp.int32),
        ],
        [image_length, slot_band, place],
        [pltpu.SMEM((images,), jnp.int32)],
    )
    half = w_out.shape[0] // 2
    if near:
        (mine,) = call(
            half_kernel, [((half, width), bf16)], [place, after(w_out, x_own)], cost=1
        )
    w_cat = joined_columns(*jnp.transpose(w_qkv, (0, 2, 1)), 0)
    b_cat = joined_columns(qv_bias[:1], jnp.zeros_like(qv_bias[:1]), qv_bias[1:], 1)
    stream, stream_own, normed, query, pack, key_own, value_own = call(
        functools.partial(embed_kernel, (tp_count, quarter, special, images)),
        [
            ((total, width), f32),
            ((block, width), f32),
            ((total, width), bf16),
            ((total, LANES), bf16),
            ((rows, 384), bf16),
            ((total, LANES), bf16),
            ((total, LANES), bf16),
        ],
        [place, at_table, *x_parts, pos_table, w_cat, b_cat, ln_gain[:1], ln_bias[:1], row_image],
        [
            pltpu.VMEM((rows, width), f32),
            pltpu.VMEM((pos_table.shape[0] - PATCH_BIG, width), f32),
        ],
        cost=4,
    )

    (slots,) = call(
        functools.partial(slots_kernel, (seq_count, bands, images)),
        [((4 * slot_count,), jnp.int32)],
        [image_length, slot_band, after(place, pack)],
        [pltpu.SMEM((images,), jnp.int32)],
        cost=4,
    )
    chips = from_chips(pack)
    if near:
        chips[3] = after(chips[3], slots)
        mine = after(mine, x_parts[2])
        (two_halves,) = call(
            functools.partial(in_order_kernel, 0, 1),
            [((2 * half, width), bf16)],
            [place, mine, exchanged(mine, 1)],
            cost=1,
        )
        (four_halves,) = call(
            functools.partial(in_order_kernel, 0, 2),
            [((4 * half, width), bf16)],
            [place, two_halves, exchanged(two_halves, 2)],
            cost=6,
        )
    pairs = with_other_core(chips)
    if near:
        (w_outs,) = call(
            assemble_kernel,
            [((tp_count, LANES + DH, width), bf16)],
            [place, four_halves, partner(four_halves, 1)],
            cost=1,
        )
    else:
        w_outs = jnp.stack([pad_heads(part) for part in from_group(w_out)])
    grad_two_w, cot_weighted, grad_hidden, grad_result = call(
        functools.partial(cotangent_kernel, (quarter, special)),
        [
            ((total, width), bf16),
            ((total, width), bf16),
            ((total, ff), f32),
            ((block, width), f32),
        ],
        [place, cot_patch, cot_special, layer_scale, after(w_down, pack)],
        [pltpu.VMEM((total, width), f32)],
        cost=3,
    )

    buffer_rows = (slot_count + images) * BAND + WINDOW
    kept = rows + images * KEPT
    keys, values, attended, attended_b, packed, query, query_patch = call(
        functools.partial(attend_kernel, (len(pairs), bands, images, rows)),
        [
            ((buffer_rows, LANES), bf16),
            ((buffer_rows, LANES), bf16),
            ((total, LANES), f32),
            ((total, LANES), bf16),
            ((kept + kept // 2, 128), bf16),
            ((total, LANES), bf16),
            ((rows, LANES), bf16),
        ],
        [slots, windows, *pairs, key_own, value_own, query],
        cost=8,
        spare=8,
    )
    attended_all = from_group(packed)
    query_chips = from_ring(after(query_patch, attended_all[1])) if near else []

    feed = call(
        functools.partial(feed_kernel, (tp_count, quarter, special)),
        [
            ((block, width), f32),
            ((block, width), f32),
            ((total, width), bf16),
            ((total, ff), bf16),
            ((total, ff), bf16),
            ((16, ff), bf16),
            ((block, width), f32),
        ]
        + [((block, width), bf16)] * (tp_count - 1),
        [
            place,
            *attended_all,
            w_outs,
            after(stream, *query_chips[1:3]),
            layer_scale,
            branch_bias,
            ln_gain[1:],
            ln_bias[1:],
            w_up,
            up_bias[None],
            grad_hidden,
        ],
        [pltpu.VMEM((total, width), f32), pltpu.VMEM((total, width), f32)],
        cost=6,
        spare=8,
    )
    mid_own, one_own, normed_two, hidden, grad_pre, up_bias_grad = feed[:6]
    two_parts = to_group(feed[6:])
    keep, send, two_sums, *two_blocks = call(
        functools.partial(feed_grad_kernel, (tp_count, quarter, special, near)),
        [
            ((ff, width), f32),
            ((ff if near else ff + width, width), bf16),
            ((8, width), f32),
            ((block, width), f32),
        ]
        + [((block, width), bf16)] * (tp_count - 1),
        [
            place,
            hidden,
            normed_two,
            grad_two_w,
            grad_pre,
            w_down,
            cot_weighted,
        ],
        [pltpu.VMEM((total, width), f32)],
        cost=0.5,
        spare=8,
    )
    if near:
        p, q, p_send, q_send = call(
            half_parts_kernel,
            [((ff // 4, width), f32)] * 2 + [((ff // 4, width), bf16)] * 2,
            [place, keep, partner(send, 1)],
            [pltpu.VMEM((ff, width), f32)],
            cost=0.1,
        )
        p2, q2, p2_send, q2_send = call(
            quarter_parts_kernel,
            [((ff // 8, width), f32)] * 2 + [((ff // 8, width), bf16)] * 2,
            [place, p, q, partner(p_send, 2), partner(q_send, 4)],
            [pltpu.VMEM((ff // 4, width), f32)] * 2,
            cost=0.1,
        )
        p3, q3 = call(
            add_two_kernel,
            [((ff // 8, width), bf16)] * 2,
            [p2, q2, partner(p2_send, 4), partner(q2_send, 2)],
            cost=0.1,
        )
    else:
        feed_all = lax.psum(send, "seq")

    (grad_two_normed,) = call(sum_kernel, [((block, width), f32)], two_parts, cost=20)
    grad_mid, grad_one, early = call(
        functools.partial(mid_back_kernel, (quarter,)),
        [((block, width), f32), ((block, width), bf16), ((8, width), f32)],
        [
            place,
            grad_two_normed,
            mid_own,
            one_own,
            grad_result,
            two_sums,
            layer_scale,
            branch_bias,
            ln_gain[1:],
        ],
        cost=2,
    )
    grad_one_all = from_group(grad_one)
    if near:
        attended = after(attended, query_chips[3], p3)
    grad_attn, grad_patch, out_grad = call(
        functools.partial(delta_kernel, (tp_count, quarter, special)),
        [((total, LANES), bf16), ((rows, LANES), bf16), ((w_out.shape[0], width), bf16)],
        [place, *grad_one_all, attended, attended_b, w_outs],
        [pltpu.VMEM((total, width), bf16)],
        cost=2,
    )
    (grad_query,) = call(
        functools.partial(query_grad_kernel, (bands, images, rows)),
        [((total, LANES), bf16)],
        [windows, query, grad_attn, keys, values],
        cost=6,
        spare=8,
    )
    if near:
        grads = with_other_core(from_ring(grad_patch, grad_query))
        queries = with_other_core(query_chips)
    else:
        queries = from_chips(after(query_patch, grad_query))
        grads = from_chips(after(grad_patch, grad_query))
    pair = call(
        functools.partial(
            pair_grad_kernel, (len(grads), bands, images, tp_count, quarter, special)
        ),
        [((total, 640), bf16), ((16, 640), bf16), ((block, width), f32)]
        + [((block, width), bf16)] * (tp_count - 1),
        [
            place,
            slots,
            windows,
            *queries,
            *grads,
            query,
            grad_attn,
            key_own,
            value_own,
            grad_query,
            w_cat,
        ],
        [
            pltpu.VMEM((buffer_rows, LANES), bf16),
            pltpu.VMEM((buffer_rows, LANES), bf16),
            pltpu.VMEM((total, 640), bf16),
            pltpu.VMEM((total, width), f32),
        ],
        outside=(3, 4) if len(grads) == 1 else (),
        cost=8,
        spare=8,
    )
    joined, joined_bias = pair[:2]
    normed_parts = to_group(pair[2:])

    last_rows = -(-(640 + 32 + w_out.shape[0]) // 128) * 128
    held = last_rows // 2 if near else last_rows
    keep_last, send_last = call(
        functools.partial(proj_grad_kernel, 2 if near else 1),
        [((held, width), f32), ((held, width), bf16)],
        [place, normed, joined, joined_bias, out_grad, up_bias_grad],
        [pltpu.VMEM((last_rows, width), f32)],
        cost=0.1,
    )
    second_done = [keep_last]
    if near:
        part = last_rows // 8
        mine, *sends = call(
            chip_parts_kernel,
            [((part, width), f32)] + [((part, width), bf16)] * 3,
            [place, keep_last, partner(send_last, 1)],
            [pltpu.VMEM((last_rows // 2, width), f32)],
            cost=0.1,
        )
        received = [partner(block, k) for block, k in zip(sends, (2, 4, 6))]
        (reduced,) = call(add_parts_kernel, [((part, width), bf16)], [mine, *received], cost=0.1)
        second_done.append(reduced)
    (grad_normed,) = call(sum_kernel, [((block, width), f32)], normed_parts, cost=20)
    patch_out, special_out, send, small = call(
        functools.partial(stream_back_kernel, (quarter,)),
        [
            ((quarter, width), f32),
            ((specials.shape[0], width), f32),
            ((quarter + 8, width), bf16),
            ((8, width), f32),
        ],
        [
            place,
            grad_normed,
            after(stream_own, *second_done),
            grad_mid,
            ln_gain[:1],
            early,
        ],
        cost=1,
    )
    arrived = from_group(send)[1:]
    two_in = [rotated(after(two_blocks[k], *arrived), k) for k in range(1, tp_count)]
    def split_sums(blocks, first):
        return call(
            functools.partial(split_kernel, first),
            [
                ((3, 3 * DH, width), f32),
                ((2, 3 * DH), f32),
                ((3 * DH, width), f32),
                ((8, width), f32),
            ],
            [place, *blocks],
            [pltpu.VMEM((last_rows, width), bf16)],
            cost=2,
        )

    if not near:
        last_blocks = [lax.psum(send_last, "seq")]
        part = last_rows
        down_grad, up_grad = feed_all[:ff].astype(f32), feed_all[ff:].astype(f32)
    if near:
        (first_sent,) = call(
            join_kernel,
            [((quarter + 8 + part + ff // 4, width), bf16)],
            [send, reduced, p3, q3],
            cost=1,
        )
        (second_sent,) = call(
            join_kernel,
            [((3 * (quarter + 8), width), bf16)],
            arrived,
            cost=1,
        )

        def use_first(blocks):
            out = call(feed_out_kernel, [((ff, width), f32)] * 2, [place, *blocks], cost=2)
            return out + split_sums(blocks, quarter + 8)

        first_blocks, second_blocks, used = two_rings(
            first_sent, second_sent, arrived, two_in, use_first
        )
        down_grad, up_grad, qkv_grad, qv_bias_grad, out_grad, up_bias_grad = used
        up_bias_grad = up_bias_grad[0]
        sent = first_blocks + second_blocks
        pos_grad, *smalls = call(
            functools.partial(position_kernel, (seq_count, tp_count, images, rows)),
            [((pos_table.shape[0], width), f32)] + [((2, width), f32)] * 4,
            [place, slots, after(spots, up_bias_grad), *sent],
            [
                pltpu.VMEM((slot_count * BAND, width), f32),
                pltpu.VMEM((seq_count * tp_count * 8, width), f32),
            ],
            cost=5,
            spare=4,
        )
    else:
        qkv_grad, qv_bias_grad, out_grad, up_bias_grad = split_sums(last_blocks, 0)
        up_bias_grad = up_bias_grad[0]
        mine = lax.dynamic_slice_in_dim(position, tp_place * quarter, quarter)[:, 0]
        used = lax.dynamic_slice_in_dim(row_image, tp_place * quarter, quarter) >= 0
        local = jax.ops.segment_sum(
            jnp.where(used, patch_out, 0.0), mine, num_segments=pos_table.shape[0]
        )
        pos_grad, small = lax.psum((local, small), ("seq", "tp"))
        smalls = [jnp.stack([small[i], small[j]]) for i, j in ((5, 7), (0, 2), (1, 3), (4, 6))]
    result, result_special = call(
        functools.partial(result_kernel, (quarter, specials.shape[0] // SPECIALS)),
        [((quarter, width), bf16), (specials.shape, bf16)],
        [mid_own, layer_scale, branch_bias, two_blocks[0], *two_in],
        cost=1,
    )
    return (
        result,
        result_special,
        patch_out,
        special_out,
        pos_grad,
        jnp.transpose(qkv_grad, (0, 2, 1)),
        qv_bias_grad,
        out_grad,
        *smalls,
        up_grad,
        up_bias_grad,
        down_grad,
    )


def solution(mesh):
    in_specs = (
        P(("seq", "tp"), None),
        P("tp", None),
        P(),
        P(),
        P(),
        P(None, None, "tp"),
        P(None, "tp"),
        P("tp", None),
        P(),
        P(),
        P(),
        P(),
        P(None, "tp"),
        P("tp"),
        P("tp", None),
        P("seq", None),
        P(),
    )
    out_specs = (
        P(("seq", "tp"), None),
        P("tp", None),
        P(("seq", "tp"), None),
        P("tp", None),
        P(),
        P(None, None, "tp"),
        P(None, "tp"),
        P("tp", None),
        P(),
        P(),
        P(),
        P(),
        P(None, "tp"),
        P("tp"),
        P("tp", None),
    )
    return jax.shard_map(
        on_device, mesh=mesh, in_specs=in_specs, out_specs=out_specs, check_vma=False
    )
```

```python
import functools
import math

import jax
import jax.numpy as jnp
from jax import lax
from jax.experimental import pallas as pl
from jax.experimental.pallas import tpu as pltpu
from jax.sharding import PartitionSpec as P

DH = 64
SPECIALS = 5
PATCH_BIG = 1369
BAND = 64

GROUP = 16
LANES = 256
FAR = 1e30
EPS = 1e-06
BIG_BANDS = (PATCH_BIG + BAND - 1) // BAND
WINDOW = (BIG_BANDS + 1) * BAND
CHUNK = 1280
KEPT = 8
VMEM_LIMIT = 60 * 1024 * 1024

bf16 = jnp.bfloat16
f32 = jnp.float32


def dot(a, b):
    return jnp.dot(a, b, preferred_element_type=f32)


def dot_nt(a, b):
    return lax.dot_general(a, b, (((1,), (1,)), ((), ())), preferred_element_type=f32)


def dot_tn(a, b):
    return lax.dot_general(a, b, (((0,), (0,)), ((), ())), preferred_element_type=f32)


def lanes_of(shape):
    return lax.broadcasted_iota(jnp.int32, shape, len(shape) - 1)


def norm_parts(values):
    centre = jnp.mean(values, axis=-1, keepdims=True)
    centred = values - centre
    spread = jnp.mean(centred * centred, axis=-1, keepdims=True)
    scale = lax.rsqrt(spread + EPS)
    return centred * scale, scale


def norm_back(unit, scale, eg):
    first = jnp.mean(eg, axis=-1, keepdims=True)
    second = jnp.mean(eg * unit, axis=-1, keepdims=True)
    return scale * (eg - first - unit * second)


def key_head(lane, h):
    return (lane >= h * DH) & (lane < (h + 1) * DH)


def value_head(lane, h):
    start = (0, DH, 3 * DH)[h]
    return (lane >= start) & (lane < start + DH)


def key_side(lane, h, images):
    image_lane = (lane >= 3 * DH) & (lane <= 3 * DH + images)
    lse_start = 3 * DH + images + 1 + 3 * h
    return key_head(lane, h) | image_lane | ((lane >= lse_start) & (lane < lse_start + 3))


DELTA_LANE = 50


def value_side(lane, h):
    start = 2 * DH + DELTA_LANE + 3 * h
    return value_head(lane, h) | ((lane >= start) & (lane < start + 3))


def three_pieces(x):
    high = x.astype(bf16).astype(f32)
    rest = x - high
    middle = rest.astype(bf16).astype(f32)
    return high, middle, (rest - middle).astype(bf16).astype(f32)


def stacked(rows, picks):
    zero = jnp.zeros_like(rows)
    return jnp.concatenate([jnp.where(pick, rows, zero) for pick in picks], axis=0)


def spread_sum(stack, picks):
    count = stack.shape[0] // len(picks)
    total = None
    for h, pick in enumerate(picks):
        part = jnp.where(pick, stack[h * count : (h + 1) * count], 0.0)
        total = part if total is None else total + part
    return total


def held_bytes(shape, dtype):
    lanes = -(-shape[-1] // 128) * 128
    rows = -(-math.prod(shape[:-1]) // 16) * 16
    return rows * lanes * jnp.dtype(dtype).itemsize


def call(body, outs, ins, scratch=(), outside=(), cost=2, spare=6):
    spaces = []
    for i, item in enumerate(ins):
        smem = item.dtype == jnp.int32 and item.ndim == 1
        space = pl.ANY if i in outside else pltpu.SMEM if smem else pltpu.VMEM
        spaces.append(pl.BlockSpec(memory_space=space))
    need = sum(held_bytes(x.shape, x.dtype) for i, x in enumerate(ins) if i not in outside)
    need += sum(held_bytes(s, d) for s, d in outs)
    need += sum(held_bytes(x.shape, x.dtype) for x in scratch)
    out_spaces = [
        pl.BlockSpec(memory_space=pltpu.SMEM if d == jnp.int32 and len(s) == 1 else pltpu.VMEM)
        for s, d in outs
    ]
    return pl.pallas_call(
        body,
        out_shape=[jax.ShapeDtypeStruct(s, d) for s, d in outs],
        in_specs=spaces,
        out_specs=out_spaces,
        scratch_shapes=list(scratch),
        cost_estimate=pl.CostEstimate(
            flops=int(cost * 10**9), bytes_accessed=0, transcendentals=0
        ),
        compiler_params=pltpu.CompilerParams(
            vmem_limit_bytes=min(need + spare * 1024 * 1024, VMEM_LIMIT)
            if need < 2**24 + 2**23
            else VMEM_LIMIT
        ),
    )(*ins)


def for_each(count, body):
    def step(i, carry):
        body(i)
        return carry

    lax.fori_loop(0, count, step, 0)


def image_starts(images, length, held):
    def begin(i, start):
        held[i] = start
        return start + (length[i] + BAND - 1) // BAND

    return lax.fori_loop(0, images, begin, jnp.int32(0))


def band_facts(images, length, slot_band, held, used, slot):
    band = slot_band[slot]

    def look(i, state):
        image, first = state
        inside = band >= held[i]
        return jnp.where(inside, i, image), jnp.where(inside, held[i], first)

    state = (jnp.int32(0), jnp.int32(0))
    if images <= 8:
        for i in range(images):
            state = look(i, state)
    else:
        state = lax.fori_loop(0, images, look, state)
    image, first = state
    left = jnp.minimum(jnp.maximum(length[image] - (band - first) * BAND, 0), BAND)
    return band, image, first, jnp.where(band < used, left, 0)


def plan_kernel(sizes, length, slot_band, place, windows, spots, own, row_image, position, held):
    seq_count, bands, images, rows = sizes
    used = image_starts(images, length, held)

    def image_facts(i, carry):
        spots[i] = held[i] * BAND
        spots[images + i] = (length[i] == PATCH_BIG).astype(jnp.int32)
        windows[bands + i] = (held[i] + i) * BAND
        return carry

    lax.fori_loop(0, images, image_facts, 0)
    windows[bands + images] = (used + images) * BAND
    in_band = lax.broadcasted_iota(jnp.int32, (BAND, 1), 0)
    for u in range(bands):
        band, image, first, valid = band_facts(
            images, length, slot_band, held, used, place[1] * bands + u
        )
        windows[u] = jnp.where(valid > 0, (first + image) * BAND, 0)
        own[u] = jnp.where(valid > 0, (band - first) * BAND, 0)
        own[bands + u] = (length[image] == PATCH_BIG).astype(jnp.int32)
        good = in_band < valid
        row_image[u * BAND : (u + 1) * BAND] = jnp.where(good, image, -1)
        offset = jnp.where(length[image] == PATCH_BIG, 0, PATCH_BIG) + (band - first) * BAND
        position[u * BAND : (u + 1) * BAND] = jnp.where(good, offset + in_band, 0)
    group = lax.broadcasted_iota(jnp.int32, (images * GROUP, 1), 0)
    row_image[rows:] = jnp.where(group % GROUP < SPECIALS, group // GROUP, -1)


def slots_kernel(sizes, length, slot_band, place, slots, held):
    seq_count, bands, images = sizes
    slot_count = seq_count * bands
    used = image_starts(images, length, held)

    def put(i, carry):
        source = i // bands
        if seq_count == 8:
            source = jnp.bitwise_xor(source, place[1])
        band, image, _, valid = band_facts(
            images, length, slot_band, held, used, source * bands + i % bands
        )
        slots[i] = jnp.where(valid > 0, (band + image + 1) * BAND, 0)
        slots[slot_count + i] = image
        slots[2 * slot_count + i] = valid
        slots[3 * slot_count + i] = band * BAND
        return carry

    lax.fori_loop(0, slot_count, put, 0)


def gather_rows_kernel(patches, specials, out):
    quarter = patches.shape[0]
    out[:quarter] = patches[...]
    padding = jnp.zeros((KEPT - SPECIALS, patches.shape[1]), f32)
    for g in range(specials.shape[0] // SPECIALS):
        group = specials[g * SPECIALS : (g + 1) * SPECIALS].astype(f32)
        out[quarter + g * KEPT : quarter + (g + 1) * KEPT] = jnp.concatenate(
            [group, padding], axis=0
        ).astype(bf16)


def kept_rows(whole, start, groups):
    at = [pl.ds(pl.multiple_of(start + g * GROUP, GROUP), KEPT) for g in range(groups)]
    return jnp.concatenate([whole[spot].astype(f32) for spot in at], axis=0)


def put_kept_rows(whole, start, rows):
    padding = jnp.zeros((GROUP - KEPT, rows.shape[1]), f32)
    rows = rows.astype(f32)
    for g in range(rows.shape[0] // KEPT):
        group = jnp.concatenate([rows[g * KEPT : (g + 1) * KEPT], padding], axis=0)
        whole[pl.ds(pl.multiple_of(start + g * GROUP, GROUP), GROUP)] = group.astype(whole.dtype)


def row_weight(count, patch_rows, seq, group=GROUP):
    row = lax.broadcasted_iota(jnp.int32, (count, 1), 0)
    special = ((row - patch_rows) % group < SPECIALS) & (seq == 0)
    return jnp.where((row < patch_rows) | special, 1.0, 0.0)


def embed_kernel(sizes, place, at_table, *refs):
    tp_count, quarter, special, images = sizes
    xs = refs[:tp_count]
    table, w_cat, b_cat, gain, shift, row_image = refs[tp_count : tp_count + 6]
    stream, own, normed, query, pack, key_own, value_own, pos, low = refs[tp_count + 6 :]
    low[...] = table[PATCH_BIG:].astype(f32)
    bands = quarter * tp_count // BAND
    for u in range(bands):
        at = pl.multiple_of(at_table[u], BAND)
        good = row_image[u * BAND : (u + 1) * BAND] >= 0

        @pl.when(at_table[bands + u] > 0)
        def _(u=u, at=at, good=good):
            pos[u * BAND : (u + 1) * BAND] = jnp.where(
                good, table[pl.ds(at, BAND)].astype(f32), 0.0
            )

        @pl.when(at_table[bands + u] == 0)
        def _(u=u, at=at, good=good):
            pos[u * BAND : (u + 1) * BAND] = jnp.where(good, low[pl.ds(at, BAND)], 0.0)

    rows = quarter * tp_count
    me = place[0]
    for k in range(tp_count):
        spot = lax.rem(me - k + tp_count, tp_count)
        patch_at = pl.multiple_of(spot * quarter, 16)
        special_at = rows + spot * special
        part = xs[k][:quarter].astype(f32) + pos[pl.ds(patch_at, quarter)]
        stream[pl.ds(patch_at, quarter)] = part
        tail = xs[k][quarter:].astype(f32)
        put_kept_rows(stream, special_at, tail)
        if k == 0:
            own[:quarter] = part
            own[quarter:] = tail
    unit, _ = norm_parts(stream[...])
    rounded = (unit * gain[...] + shift[...]).astype(bf16)
    normed[...] = rounded
    projected = (dot_nt(rounded, w_cat[...]) + b_cat[...]).astype(bf16)
    image = row_image[...]
    total = image.shape[0]
    lane = lanes_of((total, LANES))
    image_lane = (lane >= 3 * DH) & (lane <= 3 * DH + images)
    scaled = projected[:, :LANES].astype(f32) * (DH**-0.5)
    far = jnp.where(image_lane & (lane != 3 * DH + image), FAR, 0.0)
    query[...] = jnp.where(lane < 3 * DH, scaled, far).astype(bf16)
    pack[...] = projected[:rows, LANES:]
    own_lane = 3 * DH + jnp.where(image < 0, images, image)
    lse_lane = (lane > 3 * DH + images) & (lane <= 3 * DH + images + 9)
    aux = jnp.where((lane == own_lane) | lse_lane, -1.0, 0.0)
    key_own[...] = jnp.where(
        lane < 3 * DH, projected[:, LANES : 2 * LANES].astype(f32), aux
    ).astype(bf16)
    half = lanes_of((total, 128))
    value_own[:, :128] = projected[:, 512:640]
    value_own[:, 128:] = jnp.where(
        half < DH,
        jnp.where((half >= DELTA_LANE) & (half < DELTA_LANE + 9), -1.0, 0.0),
        projected[:, 384:512].astype(f32),
    ).astype(bf16)


def chunk_count(windows, bands, images):
    return (windows[bands + images] + CHUNK - 1) // CHUNK


def chunk_at(start, c):
    return pl.ds(pl.multiple_of(start + c * CHUNK, BAND), CHUNK)


def first_rows(rows):
    rows = rows.astype(f32)
    count = rows.shape[0] // GROUP
    return jnp.concatenate([rows[i * GROUP : i * GROUP + KEPT] for i in range(count)], axis=0).astype(
        bf16
    )


def put_first_rows(target, start, rows):
    padding = jnp.zeros((GROUP - KEPT, rows.shape[1]), f32)
    count = rows.shape[0] // KEPT
    rows = rows.astype(f32)
    target[pl.ds(start, count * GROUP)] = jnp.concatenate(
        [part for i in range(count) for part in (rows[i * KEPT : (i + 1) * KEPT], padding)], axis=0
    ).astype(target.dtype)


def clear_unused(clear, windows, bands, images, buffer_rows):
    lax.fori_loop(0, images, lambda i, c: clear(windows[bands + i], c), 0)
    lax.fori_loop(
        windows[bands + images] // BAND,
        jnp.maximum(
            windows[bands + images - 1] // BAND + -(-WINDOW // BAND),
            chunk_count(windows, bands, images) * (CHUNK // BAND),
        ),
        lambda i, c: clear(i * BAND, c),
        0,
    )


def half_kernel(place, rows, out):
    half = out.shape[0]
    out[...] = rows[pl.ds(pl.multiple_of(lax.rem(place[1], 2) * half, 16), half)]


def in_order_kernel(axis, bit, place, mine, other, out):
    count = mine.shape[0]
    side = lax.rem(place[axis] // bit, 2)
    out[pl.ds(pl.multiple_of(side * count, 16), count)] = mine[...]
    out[pl.ds(pl.multiple_of((1 - side) * count, 16), count)] = other[...]


def assemble_kernel(place, mine, other, out):
    count = out.shape[0]
    half = mine.shape[0] // count
    cut = 2 * DH - half
    for k in range(count):
        source = lax.rem(place[0] - k + count, count)
        spot = (source % 2 * 2 + source // 2) * half
        at = pl.multiple_of(spot, 16)
        late = pl.multiple_of(spot + cut, 16)
        out[k, 2 * DH : 3 * DH] = jnp.zeros((DH, out.shape[2]), bf16)
        out[k, 4 * DH :] = jnp.zeros((DH, out.shape[2]), bf16)

        def fill(low, high, k=k, at=at, late=late):
            out[k, :half] = low[pl.ds(at, half)]
            out[k, half : 2 * DH] = high[pl.ds(at, cut)]
            out[k, 3 * DH : 4 * DH] = high[pl.ds(late, half - cut)]

        @pl.when(place[1] % 2 == 0)
        def _(fill=fill):
            fill(mine, other)

        @pl.when(place[1] % 2 == 1)
        def _(fill=fill):
            fill(other, mine)


def attend_kernel(sizes, slots, windows, *refs):
    blocks_count, bands, images, rows = sizes
    blocks = refs[:blocks_count]
    key_own, value_own, query = refs[blocks_count : blocks_count + 3]
    keys, values, attended, attended_b, packed, query_out, query_patch = refs[blocks_count + 3 :]
    lane = lanes_of((1, LANES))
    lse_lane = (lane > 3 * DH + images) & (lane <= 3 * DH + images + 9)
    empty = jnp.where((lane == 3 * DH + images) | lse_lane, -1.0, 0.0)
    buffer_rows = keys.shape[0]

    def clear(at, carry):
        at = pl.multiple_of(at, BAND)
        keys[pl.ds(at, BAND)] = jnp.broadcast_to(empty, (BAND, LANES)).astype(bf16)
        values[pl.ds(at, BAND)] = jnp.zeros((BAND, LANES), bf16)
        return carry

    clear_unused(clear, windows, bands, images, buffer_rows)
    band_lane = lanes_of((BAND, LANES))
    half = lanes_of((BAND, 128))
    in_band = lax.broadcasted_iota(jnp.int32, (BAND, LANES), 0)
    band_lse = (band_lane > 3 * DH + images) & (band_lane <= 3 * DH + images + 9)
    delta_aux = jnp.where((half >= DELTA_LANE) & (half < DELTA_LANE + 9), -1.0, 0.0)
    per_block = blocks[0].shape[0] // BAND
    slot_count = blocks_count * per_block
    for b in range(blocks_count):

        def place(j, b=b):
            slot = b * per_block + j
            valid = slots[2 * slot_count + slot]

            @pl.when(valid > 0)
            def _():
                at = pl.multiple_of(slots[slot], BAND)
                image = slots[slot_count + slot]
                source = blocks[b][pl.ds(pl.multiple_of(j * BAND, BAND), BAND)]
                own_lane = 3 * DH + jnp.where(in_band < valid, image, images)
                aux = jnp.where((band_lane == own_lane) | band_lse, -1.0, 0.0)
                keys[pl.ds(at, BAND)] = jnp.where(
                    band_lane < 3 * DH, source[:, :LANES].astype(f32), aux
                ).astype(bf16)
                values[pl.ds(at, BAND), :128] = source[:, 256:384]
                values[pl.ds(at, BAND), 128:] = jnp.where(
                    half < DH, delta_aux, source[:, 128:256].astype(f32)
                ).astype(bf16)

        for_each(per_block, place)

    def place_special(i):
        at = pl.multiple_of(windows[bands + i], BAND)
        source = pl.ds(pl.multiple_of(rows + i * GROUP, GROUP), GROUP)
        keys[pl.ds(at, GROUP)] = key_own[source]
        values[pl.ds(at, GROUP)] = value_own[source]

    for_each(images, place_special)
    key_picks = [key_side(lane, h, images) for h in range(3)]
    value_picks = [value_head(lane, h) for h in range(3)]

    chunks = chunk_count(windows, bands, images)

    def finish(count, own, top, total, summed):
        usable = total > 0.0
        safe = jnp.where(usable, total, 1.0)
        result = spread_sum(summed / safe, value_picks)
        lse = jnp.where(usable, top + jnp.log(safe), 0.0)
        row = own.astype(f32)
        for h in range(3):
            for piece, part in enumerate(three_pieces(lse[h * count : (h + 1) * count])):
                row = jnp.where(lane == 3 * DH + images + 1 + 3 * h + piece, part, row)
        return result, row

    for u in range(bands):
        window = pl.ds(pl.multiple_of(windows[u], BAND), WINDOW)
        spot = pl.ds(u * BAND, BAND)
        own = query[spot]
        scores = dot_nt(stacked(own, key_picks), keys[window])
        top = jnp.maximum(jnp.max(scores, axis=-1, keepdims=True), -0.1 * FAR)
        weights = jnp.exp(scores - top)
        total = jnp.sum(weights, axis=-1, keepdims=True)
        result, row = finish(BAND, own, top, total, dot(weights.astype(bf16), values[window]))
        attended[spot] = result
        attended_b[spot] = result.astype(bf16)
        query_out[spot] = row.astype(bf16)

    own = first_rows(query[rows:])
    stack = stacked(own, key_picks)
    count = stack.shape[0]

    def add(c, state):
        top, total, summed = state
        scores = dot_nt(stack, keys[chunk_at(0, c)])
        new_top = jnp.maximum(top, jnp.max(scores, axis=-1, keepdims=True))
        rescale = jnp.exp(top - new_top)
        weights = jnp.exp(scores - new_top)
        return (
            new_top,
            total * rescale + jnp.sum(weights, axis=-1, keepdims=True),
            summed * rescale + dot(weights.astype(bf16), values[chunk_at(0, c)]),
        )

    start = (
        jnp.full((count, 1), -0.1 * FAR, f32),
        jnp.zeros((count, 1), f32),
        jnp.zeros((count, LANES), f32),
    )
    result, row = finish(count // 3, own, *lax.fori_loop(0, chunks, add, start))
    put_first_rows(attended, rows, result)
    put_first_rows(attended_b, rows, result)
    put_first_rows(query_out, rows, row)
    query_patch[...] = query_out[:rows]
    kept = rows + images * KEPT
    half = kept // 2
    tails = kept_rows(attended, rows, images)
    packed[:rows] = attended_b[:rows, :128]
    packed[rows:kept] = tails[:, :128].astype(bf16)
    third = jnp.concatenate([attended[:rows, 128:], tails[:, 128:]], axis=0)
    upper = pltpu.roll(third[:half], DH, 1)
    packed[kept:] = jnp.where(lanes_of((1, 128)) < DH, upper, third[half:]).astype(bf16)


def cotangent_kernel(
    sizes, place, patch, special_rows, scale, w_down, two_weighted, weighted, hidden, own, whole
):
    quarter, special = sizes
    rows = patch.shape[0]
    whole[:rows] = patch[...].astype(f32)
    padding = jnp.zeros((GROUP - SPECIALS, patch.shape[1]), f32)
    for g in range(special_rows.shape[0] // SPECIALS):
        group = special_rows[g * SPECIALS : (g + 1) * SPECIALS].astype(f32)
        whole[rows + g * GROUP : rows + (g + 1) * GROUP] = jnp.concatenate([group, padding], axis=0)
    value = whole[...]
    weight = row_weight(whole.shape[0], rows, place[1])
    grad_two = (value * scale[1:2]).astype(bf16)
    weighted[...] = (value * weight).astype(bf16)
    two_weighted[...] = (grad_two.astype(f32) * weight).astype(bf16)
    hidden[...] = dot_nt(grad_two, w_down[...])
    own[:quarter] = whole[pl.ds(pl.multiple_of(place[0] * quarter, 16), quarter)]
    own[quarter:] = kept_rows(whole, rows + place[0] * special, special // GROUP)


def result_kernel(sizes, mid, scale, bias, *refs):
    quarter, groups = sizes
    *parts, patch, special = refs
    two = parts[0][...]
    for part in parts[1:]:
        two += part[: two.shape[0]].astype(f32)
    result = (mid[...] + scale[1:2] * (two + bias[1:2])).astype(bf16)
    patch[...] = result[:quarter]
    cut_groups(special, result[quarter:].astype(f32), groups)


def cut_groups(target, rows, groups):
    for g in range(groups):
        target[g * SPECIALS : (g + 1) * SPECIALS] = rows[g * KEPT : g * KEPT + SPECIALS].astype(
            target.dtype
        )


def feed_kernel(sizes, place, *refs):
    tp_count, quarter, special = sizes
    attended = refs[:tp_count]
    w_outs, stream, scale, bias, gain, shift, w_up, up_bias, grad_hidden = refs[
        tp_count : tp_count + 9
    ]
    mid_own, one_own, normed, hidden_out, grad_pre_out, bias_out = refs[
        tp_count + 9 : tp_count + 15
    ]
    parts = refs[tp_count + 15 : 2 * tp_count + 15]
    mid, partial = refs[2 * tp_count + 15 :]
    rows = quarter * tp_count
    me = place[0]
    kept = attended[0].shape[0] * 2 // 3
    one = 0.0
    upper, lower = 0.0, 0.0
    for k in range(tp_count):
        one += dot(attended[k][:kept], w_outs[k, : 2 * DH])
        upper += dot(attended[k][kept:], w_outs[k, 3 * DH :])
        lower += dot(attended[k][kept:], w_outs[k, 2 * DH : 4 * DH])
    one = one + jnp.concatenate([upper, lower], axis=0)
    partial[:rows] = one[:rows]
    put_kept_rows(partial, rows, one[rows:])
    value = stream[...] + scale[0:1] * (partial[...] + bias[0:1])
    mid[...] = value
    own_patch = pl.ds(pl.multiple_of(me * quarter, 16), quarter)
    own_special = rows + me * special, special // GROUP
    mid_own[:quarter] = mid[own_patch]
    mid_own[quarter:] = kept_rows(mid, *own_special)
    one_own[:quarter] = partial[own_patch]
    one_own[quarter:] = kept_rows(partial, *own_special)
    unit, _ = norm_parts(value)
    rounded = (unit * gain[...] + shift[...]).astype(bf16)
    normed[...] = rounded
    pre = dot(rounded, w_up[...]) + up_bias[...]
    share = 0.5 * (1.0 + lax.erf(pre * (0.5**0.5)))
    hidden_out[...] = (pre * share).astype(bf16)
    slope = share + pre * jnp.exp(-0.5 * pre * pre) * (0.5 / jnp.pi) ** 0.5
    grad_pre = (grad_hidden[...] * slope).astype(bf16)
    weight = row_weight(value.shape[0], rows, place[1])
    weighted = grad_pre.astype(f32) * weight
    grad_pre_out[...] = weighted.astype(bf16)
    bias_out[...] = jnp.broadcast_to(jnp.sum(weighted, axis=0, keepdims=True), bias_out.shape).astype(bf16)
    partial[...] = dot_nt(grad_pre, w_up[...])
    send_blocks(me, parts, partial, quarter, special)


def feed_grad_kernel(sizes, place, *refs):
    tp_count, quarter, special, split = sizes
    hidden, normed, grad_two, grad_pre, w_down, grad_result, keep, send, send_late, sums = refs[:10]
    two_blocks = refs[10 : 10 + tp_count]
    half = send.shape[0]
    partial = refs[-1]
    ff = hidden.shape[1]
    down = dot_tn(hidden[...], grad_two[...])
    up = dot_tn(normed[...], grad_pre[...])
    if split:

        @pl.when(place[1] % 2 == 0)
        def _():
            keep[...] = down
            send[...] = up[:half].astype(bf16)
            send_late[...] = up[half:].astype(bf16)

        @pl.when(place[1] % 2 == 1)
        def _():
            keep[...] = up
            send[...] = down[:half].astype(bf16)
            send_late[...] = down[half:].astype(bf16)

    else:
        keep[...] = down
        send[...] = down.astype(bf16)
        send_late[...] = up.astype(bf16)
    two = dot(hidden[...], w_down[...])
    sums[...] = jnp.broadcast_to(
        jnp.sum(two * grad_result[...].astype(f32), axis=0, keepdims=True), sums.shape
    )
    partial[...] = two
    send_blocks(place[0], two_blocks, partial, quarter, special)


def proj_grad_kernel(parts, place, normed, joined, bias, out_grad, up_bias, keep, send, whole):
    columns = joined.shape[1]
    whole[:columns] = dot_tn(joined[...], normed[...])
    whole[columns : columns + 16, :columns] = bias[...].astype(f32)
    whole[columns : columns + 16, columns:] = jnp.zeros((16, normed.shape[1] - columns), f32)
    start = columns + 16 + out_grad.shape[0]
    whole[columns + 16 : start] = out_grad[...].astype(f32)
    whole[start : start + 16] = up_bias[...].astype(f32)
    whole[start + 16 :] = jnp.zeros((whole.shape[0] - start - 16, normed.shape[1]), f32)
    half = keep.shape[0]
    core = lax.rem(place[1], parts) if parts == 2 else 0
    keep[...] = whole[pl.ds(pl.multiple_of(core * half, 16), half)]
    send[...] = whole[pl.ds(pl.multiple_of((1 - core) * half if parts == 2 else 0, 16), half)].astype(bf16)


def chip_parts_kernel(place, keep, received, mine, *sends_and_whole):
    *sends, whole = sends_and_whole
    whole[...] = keep[...] + received[...].astype(f32)
    part = mine.shape[0]
    chip = place[1] // 2
    mine[...] = whole[pl.ds(pl.multiple_of(chip * part, 16), part)]
    for i, send in enumerate(sends):
        at = pl.multiple_of(jnp.bitwise_xor(chip, i + 1) * part, 16)
        send[...] = whole[pl.ds(at, part)].astype(bf16)


def add_parts_kernel(mine, first, second, third, out):
    total = mine[...] + first[...].astype(f32) + second[...].astype(f32) + third[...].astype(f32)
    out[...] = total.astype(bf16)


def split_kernel(first, place, *refs):
    *blocks, out, bias, out_w, up_bias, sums = refs
    part = sums.shape[0] // len(blocks)
    start = first
    if len(blocks) == 1:
        sums[...] = blocks[0][...]
    else:
        for k, block in enumerate(blocks):
            source = jnp.bitwise_xor(place[1], k)
            at = (lax.rem(source, 2) * (len(blocks) // 2) + source // 2) * part
            sums[pl.ds(pl.multiple_of(at, 16), part)] = block[start : start + part]
    out[0] = sums[: 3 * DH].astype(f32)
    out[1] = sums[4 * DH : 7 * DH].astype(f32)
    out[2, : 2 * DH] = sums[8 * DH : 10 * DH].astype(f32)
    out[2, 2 * DH :] = sums[7 * DH : 8 * DH].astype(f32)
    tail = sums[10 * DH : 10 * DH + 8].astype(f32)
    third = pltpu.roll(tail[:, 384:512], DH, 1)
    bias[0:1] = tail[0:1, : 3 * DH]
    bias[1:2, :128] = tail[0:1, 512:640]
    bias[1:2, 128:] = third[0:1, :DH]
    start = 10 * DH + 16
    out_w[...] = sums[start : start + out_w.shape[0]].astype(f32)
    start += out_w.shape[0]
    up_bias[...] = sums[start : start + 8].astype(f32)


def half_parts_kernel(place, keep, received, received_late, p_keep, q_keep, p_send, q_send, whole):
    half = received.shape[0]
    whole[:half] = keep[:half] + received[...].astype(f32)
    whole[half:] = keep[half:] + received_late[...].astype(f32)
    part = p_keep.shape[0]
    x, y = lax.rem(place[1] // 2, 2), place[1] // 4
    for start, side, mine, send in ((0, x, p_keep, p_send), (2 * part, y, q_keep, q_send)):
        mine[...] = whole[pl.ds(pl.multiple_of(start + side * part, 16), part)]
        send[...] = whole[pl.ds(pl.multiple_of(start + (1 - side) * part, 16), part)].astype(bf16)


def quarter_parts_kernel(place, p, q, p_in, q_in, p_keep, q_keep, p_send, q_send, p_all, q_all):
    part = p_keep.shape[0]
    x, y = lax.rem(place[1] // 2, 2), place[1] // 4
    p_all[...] = p[...] + p_in[...].astype(f32)
    q_all[...] = q[...] + q_in[...].astype(f32)
    for whole, side, mine, send in ((p_all, y, p_keep, p_send), (q_all, x, q_keep, q_send)):
        mine[...] = whole[pl.ds(pl.multiple_of(side * part, 16), part)]
        send[...] = whole[pl.ds(pl.multiple_of((1 - side) * part, 16), part)].astype(bf16)


def add_two_kernel(p, q, p_in, q_in, p_out, q_out):
    p_out[...] = (p[...] + p_in[...].astype(f32)).astype(bf16)
    q_out[...] = (q[...] + q_in[...].astype(f32)).astype(bf16)


def feed_out_kernel(place, *refs):
    *blocks, down, up = refs
    part = down.shape[0] // 8
    for k, block in enumerate(blocks):
        source = jnp.bitwise_xor(place[1], k)
        x, y = lax.rem(source // 2, 2), source // 4
        start = block.shape[0] - 2 * part
        spots = (2 * x + y) * part, (4 + 2 * y + x) * part

        def put(out, block=block, start=start, spots=spots):
            for i, spot in enumerate(spots):
                rows = block[start + i * part : start + (i + 1) * part]
                out[pl.ds(pl.multiple_of(spot, 16), part)] = rows.astype(f32)

        @pl.when(lax.rem(source, 2) == 0)
        def _(put=put):
            put(down)

        @pl.when(lax.rem(source, 2) == 1)
        def _(put=put):
            put(up)


def send_blocks(me, parts, partial, quarter, special):
    tp_count = len(parts)
    rows = quarter * tp_count
    for k in range(tp_count):
        spot = lax.rem(me + k, tp_count)
        patch_at = pl.ds(pl.multiple_of(spot * quarter, 16), quarter)
        tail = kept_rows(partial, rows + spot * special, special // GROUP)
        parts[k][:quarter] = partial[patch_at].astype(parts[k].dtype)
        parts[k][quarter:] = tail.astype(parts[k].dtype)


def mid_back_kernel(sizes, place, *refs):
    (quarter,) = sizes
    parts, mid, one, grad_result, two_sums, scale, bias, gain = refs[:8]
    grad_mid_out, grad_one_out, small = refs[8:]
    weight = row_weight(mid.shape[0], quarter, place[1], KEPT)
    incoming = parts[...]
    unit, scaling = norm_parts(mid[...])
    grad_mid = grad_result[...] + norm_back(unit, scaling, incoming * gain[...])
    weighted = incoming * weight
    weighted_mid = grad_mid * weight
    result_sum = jnp.sum(grad_result[...] * weight, axis=0, keepdims=True)
    small[0:2] = jnp.zeros((2, small.shape[1]), f32)
    small[2:3] = jnp.sum(weighted * unit, axis=0, keepdims=True)
    small[3:4] = jnp.sum(weighted, axis=0, keepdims=True)
    small[4:5] = jnp.sum(weighted_mid * (one[...] + bias[0:1]), axis=0, keepdims=True)
    small[5:6] = jnp.sum(weighted_mid, axis=0, keepdims=True) * scale[0:1]
    small[6:7] = two_sums[0:1] + result_sum * bias[1:2]
    small[7:8] = result_sum * scale[1:2]
    grad_mid_out[...] = grad_mid
    grad_one = (grad_mid * scale[0:1]).astype(bf16)
    grad_one_out[...] = grad_one


def delta_kernel(sizes, place, *refs):
    tp_count, quarter, special = sizes
    parts = refs[:tp_count]
    attended, attended_b, w_outs, out, out_patch, out_grad, whole = refs[tp_count:]
    rows = quarter * tp_count
    me = place[0]
    for k in range(tp_count):
        spot = lax.rem(me - k + tp_count, tp_count)
        whole[pl.ds(pl.multiple_of(spot * quarter, 16), quarter)] = parts[k][:quarter]
        put_kept_rows(whole, rows + spot * special, parts[k][quarter:])
    value = dot_nt(whole[...], w_outs[0, :LANES]).astype(bf16).astype(f32)
    total = value.shape[0]
    product = value * attended[...]
    lane = lanes_of(value.shape)
    for h in range(3):
        delta = jnp.sum(jnp.where(value_head(lane, h), product, 0.0), axis=-1, keepdims=True)
        for piece, part in enumerate(three_pieces(delta)):
            value = jnp.where(lane == 2 * DH + DELTA_LANE + 3 * h + piece, part, value)
    out[...] = value.astype(bf16)
    out_patch[...] = value[:rows].astype(bf16)
    weighted = (whole[...].astype(f32) * row_weight(total, rows, place[1])).astype(bf16)
    product = dot_tn(attended_b[...], weighted).astype(bf16)
    out_grad[: 2 * DH] = product[: 2 * DH]
    out_grad[2 * DH :] = product[3 * DH :]


def query_grad_kernel(sizes, windows, query, grad, keys, values, out):
    bands, images, rows = sizes
    lane = lanes_of((1, LANES))
    key_picks = [key_side(lane, h, images) for h in range(3)]
    value_picks = [value_side(lane, h) for h in range(3)]
    head_picks = [key_head(lane, h) for h in range(3)]

    def part(own, pulled, chunk):
        key_part = keys[chunk]
        probs = jnp.exp(dot_nt(own, key_part))
        return dot((probs * dot_nt(pulled, values[chunk])).astype(bf16), key_part)

    for u in range(bands):
        window = pl.ds(pl.multiple_of(windows[u], BAND), WINDOW)
        spot = pl.ds(u * BAND, BAND)
        summed = part(stacked(query[spot], key_picks), stacked(grad[spot], value_picks), window)
        out[spot] = (spread_sum(summed, head_picks) * DH**-0.5).astype(bf16)

    own = stacked(first_rows(query[rows:]), key_picks)
    pulled = stacked(first_rows(grad[rows:]), value_picks)
    summed = lax.fori_loop(
        0,
        chunk_count(windows, bands, images),
        lambda c, summed: summed + part(own, pulled, chunk_at(0, c)),
        jnp.zeros((own.shape[0], LANES), f32),
    )
    put_first_rows(out, rows, spread_sum(summed, head_picks) * DH**-0.5)


def pair_grad_kernel(sizes, place, slots, windows, *refs):
    blocks_count, bands, images, tp_count, quarter, special = sizes
    query_blocks = refs[:blocks_count]
    blocks = refs[blocks_count : 2 * blocks_count]
    rest = refs[2 * blocks_count :]
    query_own, grad_own, key_own, value_own, grad_query, w_cat, joined_out, bias_out = rest[:8]
    parts = rest[8 : 8 + tp_count]
    queries, grads, joined, partial = rest[8 + tp_count :]
    rows = quarter * tp_count
    lane = lanes_of((1, LANES))
    image_lane = (lane >= 3 * DH) & (lane <= 3 * DH + images)
    empty = jnp.where(image_lane, FAR, 0.0)

    def clear(at, carry):
        at = pl.multiple_of(at, BAND)
        queries[pl.ds(at, BAND)] = jnp.broadcast_to(empty, (BAND, LANES)).astype(bf16)
        grads[pl.ds(at, BAND)] = jnp.zeros((BAND, LANES), bf16)
        return carry

    clear_unused(clear, windows, bands, images, queries.shape[0])
    per_block = blocks[0].shape[0] // BAND
    slot_count = blocks_count * per_block
    for b in range(blocks_count):

        def put(j, b=b):
            slot = b * per_block + j

            @pl.when(slots[2 * slot_count + slot] > 0)
            def _():
                at = pl.multiple_of(slots[slot], BAND)
                source = pl.ds(pl.multiple_of(j * BAND, BAND), BAND)
                if blocks_count == 1:
                    target = pl.ds(at, BAND)
                    pltpu.sync_copy(blocks[b].at[source], grads.at[target])
                    pltpu.sync_copy(query_blocks[b].at[source], queries.at[target])
                else:
                    grads[pl.ds(at, BAND)] = blocks[b][source]
                    queries[pl.ds(at, BAND)] = query_blocks[b][source]

        for_each(per_block, put)

    def put_special(i):
        at = pl.multiple_of(windows[bands + i], BAND)
        source = pl.ds(pl.multiple_of(rows + i * GROUP, GROUP), GROUP)
        queries[pl.ds(at, GROUP)] = query_own[source]
        grads[pl.ds(at, GROUP)] = grad_own[source]

    for_each(images, put_special)
    key_picks = [key_side(lane, h, images) for h in range(3)]
    value_picks = [value_side(lane, h) for h in range(3)]
    key_heads = [key_head(lane, h) for h in range(3)]
    value_heads = [value_head(lane, h) for h in range(3)]

    def part(own, held, chunk, state):
        grad_key, grad_value = state
        query_part, grad_part = queries[chunk], grads[chunk]
        probs = jnp.exp(dot_nt(own, query_part))
        scores = (probs * dot_nt(held, grad_part)).astype(bf16)
        return (
            grad_key + dot(scores, query_part),
            grad_value + dot(probs.astype(bf16), grad_part),
        )

    def finish(state):
        grad_key = spread_sum(state[0], key_heads)
        grad_value = spread_sum(state[1], value_heads)
        half = lanes_of((1, 128))
        last = jnp.where(half < DH, grad_key[:, 128:], grad_value[:, 128:])
        return jnp.concatenate([grad_key[:, :128], last, grad_value[:, :128]], axis=1)

    joined[:, :256] = grad_query[...]

    def band(u):
        window = pl.ds(pl.multiple_of(windows[u], BAND), WINDOW)
        spot = pl.ds(pl.multiple_of(u * BAND, BAND), BAND)
        own, held = stacked(key_own[spot], key_picks), stacked(value_own[spot], value_picks)
        joined[spot, 256:] = finish(part(own, held, window, (0.0, 0.0))).astype(bf16)

    for u in range(bands):
        band(u)
    own = stacked(first_rows(key_own[rows:]), key_picks)
    held = stacked(first_rows(value_own[rows:]), value_picks)
    blank = jnp.zeros((own.shape[0], LANES), f32)
    state = lax.fori_loop(
        0,
        chunk_count(windows, bands, images),
        lambda c, state: part(own, held, chunk_at(0, c), state),
        (blank, blank),
    )
    put_first_rows(joined.at[:, 256:], rows, finish(state))
    partial[...] = dot(joined[...], w_cat[...])
    send_blocks(place[0], parts, partial, quarter, special)
    weighted = joined[...].astype(f32) * row_weight(joined.shape[0], rows, place[1])
    joined_out[...] = weighted.astype(bf16)
    bias_out[...] = jnp.broadcast_to(jnp.sum(weighted, axis=0, keepdims=True), bias_out.shape).astype(bf16)


def sum_kernel(*refs):
    *parts, out = refs
    total = parts[0][...]
    for part in parts[1:]:
        total += part[...].astype(f32)
    out[...] = total


def stream_back_kernel(sizes, place, *refs):
    quarter, = sizes
    parts, stream, grad_mid, gain, early, out, out_special, send, small = refs
    weight = row_weight(stream.shape[0], quarter, place[1], KEPT)
    incoming = parts[...]
    unit, scaling = norm_parts(stream[...])
    result = grad_mid[...] + norm_back(unit, scaling, incoming * gain[...])
    out[...] = result[:quarter]
    cut_groups(out_special, result[quarter:], out_special.shape[0] // SPECIALS)
    weighted = incoming * weight
    first = jnp.sum(weighted * unit, axis=0, keepdims=True)
    second = jnp.sum(weighted, axis=0, keepdims=True)
    sums = jnp.concatenate([first, second, early[2:8]], axis=0)
    small[...] = sums
    send[:quarter] = result[:quarter].astype(bf16)
    send[quarter:] = sums.astype(bf16)


def join_kernel(*refs):
    *parts, out = refs
    start = 0
    for part in parts:
        out[start : start + part.shape[0]] = part[...]
        start += part.shape[0]


def pack_kernel(cut, x_first, y_first, second, to_y, to_x):
    to_y[:cut] = x_first[:cut]
    to_y[cut:] = second[...]
    rest = y_first.shape[0] - cut
    to_x[:rest] = y_first[cut:]
    to_x[rest:] = second[...]


def unpack_kernel(cut, cut_second, from_x, from_y, diagonal, x_second, y_second, to_y, to_x):
    rest = diagonal.shape[0] - cut
    diagonal[:cut] = from_y[:cut]
    diagonal[cut:] = from_x[:rest]
    x_second[...] = from_x[rest:]
    y_second[...] = from_y[cut:]
    to_y[...] = from_x[rest : rest + cut_second]
    to_x[...] = from_y[cut + cut_second :]


def position_kernel(sizes, place, slots, spots, *refs):
    seq_count, tp_count, images, rows = sizes
    blocks = refs[: 2 * seq_count]
    out, *smalls, ordered, tiny = refs[2 * seq_count :]
    bands = rows // BAND
    slot_count = seq_count * bands
    quarter = rows // tp_count
    piece = 32
    for c in range(tp_count):
        tp = lax.rem(place[0] - c + tp_count, tp_count)
        for k in range(seq_count):
            block = blocks[k] if c == 0 else blocks[seq_count + k]
            block = block.at[pl.ds(max(c - 1, 0) * (quarter + 8), quarter + 8)]
            seq = jnp.bitwise_xor(place[1], k)
            tiny[pl.ds(pl.multiple_of((seq * tp_count + tp) * 8, 8), 8)] = block[
                quarter : quarter + 8
            ].astype(f32)
            for r in range(quarter // piece):
                spot = tp * (quarter // piece) + r
                slot = k * bands + spot // 2
                shift = (spot % 2) * piece
                at = pl.multiple_of(slots[3 * slot_count + slot] + shift, piece)
                ordered[pl.ds(at, piece)] = block[r * piece : (r + 1) * piece]
    total = tiny[0:8]
    for i in range(1, seq_count * tp_count):
        total += tiny[i * 8 : (i + 1) * 8]
    for out_small, first, second in zip(smalls, (5, 0, 1, 4), (7, 2, 3, 6)):
        out_small[0:1] = total[first : first + 1]
        out_small[1:2] = total[second : second + 1]
    low_rows = out.shape[0] - PATCH_BIG
    seen_big, seen_low = jnp.int32(0), jnp.int32(0)
    for i in range(images):
        at = pl.multiple_of(spots[i], BAND)
        is_big = spots[images + i]
        seen = jnp.where(is_big > 0, seen_big, seen_low)

        @pl.when((is_big > 0) & (seen == 0))
        def _():
            out[:PATCH_BIG] = ordered[pl.ds(at, BIG_BANDS * BAND)][:PATCH_BIG].astype(f32)

        @pl.when((is_big > 0) & (seen > 0))
        def _():
            out[:PATCH_BIG] += ordered[pl.ds(at, BIG_BANDS * BAND)][:PATCH_BIG].astype(f32)

        @pl.when((is_big == 0) & (seen == 0))
        def _():
            out[PATCH_BIG:] = ordered[pl.ds(at, low_rows)].astype(f32)

        @pl.when((is_big == 0) & (seen > 0))
        def _():
            out[PATCH_BIG:] += ordered[pl.ds(at, low_rows)].astype(f32)

        seen_big += is_big
        seen_low += 1 - is_big


def rotated(x, k):
    count = lax.axis_size("tp")
    return lax.ppermute(x, "tp", [(i, (i + k) % count) for i in range(count)])


def from_group(x):
    return [x] + [rotated(x, k) for k in range(1, lax.axis_size("tp"))]


def to_group(blocks):
    return [blocks[0]] + [rotated(blocks[k], k) for k in range(1, len(blocks))]


def exchanged(x, k):
    count = lax.axis_size("tp")
    return lax.ppermute(x, "tp", [(i, i ^ k) for i in range(count)])


def partner(x, k):
    count = lax.axis_size("seq")
    return lax.ppermute(x, "seq", [(i, i ^ k) for i in range(count)])


def from_chips(x):
    if lax.axis_size("seq") != 8:
        return [lax.all_gather(x, "seq", axis=0, tiled=True)]
    return [x] + [partner(x, k) for k in (2, 4, 6)]


def from_ring(x, *late):
    rows = x.shape[0]
    cut = -(-rows // 32) * 16
    along_x, along_y = partner(x, 2), partner(x, 4)
    halves = [partner(after(along_x, *late)[:cut], 4), partner(after(along_y, *late)[cut:], 2)]
    (diagonal,) = call(join_kernel, [(x.shape, x.dtype)], halves, cost=1)
    return [x, along_x, along_y, diagonal]


def two_rings(first, second, ready, passed, use_first):
    cut, cut_second = -(-first.shape[0] // 32) * 16, -(-second.shape[0] // 32) * 16
    rest, rest_second = first.shape[0] - cut, second.shape[0] - cut_second
    width = first.shape[1]
    x_first, y_first = partner(first, 2), partner(first, 4)
    to_y, to_x = call(
        functools.partial(pack_kernel, cut),
        [((cut + second.shape[0], width), bf16), ((rest + second.shape[0], width), bf16)],
        [after(x_first, *ready), y_first, second],
        cost=1,
    )
    from_x, from_y = partner(to_x, 2), partner(to_y, 4)
    diagonal, x_second, y_second, to_y, to_x = call(
        functools.partial(unpack_kernel, cut, cut_second),
        [
            (first.shape, bf16),
            (second.shape, bf16),
            (second.shape, bf16),
            ((cut_second, width), bf16),
            ((rest_second, width), bf16),
        ],
        [after(from_x, *passed), from_y],
        cost=1,
    )
    first_blocks = with_other_core([first, x_first, y_first, diagonal])
    used = use_first(first_blocks)
    low, high = partner(to_y, 4), partner(to_x, 2)
    (diagonal_second,) = call(
        join_kernel, [(second.shape, bf16)], [after(low, *used), high], cost=1
    )
    second_blocks = with_other_core([second, x_second, y_second, diagonal_second])
    return first_blocks, second_blocks, used


def with_other_core(blocks):
    if len(blocks) == 1:
        return blocks
    odd = [partner(block, 1) for block in blocks]
    return [block for pair in zip(blocks, odd) for block in pair]


def from_bands(x):
    return with_other_core(from_chips(x))


def after(value, *others):
    return lax.optimization_barrier((value,) + tuple(others))[0]


def pad_heads(rows):
    gap = jnp.zeros_like(rows[:DH])
    return jnp.concatenate([rows[: 2 * DH], gap, rows[2 * DH :], gap], axis=0)


def joined_columns(query, key, value, axis):
    cut = functools.partial(lax.slice_in_dim, axis=axis)
    return jnp.concatenate(
        [
            query,
            jnp.zeros_like(cut(query, 0, DH)),
            key,
            cut(value, 2 * DH, 3 * DH),
            cut(value, 0, 2 * DH),
        ],
        axis=axis,
    )


def on_device(
    patches,
    specials,
    pos_table,
    image_length,
    slot_band,
    w_qkv,
    qv_bias,
    w_out,
    branch_bias,
    ln_gain,
    ln_bias,
    layer_scale,
    w_up,
    up_bias,
    w_down,
    cot_patch,
    cot_special,
):
    seq_count = lax.axis_size("seq")
    tp_count = lax.axis_size("tp")
    seq_place = lax.axis_index("seq")
    tp_place = lax.axis_index("tp")
    near = seq_count == 8
    quarter, width = patches.shape
    ff = w_up.shape[1]
    images = image_length.shape[0]
    rows = quarter * tp_count
    bands = rows // BAND
    slot_count = slot_band.shape[0]
    special = (specials.shape[0] // SPECIALS) * GROUP
    special_rows = special * tp_count
    total = rows + special_rows
    block = quarter + special // GROUP * KEPT
    place = jnp.stack([tp_place, seq_place]).astype(jnp.int32)

    (x_own,) = call(
        gather_rows_kernel,
        [((block, width), bf16)],
        [patches, specials],
        cost=1,
        spare=58,
    )
    x_parts = from_group(x_own)
    windows, spots, at_table, row_image, position = call(
        functools.partial(plan_kernel, (seq_count, bands, images, rows)),
        [
            ((bands + images + 1,), jnp.int32),
            ((2 * images,), jnp.int32),
            ((2 * bands,), jnp.int32),
            ((total, 1), jnp.int32),
            ((rows, 1), jnp.int32),
        ],
        [image_length, slot_band, place],
        [pltpu.SMEM((images,), jnp.int32)],
    )
    half = w_out.shape[0] // 2
    if near:
        (mine,) = call(
            half_kernel, [((half, width), bf16)], [place, after(w_out, x_own)], cost=1
        )
    w_cat = joined_columns(*jnp.transpose(w_qkv, (0, 2, 1)), 0)
    b_cat = joined_columns(qv_bias[:1], jnp.zeros_like(qv_bias[:1]), qv_bias[1:], 1)
    stream, stream_own, normed, query, pack, key_own, value_own = call(
        functools.partial(embed_kernel, (tp_count, quarter, special, images)),
        [
            ((total, width), f32),
            ((block, width), f32),
            ((total, width), bf16),
            ((total, LANES), bf16),
            ((rows, 384), bf16),
            ((total, LANES), bf16),
            ((total, LANES), bf16),
        ],
        [place, at_table, *x_parts, pos_table, w_cat, b_cat, ln_gain[:1], ln_bias[:1], row_image],
        [
            pltpu.VMEM((rows, width), f32),
            pltpu.VMEM((pos_table.shape[0] - PATCH_BIG, width), f32),
        ],
        cost=4,
    )

    (slots,) = call(
        functools.partial(slots_kernel, (seq_count, bands, images)),
        [((4 * slot_count,), jnp.int32)],
        [image_length, slot_band, after(place, pack)],
        [pltpu.SMEM((images,), jnp.int32)],
        cost=4,
    )
    chips = from_chips(pack)
    if near:
        chips[3] = after(chips[3], slots)
        mine = after(mine, x_parts[2])
        (two_halves,) = call(
            functools.partial(in_order_kernel, 0, 2),
            [((2 * half, width), bf16)],
            [place, mine, exchanged(mine, 2)],
            cost=1,
        )
        (four_halves,) = call(
            functools.partial(in_order_kernel, 0, 1),
            [((4 * half, width), bf16)],
            [place, two_halves, exchanged(two_halves, 1)],
            cost=6,
        )
    pairs = with_other_core(chips)
    if near:
        (w_outs,) = call(
            assemble_kernel,
            [((tp_count, LANES + DH, width), bf16)],
            [place, four_halves, partner(four_halves, 1)],
            cost=1,
        )
    else:
        w_outs = jnp.stack([pad_heads(part) for part in from_group(w_out)])
    grad_two_w, cot_weighted, grad_hidden, grad_result = call(
        functools.partial(cotangent_kernel, (quarter, special)),
        [
            ((total, width), bf16),
            ((total, width), bf16),
            ((total, ff), f32),
            ((block, width), f32),
        ],
        [place, cot_patch, cot_special, layer_scale, after(w_down, pack)],
        [pltpu.VMEM((total, width), f32)],
        cost=3,
    )

    buffer_rows = (slot_count + images) * BAND + WINDOW
    kept = rows + images * KEPT
    keys, values, attended, attended_b, packed, query, query_patch = call(
        functools.partial(attend_kernel, (len(pairs), bands, images, rows)),
        [
            ((buffer_rows, LANES), bf16),
            ((buffer_rows, LANES), bf16),
            ((total, LANES), f32),
            ((total, LANES), bf16),
            ((kept + kept // 2, 128), bf16),
            ((total, LANES), bf16),
            ((rows, LANES), bf16),
        ],
        [slots, windows, *pairs, key_own, value_own, query],
        cost=8,
        spare=8,
    )
    attended_all = from_group(packed)
    query_chips = from_ring(after(query_patch, attended_all[1])) if near else []

    feed = call(
        functools.partial(feed_kernel, (tp_count, quarter, special)),
        [
            ((block, width), f32),
            ((block, width), f32),
            ((total, width), bf16),
            ((total, ff), bf16),
            ((total, ff), bf16),
            ((16, ff), bf16),
            ((block, width), f32),
        ]
        + [((block, width), bf16)] * (tp_count - 1),
        [
            place,
            *attended_all,
            w_outs,
            after(stream, *query_chips[1:3]),
            layer_scale,
            branch_bias,
            ln_gain[1:],
            ln_bias[1:],
            w_up,
            up_bias[None],
            grad_hidden,
        ],
        [pltpu.VMEM((total, width), f32), pltpu.VMEM((total, width), f32)],
        cost=6,
        spare=8,
    )
    mid_own, one_own, normed_two, hidden, grad_pre, up_bias_grad = feed[:6]
    two_parts = to_group(feed[6:])
    keep, send, send_late, two_sums, *two_blocks = call(
        functools.partial(feed_grad_kernel, (tp_count, quarter, special, near)),
        [
            ((ff, width), f32),
            ((ff // 2 if near else ff, width), bf16),
            ((width // 2 if near else width, width), bf16),
            ((8, width), f32),
            ((block, width), f32),
        ]
        + [((block, width), bf16)] * (tp_count - 1),
        [
            place,
            hidden,
            normed_two,
            grad_two_w,
            grad_pre,
            w_down,
            cot_weighted,
        ],
        [pltpu.VMEM((total, width), f32)],
        cost=0.5,
        spare=8,
    )
    if near:
        p, q, p_send, q_send = call(
            half_parts_kernel,
            [((ff // 4, width), f32)] * 2 + [((ff // 4, width), bf16)] * 2,
            [place, keep, partner(send, 1), partner(send_late, 1)],
            [pltpu.VMEM((ff, width), f32)],
            cost=0.1,
        )
        p2, q2, p2_send, q2_send = call(
            quarter_parts_kernel,
            [((ff // 8, width), f32)] * 2 + [((ff // 8, width), bf16)] * 2,
            [place, p, q, partner(p_send, 2), partner(q_send, 4)],
            [pltpu.VMEM((ff // 4, width), f32)] * 2,
            cost=0.1,
        )
        p3, q3 = call(
            add_two_kernel,
            [((ff // 8, width), bf16)] * 2,
            [p2, q2, partner(p2_send, 4), partner(q2_send, 2)],
            cost=0.1,
        )
    else:
        feed_all = jnp.concatenate(lax.psum((send, send_late), "seq"), axis=0)

    (grad_two_normed,) = call(sum_kernel, [((block, width), f32)], two_parts, cost=20)
    grad_mid, grad_one, early = call(
        functools.partial(mid_back_kernel, (quarter,)),
        [((block, width), f32), ((block, width), bf16), ((8, width), f32)],
        [
            place,
            grad_two_normed,
            mid_own,
            one_own,
            grad_result,
            two_sums,
            layer_scale,
            branch_bias,
            ln_gain[1:],
        ],
        cost=2,
    )
    grad_one_all = from_group(grad_one)
    if near:
        attended = after(attended, query_chips[3])
    grad_attn, grad_patch, out_grad = call(
        functools.partial(delta_kernel, (tp_count, quarter, special)),
        [((total, LANES), bf16), ((rows, LANES), bf16), ((w_out.shape[0], width), bf16)],
        [place, *grad_one_all, attended, attended_b, w_outs],
        [pltpu.VMEM((total, width), bf16)],
        cost=2,
    )
    (grad_query,) = call(
        functools.partial(query_grad_kernel, (bands, images, rows)),
        [((total, LANES), bf16)],
        [windows, query, grad_attn, after(keys, p2) if near else keys, values],
        cost=6,
        spare=8,
    )
    if near:
        grads = with_other_core(from_ring(grad_patch, grad_query))
        queries = with_other_core(query_chips)
    else:
        queries = from_chips(after(query_patch, grad_query))
        grads = from_chips(after(grad_patch, grad_query))
    pair = call(
        functools.partial(
            pair_grad_kernel, (len(grads), bands, images, tp_count, quarter, special)
        ),
        [((total, 640), bf16), ((16, 640), bf16), ((block, width), f32)]
        + [((block, width), bf16)] * (tp_count - 1),
        [
            place,
            slots,
            windows,
            *queries,
            *grads,
            query,
            grad_attn,
            key_own,
            value_own,
            grad_query,
            w_cat,
        ],
        [
            pltpu.VMEM((buffer_rows, LANES), bf16),
            pltpu.VMEM((buffer_rows, LANES), bf16),
            pltpu.VMEM((total, 640), bf16),
            pltpu.VMEM((total, width), f32),
        ],
        outside=(3, 4) if len(grads) == 1 else (),
        cost=8,
        spare=8,
    )
    joined, joined_bias = pair[:2]
    normed_parts = to_group(pair[2:])

    last_rows = -(-(640 + 32 + w_out.shape[0]) // 128) * 128
    held = last_rows // 2 if near else last_rows
    keep_last, send_last = call(
        functools.partial(proj_grad_kernel, 2 if near else 1),
        [((held, width), f32), ((held, width), bf16)],
        [place, normed, joined, joined_bias, out_grad, up_bias_grad],
        [pltpu.VMEM((last_rows, width), f32)],
        cost=0.1,
    )
    second_done = [keep_last]
    if near:
        part = last_rows // 8
        mine, *sends = call(
            chip_parts_kernel,
            [((part, width), f32)] + [((part, width), bf16)] * 3,
            [place, keep_last, partner(send_last, 1)],
            [pltpu.VMEM((last_rows // 2, width), f32)],
            cost=0.1,
        )
        received = [partner(block, k) for block, k in zip(sends, (2, 4, 6))]
        (reduced,) = call(add_parts_kernel, [((part, width), bf16)], [mine, *received], cost=0.1)
        second_done.append(reduced)
    (grad_normed,) = call(sum_kernel, [((block, width), f32)], normed_parts, cost=20)
    patch_out, special_out, send, small = call(
        functools.partial(stream_back_kernel, (quarter,)),
        [
            ((quarter, width), f32),
            ((specials.shape[0], width), f32),
            ((quarter + 8, width), bf16),
            ((8, width), f32),
        ],
        [
            place,
            grad_normed,
            after(stream_own, *second_done),
            grad_mid,
            ln_gain[:1],
            early,
        ],
        cost=1,
    )
    arrived = from_group(send)[1:]
    two_in = [rotated(after(two_blocks[k], *arrived), k) for k in range(1, tp_count)]
    def split_sums(blocks, first):
        return call(
            functools.partial(split_kernel, first),
            [
                ((3, 3 * DH, width), f32),
                ((2, 3 * DH), f32),
                ((3 * DH, width), f32),
                ((8, width), f32),
            ],
            [place, *blocks],
            [pltpu.VMEM((last_rows, width), bf16)],
            cost=2,
        )

    if not near:
        last_blocks = [lax.psum(send_last, "seq")]
        part = last_rows
        down_grad, up_grad = feed_all[:ff].astype(f32), feed_all[ff:].astype(f32)
    if near:
        (first_sent,) = call(
            join_kernel,
            [((quarter + 8 + part + ff // 4, width), bf16)],
            [send, reduced, p3, q3],
            cost=1,
        )
        (second_sent,) = call(
            join_kernel,
            [((3 * (quarter + 8), width), bf16)],
            arrived,
            cost=1,
        )

        def use_first(blocks):
            out = call(feed_out_kernel, [((ff, width), f32)] * 2, [place, *blocks], cost=2)
            return out + split_sums(blocks, quarter + 8)

        first_blocks, second_blocks, used = two_rings(
            first_sent, second_sent, arrived, two_in, use_first
        )
        down_grad, up_grad, qkv_grad, qv_bias_grad, out_grad, up_bias_grad = used
        up_bias_grad = up_bias_grad[0]
        sent = first_blocks + second_blocks
        pos_grad, *smalls = call(
            functools.partial(position_kernel, (seq_count, tp_count, images, rows)),
            [((pos_table.shape[0], width), f32)] + [((2, width), f32)] * 4,
            [place, slots, after(spots, up_bias_grad), *sent],
            [
                pltpu.VMEM((slot_count * BAND, width), bf16),
                pltpu.VMEM((seq_count * tp_count * 8, width), f32),
            ],
            cost=5,
            spare=4,
        )
    else:
        qkv_grad, qv_bias_grad, out_grad, up_bias_grad = split_sums(last_blocks, 0)
        up_bias_grad = up_bias_grad[0]
        mine = lax.dynamic_slice_in_dim(position, tp_place * quarter, quarter)[:, 0]
        used = lax.dynamic_slice_in_dim(row_image, tp_place * quarter, quarter) >= 0
        local = jax.ops.segment_sum(
            jnp.where(used, patch_out, 0.0), mine, num_segments=pos_table.shape[0]
        )
        pos_grad, small = lax.psum((local, small), ("seq", "tp"))
        smalls = [jnp.stack([small[i], small[j]]) for i, j in ((5, 7), (0, 2), (1, 3), (4, 6))]
    result, result_special = call(
        functools.partial(result_kernel, (quarter, specials.shape[0] // SPECIALS)),
        [((quarter, width), bf16), (specials.shape, bf16)],
        [mid_own, layer_scale, branch_bias, two_blocks[0], *two_in],
        cost=1,
    )
    return (
        result,
        result_special,
        patch_out,
        special_out,
        pos_grad,
        jnp.transpose(qkv_grad, (0, 2, 1)),
        qv_bias_grad,
        out_grad,
        *smalls,
        up_grad,
        up_bias_grad,
        down_grad,
    )


def solution(mesh):
    in_specs = (
        P(("seq", "tp"), None),
        P("tp", None),
        P(),
        P(),
        P(),
        P(None, None, "tp"),
        P(None, "tp"),
        P("tp", None),
        P(),
        P(),
        P(),
        P(),
        P(None, "tp"),
        P("tp"),
        P("tp", None),
        P("seq", None),
        P(),
    )
    out_specs = (
        P(("seq", "tp"), None),
        P("tp", None),
        P(("seq", "tp"), None),
        P("tp", None),
        P(),
        P(None, None, "tp"),
        P(None, "tp"),
        P("tp", None),
        P(),
        P(),
        P(),
        P(),
        P(None, "tp"),
        P("tp"),
        P("tp", None),
    )
    return jax.shard_map(
        on_device, mesh=mesh, in_specs=in_specs, out_specs=out_specs, check_vma=False
    )
```
